128 devices in a mesh: expert: 16 (over x, z_lo, core), dp: 8 (over y, z_hi).
Axes of the slice: x: 4, y: 4, z: 4 (z_hi: 2, z_lo: 2; z = z_hi * 2 + z_lo), core: 2. Of those that a mesh axis runs over, the one named last changes fastest.
Arguments:
- tokens: bfloat16 [16384, 2048], P(('expert', 'dp')), may hold values from -6 to 6
- cotangent: bfloat16 [16384, 2048], P(('expert', 'dp')), may hold values from -1.5 to 1.5
- route_gates: float32 [16384, 6], P(('expert', 'dp')), may hold values from 0.1 to 1
- expert_ids: int32 [16384, 6], P(('expert', 'dp')), may hold values from 0 to 31, as said below
- slot_index: int32 [16384, 6], P(('expert', 'dp')), may hold values from 0 to 31, as said below
- w_gate: bfloat16 [32, 2048, 704], P('expert'), may hold values from -0.125 to 0.125
- w_up: bfloat16 [32, 2048, 704], P('expert'), may hold values from -0.125 to 0.125
- w_down: bfloat16 [32, 704, 2048], P('expert'), may hold values from -0.21875 to 0.21875
Outputs:
- layer_out: bfloat16 [16384, 2048], P(('expert', 'dp'))
- grad_tokens: bfloat16 [16384, 2048], P(('expert', 'dp'))
- grad_gates: float32 [16384, 6], P(('expert', 'dp'))
- grad_w_gate: float32 [32, 2048, 704], P('expert', 'dp')
- grad_w_up: float32 [32, 2048, 704], P('expert', 'dp')
- grad_w_down: float32 [32, 704, 2048], P('expert', None, 'dp')
The draws below stay inside these ranges and needn't reach their ends.
Inputs may be any that keep to these rules, and one draw needn't show every extreme that they name: `expert_ids`: each row names 6 different experts. Among the rows of one device no expert is named more than 32 times, and in the rows of every device some expert is named exactly 32 times. `slot_index`: among the rows of one device, the choices that name the same expert have distinct slots.
All inputs are finite; a program needn't handle non-finite values.
Results may differ from the reference program's by a relative error of at most 0.014.
Values may be sent and summed in bfloat16 or wider, within the bound.
A program may use at most 192 MiB of HBM per device.

```python
import math
import jax
import jax.numpy as jnp
from jax import lax

D = 2048
H = 704
TOPK = 6
TOK_DEV = 128
EXPERTS = 32
CAP = 32
TOKENS = 16384
N_EXPERT = 16
N_DP = 8


def shuffle_rows(subkeys, length):

    def one_order(subkey):
        return jax.random.permutation(subkey, length)
    return jax.vmap(one_order)(subkeys)


def routing(key):
    blocks = TOKENS // TOK_DEV
    cell_count = EXPERTS * CAP
    assigned = TOK_DEV * TOPK
    subkeys = jax.random.split(key, 5)
    main_expert = jax.random.randint(subkeys[0], (), 0, EXPERTS)
    second_expert = (main_expert + 1 + jax.random.randint(subkeys[1], (blocks, 1), 0, EXPERTS - 1)) % EXPERTS
    owner = (jnp.arange(cell_count, dtype=jnp.int32) // CAP)[None, :]
    priority = jnp.where(owner == main_expert, 0, jnp.where(owner == second_expert, 1, 2))
    shuffled = shuffle_rows(jax.random.split(subkeys[2], blocks), cell_count)
    scores = priority * cell_count + shuffled
    chosen = jnp.sort(jnp.argsort(scores, axis=1, stable=True)[:, :assigned], axis=1)
    experts = (chosen // CAP).reshape(blocks, TOPK, TOK_DEV).transpose(0, 2, 1)
    slot_table = (chosen % CAP).reshape(blocks, TOPK, TOK_DEV).transpose(0, 2, 1)
    row_order = shuffle_rows(jax.random.split(subkeys[3], blocks), TOK_DEV)
    experts = jnp.take_along_axis(experts, row_order[:, :, None], axis=1)
    slot_table = jnp.take_along_axis(slot_table, row_order[:, :, None], axis=1)
    column_scores = jax.random.randint(subkeys[4], (blocks, TOK_DEV, TOPK), 0, 1 << 20) * TOPK + jnp.arange(TOPK)[None, None, :]
    column_order = jnp.argsort(column_scores, axis=2)
    experts = jnp.take_along_axis(experts, column_order, axis=2)
    slot_table = jnp.take_along_axis(slot_table, column_order, axis=2)
    return (experts.reshape(TOKENS, TOPK).astype(jnp.int32), slot_table.reshape(TOKENS, TOPK).astype(jnp.int32))


def draw_expert_ids(key, part):
    return routing(key)[0]


def draw_slot_index(key, part):
    return routing(key)[1]


def steps_of(key, shape, pieces, least, top_value):
    level, own = 1.0, jax.random.fold_in(key, 6)
    for position, blocks in pieces:
        draws = jnp.exp(jax.random.uniform(jax.random.fold_in(own, position), (blocks,), jnp.float32, least / len(pieces), top_value / len(pieces)))
        level = level * jnp.repeat(draws, shape[position] // blocks).reshape([-1 if axis == position else 1 for axis in range(len(shape))])
    return level


def noise(rng, extent, scale, bound, cuts=(), held_as=jnp.bfloat16):
    level = steps_of(rng, extent, cuts, -0.22, 0.18) if cuts else 1.0
    result = jax.random.normal(rng, extent, jnp.float32) * scale * level
    return jnp.minimum(jnp.maximum(result, -bound), bound).astype(held_as)


def setup_inputs(seed: int = 0) -> dict:
    streams_of = jax.random.split(jax.random.key(seed), 9)
    tokens = noise(streams_of[0], (TOKENS, D), 1.0, 6.0, ((0, 128),))
    cotangent = noise(streams_of[1], (TOKENS, D), 0.25, 1.5, ((0, 128),))
    route_gates = jnp.clip(jnp.exp(math.log(1.0) - 2.3025851 * jax.random.uniform(streams_of[2], (TOKENS, TOPK), jnp.float32) ** steps_of(streams_of[2], (TOKENS, TOPK), ((0, 128),), -0.2, 0.2)), 0.1, 1.0)
    expert_ids = draw_expert_ids(jax.random.fold_in(streams_of[8], 71), 0)
    slot_index = draw_slot_index(jax.random.fold_in(streams_of[8], 71), 0)
    w_gate = noise(streams_of[5], (EXPERTS, D, H), D ** -0.5, 0.125, ((0, 16),))
    w_up = noise(streams_of[6], (EXPERTS, D, H), D ** -0.5, 0.125, ((0, 16),))
    w_down = noise(streams_of[7], (EXPERTS, H, D), H ** -0.5, 0.21875, ((0, 16),))
    return dict(tokens=tokens, cotangent=cotangent, route_gates=route_gates, expert_ids=expert_ids, slot_index=slot_index, w_gate=w_gate, w_up=w_up, w_down=w_down)


def grouped_sum(left_rows, right_rows):
    left_full = left_rows.reshape(N_EXPERT, N_DP, CAP, left_rows.shape[1]).astype(jnp.float32)
    right_full = right_rows.reshape(N_EXPERT, N_DP, CAP, right_rows.shape[1]).astype(jnp.float32)
    partial_sums = jnp.einsum("adcm,adch->dmh", left_full, right_full).astype(jnp.bfloat16)
    partial_sums = lax.optimization_barrier(partial_sums)
    return jnp.sum(partial_sums.astype(jnp.float32), axis=0)


def reference(tokens, cotangent, route_gates, expert_ids, slot_index, w_gate, w_up, w_down):
    blocks = TOKENS // TOK_DEV
    cell_count = EXPERTS * CAP
    per_block = TOK_DEV * TOPK
    local_flat = (expert_ids * CAP + slot_index).reshape(blocks, per_block).astype(jnp.int32)
    block_ids = jnp.arange(blocks, dtype=jnp.int32)[:, None]
    block_grid = jnp.broadcast_to(block_ids, local_flat.shape)
    pair_grid = jnp.broadcast_to(jnp.arange(per_block, dtype=jnp.int32)[None, :], local_flat.shape)
    inverse = jnp.full((blocks, cell_count), per_block, jnp.int32).at[block_grid, local_flat].set(pair_grid)
    filled = inverse < per_block
    global_pair = jnp.where(filled, block_ids * per_block + inverse, TOKENS * TOPK).astype(jnp.int32)
    global_token = jnp.where(filled, block_ids * TOK_DEV + inverse // TOPK, TOKENS).astype(jnp.int32)
    gate_flat = route_gates.reshape(-1)

    def expert_step(carry, expert_index):
        out_total, grad_total, gate_total = carry
        pair_index = lax.dynamic_slice_in_dim(global_pair, expert_index * CAP, CAP, 1).reshape(-1)
        token_index = lax.dynamic_slice_in_dim(global_token, expert_index * CAP, CAP, 1).reshape(-1)
        routed = jnp.take(tokens, token_index, axis=0, mode="fill", fill_value=0)
        gate_value = jnp.take(gate_flat, pair_index, mode="fill", fill_value=0.0)
        gate_matrix = w_gate[expert_index]
        up_matrix = w_up[expert_index]
        down_matrix = w_down[expert_index]
        gate_pre = jnp.dot(routed, gate_matrix, preferred_element_type=jnp.float32)
        up_pre = jnp.dot(routed, up_matrix, preferred_element_type=jnp.float32)
        hidden = (jax.nn.silu(gate_pre) * up_pre).astype(jnp.bfloat16)
        out_rows = jnp.dot(hidden, down_matrix, preferred_element_type=jnp.float32).astype(jnp.bfloat16)
        out_wide = out_rows.astype(jnp.float32)
        cot_rows = jnp.take(cotangent, token_index, axis=0, mode="fill", fill_value=0).astype(jnp.float32)
        out_total = out_total.at[token_index].add(gate_value[:, None] * out_wide, mode="drop")
        gate_total = gate_total.at[pair_index].add(jnp.sum(cot_rows * out_wide, axis=1), mode="drop")
        grad_rows = (gate_value[:, None] * cot_rows).astype(jnp.bfloat16)
        grad_hidden = jnp.dot(grad_rows, down_matrix.T, preferred_element_type=jnp.float32)
        sigmoid_gate = jax.nn.sigmoid(gate_pre)
        grad_gate_pre = (grad_hidden * up_pre * sigmoid_gate * (1.0 + gate_pre * (1.0 - sigmoid_gate))).astype(jnp.bfloat16)
        grad_up_pre = (grad_hidden * gate_pre * sigmoid_gate).astype(jnp.bfloat16)
        grad_input = jnp.dot(grad_gate_pre, gate_matrix.T, preferred_element_type=jnp.float32)
        grad_input = grad_input + jnp.dot(grad_up_pre, up_matrix.T, preferred_element_type=jnp.float32)
        grad_input = grad_input.astype(jnp.bfloat16)
        grad_total = grad_total.at[token_index].add(grad_input.astype(jnp.float32), mode="drop")
        grad_gate_matrix = grouped_sum(routed, grad_gate_pre)
        grad_up_matrix = grouped_sum(routed, grad_up_pre)
        grad_down_matrix = grouped_sum(grad_rows, hidden).T
        return (out_total, grad_total, gate_total), (grad_gate_matrix, grad_up_matrix, grad_down_matrix)

    start_carry = (jnp.zeros((TOKENS, D), jnp.float32), jnp.zeros((TOKENS, D), jnp.float32), jnp.zeros((TOKENS * TOPK,), jnp.float32))
    final_carry, stacked = lax.scan(expert_step, start_carry, jnp.arange(EXPERTS, dtype=jnp.int32))
    out_total, grad_total, gate_total = final_carry
    layer_out = out_total.astype(jnp.bfloat16)
    grad_tokens = grad_total.astype(jnp.bfloat16)
    grad_gates = gate_total.reshape(TOKENS, TOPK)
    return (layer_out, grad_tokens, grad_gates, stacked[0], stacked[1], stacked[2])
```

```python
import functools

import jax
import jax.numpy as jnp
from jax import lax
from jax.experimental import pallas as pl
from jax.experimental.pallas import tpu as pltpu
from jax.sharding import PartitionSpec as P

MESH = pl.DeviceIdType.MESH
F32 = jnp.float32
BF16 = jnp.bfloat16
NX = 4
NY = 4


def slot_of(dx, dz, dc):
    return (dx % NX) * 4 + (dz % 2) * 2 + (dc % 2)


class Place:
    def __init__(self):
        e = lax.axis_index("expert")
        q = lax.axis_index("dp")
        self.e, self.q = e, q
        self.x, self.zl, self.c = e // 4, (e // 2) % 2, e % 2
        self.y, self.zh = q // 2, q % 2

    def group(self, dx=0, dz=0, dc=0):
        x = lax.rem(self.x + (dx % NX), NX) if dx % NX else self.x
        z = 1 - self.zl if dz % 2 else self.zl
        c = 1 - self.c if dc % 2 else self.c
        return (x * 4 + z * 2 + c, self.q)

    def col(self, dy=0, dz=0):
        y = lax.rem(self.y + (dy % NY), NY) if dy % NY else self.y
        z = 1 - self.zh if dz % 2 else self.zh
        return (self.e, y * 2 + z)


def enter(peers):
    barrier = pltpu.get_barrier_semaphore()
    for peer in peers:
        pl.semaphore_signal(barrier, inc=1, device_id=peer, device_id_type=MESH)
    pl.semaphore_wait(barrier, len(peers))


class Sends:
    def __init__(self, send_sem, recv_sem):
        self.send_sem, self.recv_sem = send_sem, recv_sem
        self.made = []

    def start(self, src, dst, peer):
        i = len(self.made)
        copy = pltpu.make_async_remote_copy(
            src_ref=src,
            dst_ref=dst,
            send_sem=self.send_sem.at[i],
            recv_sem=self.recv_sem.at[i],
            device_id=peer,
            device_id_type=MESH,
        )
        copy.start()
        self.made.append(copy)
        return copy

    def drain(self):
        for copy in self.made:
            copy.wait_send()


GROUP = [(dx, dz, dc) for dx in range(NX) for dz in range(2) for dc in range(2)]
A = (0, 64)
B = (64, 128)
A0, A1, B0, B1 = (0, 32), (32, 64), (64, 96), (96, 128)


def gather_rows(sends, place, own, buf):
    arrived = {}

    def push(dx, dz, dc, rows, ddx=0, ddz=0, ddc=0):
        lo, hi = rows
        here = own if (dx, dz, dc) == (0, 0, 0) else buf.at[slot_of(dx, dz, dc)]
        there = ((dx - ddx) % NX, (dz - ddz) % 2, (dc - ddc) % 2)
        arrived[there + (rows,)] = sends.start(
            here.at[pl.ds(lo, hi - lo)],
            buf.at[slot_of(*there), pl.ds(lo, hi - lo)],
            place.group(ddx, ddz, ddc),
        )

    def take(dx, dz, rows):
        arrived[(dx % NX, dz % 2, 0, rows)].wait_recv()
        push(dx % NX, dz % 2, 0, rows, ddc=1)

    yield
    push(0, 0, 0, B, ddz=1)
    push(0, 0, 0, A, ddx=1)
    push(0, 0, 0, A, ddx=-1)
    push(0, 0, 0, B, ddx=1)
    push(0, 0, 0, B, ddx=-1)
    push(0, 0, 0, A, ddz=1)
    push(0, 0, 0, (0, 128), ddc=1)
    yield
    take(0, 1, B)
    push(0, 1, 0, B, ddx=1)
    push(0, 1, 0, B, ddx=-1)
    yield
    take(1, 0, A)
    push(1, 0, 0, A0, ddx=-1)
    push(1, 0, 0, A, ddz=1)
    take(-1, 0, A)
    push(3, 0, 0, A1, ddx=1)
    push(3, 0, 0, A, ddz=1)
    yield
    take(1, 0, B)
    push(1, 0, 0, B0, ddx=-1)
    take(-1, 0, B)
    push(3, 0, 0, B1, ddx=1)
    take(0, 1, A)
    yield
    take(1, 1, B)
    push(1, 1, 0, B0, ddx=-1)
    take(-1, 1, B)
    push(3, 1, 0, B1, ddx=1)
    take(2, 0, A0)
    push(2, 0, 0, A0, ddz=1)
    take(2, 0, A1)
    push(2, 0, 0, A1, ddz=1)
    yield
    take(1, 1, A)
    take(3, 1, A)
    take(2, 0, B0)
    take(2, 0, B1)
    take(2, 1, B0)
    take(2, 1, B1)
    take(2, 1, A0)
    take(2, 1, A1)
    yield
    for key in list(arrived):
        if key[2] == 1:
            arrived[key].wait_recv()
    yield


def dispatch_kernel(tok, cot, meta, tok_all, cot_all, meta_all, send_sem, recv_sem, own_sem):
    place = Place()
    enter([place.group(*r) for r in GROUP[1:]])
    sends = Sends(send_sem, recv_sem)
    own = [
        pltpu.make_async_copy(tok, tok_all.at[0], own_sem.at[0]),
        pltpu.make_async_copy(cot, cot_all.at[0], own_sem.at[1]),
        pltpu.make_async_copy(meta, meta_all.at[0], own_sem.at[2]),
    ]
    metas = []
    for r in GROUP[1:]:
        dst = meta_all.at[slot_of(-r[0], r[1], r[2])]
        metas.append(sends.start(meta, dst, place.group(*r)))
    first = gather_rows(sends, place, tok, tok_all)
    second = gather_rows(sends, place, cot, cot_all)
    next(first)
    next(first)
    for copy in own:
        copy.start()
    next(first)
    next(first)
    next(first)
    next(first)
    next(second)
    next(second)
    for _ in first:
        pass
    for _ in second:
        pass
    for copy in metas:
        copy.wait_recv()
    for copy in own:
        copy.wait()
    sends.drain()


def dispatch(tok, cot, meta):
    n = 128
    hbm = pl.BlockSpec(memory_space=pl.ANY)
    return pl.pallas_call(
        dispatch_kernel,
        out_shape=(
            jax.ShapeDtypeStruct((16,) + tok.shape, BF16),
            jax.ShapeDtypeStruct((16,) + cot.shape, BF16),
            jax.ShapeDtypeStruct((16,) + meta.shape, F32),
        ),
        in_specs=[hbm, hbm, hbm],
        out_specs=(hbm, hbm, hbm),
        scratch_shapes=[
            pltpu.SemaphoreType.DMA((n,)),
            pltpu.SemaphoreType.DMA((n,)),
            pltpu.SemaphoreType.DMA((3,)),
        ],
        compiler_params=pltpu.CompilerParams(collective_id=0, has_side_effects=True),
    )(tok, cot, meta)


def add_into(dst, terms, chunk):
    rows = dst.shape[0]

    @pl.loop(0, rows // chunk)
    def _(i):
        at = pl.ds(pl.multiple_of(i * chunk, chunk), chunk)
        total = terms[0][at].astype(F32)
        for term in terms[1:]:
            total = total + term[at].astype(F32)
        dst[at] = total.astype(dst.dtype)


class Tree:
    def __init__(self, sends, peer, part, land, out, chunk):
        self.sends, self.peer, self.part = sends, peer, part
        self.land, self.out, self.chunk = land, out, chunk

    def open(self):
        s, p, peer = self.sends, self.part, self.peer
        self.far = [
            s.start(p(2, 0), self.land(0, 0), peer(-1)),
            s.start(p(2, 1), self.land(0, 1), peer(1)),
        ]
        self.near = [
            s.start(p(1, 0), self.land(1, 0), peer(1)),
            s.start(p(-1, 1), self.land(1, 1), peer(-1)),
        ]

    def relay(self):
        self.via = []
        for h, d in ((0, -1), (1, 1)):
            self.far[h].wait_recv()
            add_into(self.out(h), [self.part(d, h), self.land(0, h)], self.chunk)
            self.via.append(self.sends.start(self.out(h), self.land(2, h), self.peer(d)))

    def close(self, h):
        self.near[h].wait_recv()
        self.via[h].wait_recv()
        return [self.part(0, h), self.land(1, h), self.land(2, h)]


H_ROWS = 704
W_COLS = 256


def reduce_kernel(
    p_hbm, o_hbm, gates_in,
    rows_out, gates_out, grads_out,
    own_p, land_y, land_z, out_y, out_z, t_down, land_d, land_dz, out_d,
    t_rows, land_s, land_za, u_rows, land_xa, out_xa, land_xb, out_xb, v_rows, land_zb,
    gates_land, send_sem, recv_sem, load_sem,
):
    place = Place()
    peers = [place.group(*r) for r in GROUP[1:]] + [place.col(1), place.col(-1), place.col(0, 1)]
    enter(peers)
    sends = Sends(send_sem, recv_sem)
    loads = []

    def load(src, dst):
        copy = pltpu.make_async_copy(src, dst, load_sem.at[len(loads)])
        copy.start()
        loads.append(copy)
        return copy

    def yy(d):
        return lax.rem(place.y + (d % NY), NY) if d % NY else place.y

    def p_slice(m, e, d, z):
        at = pl.multiple_of((yy(d) * 2 + z) * W_COLS, W_COLS)
        return p_hbm.at[m, e, :, pl.ds(at, W_COLS)]

    shares = []
    for r in range(2):
        got = []
        for dx in range(NX):
            for dz in range(2):
                got.append(
                    sends.start(
                        o_hbm.at[r, slot_of(dx, dz, 1)], land_s.at[r, dx * 2 + dz],
                        place.group(0, 0, 1),
                    )
                )
        shares.append(got)
    down_z = {}
    own_loads = {}
    for e in range(2):
        for d in (2, 1, 3, 0):
            down_z[e, d] = sends.start(
                p_slice(2, e, d, 1 - place.zh), land_dz.at[e, d], place.col(0, 1)
            )
    trees = []
    for m in range(2):
        for e in range(2):
            me = m * 2 + e

            def part(d, h, m=m, e=e, me=me):
                return own_part(m, e, me, d, h)

            def own_part(m, e, me, d, h):
                return p_slice(m, e, d, h)

            def held(d, h, me=me):
                return own_p.at[me, {-1: 0, 1: 1, 0: 2 + h}[d]]

            def land(k, h, me=me):
                return land_y.at[me, k, h]

            def out(h, me=me):
                return out_y.at[me, h]

            tree = Tree(sends, place.col, part, land, out, 64)
            tree.open()
            tree.part = held
            own_loads[me] = [
                load(p_slice(m, e, -1, 0), own_p.at[me, 0]),
                load(p_slice(m, e, 1, 1), own_p.at[me, 1]),
                load(p_slice(m, e, 0, 0), own_p.at[me, 2]),
                load(p_slice(m, e, 0, 1), own_p.at[me, 3]),
            ]
            trees.append(tree)
    for e in range(2):
        own_loads[4 + e] = [
            load(p_slice(2, e, d, place.zh), t_down.at[e, d]) for d in range(NY)
        ]
    own_rows = [
        load(o_hbm.at[r, slot_of(dx, dz, 0)], t_rows.at[r, dx * 2 + dz])
        for r in range(2) for dx in range(NX) for dz in range(2)
    ]
    gate_sends = []
    for r in GROUP[1:]:
        gate_sends.append(
            sends.start(
                gates_in.at[slot_of(*r)], gates_land.at[slot_of(-r[0], r[1], r[2])],
                place.group(*r),
            )
        )

    row_state = []
    for r in range(2):
        for i in range(8):
            shares[r][i].wait_recv()
            own_rows[r * 8 + i].wait()
            add_into(t_rows.at[r, i], [t_rows.at[r, i], land_s.at[r, i]], 32)
        za = {}
        for dx in (2, 1, 3, 0):
            za[dx] = sends.start(
                t_rows.at[r, dx * 2 + 1, pl.ds(0, 64)], land_za.at[r, dx], place.group(0, 1, 0)
            )
        tb = []
        for dz in (1, 0):
            tree = Tree(
                sends, place.group,
                lambda d, h, r=r, dz=dz: t_rows.at[r, (d % NX) * 2 + dz, pl.ds(64 + 32 * h, 32)],
                lambda k, h, r=r, dz=dz: land_xb.at[r, dz, k, h],
                lambda h, r=r, dz=dz: out_xb.at[r, dz, h],
                32,
            )
            tree.open()
            tb.append(tree)
        row_state.append((za, tb))

    def rows_mid(r):
        za, tb = row_state[r]
        for dx in (2, 1, 3, 0):
            za[dx].wait_recv()
            add_into(
                u_rows.at[r, dx],
                [t_rows.at[r, dx * 2, pl.ds(0, 64)], land_za.at[r, dx]], 32,
            )
        ta = Tree(
            sends, place.group,
            lambda d, h: u_rows.at[r, d % NX, pl.ds(32 * h, 32)],
            lambda k, h: land_xa.at[r, k, h],
            lambda h: out_xa.at[r, h],
            32,
        )
        ta.open()
        for tree in tb:
            tree.relay()
        return ta

    def rows_end(r, ta):
        za, tb = row_state[r]
        ta.relay()
        for h in range(2):
            add_into(v_rows.at[r, 1, pl.ds(32 * h, 32)], tb[0].close(h), 32)
        zb = sends.start(v_rows.at[r, 1], land_zb.at[r], place.group(0, 1, 0))
        for h in range(2):
            add_into(v_rows.at[r, 0, pl.ds(32 * h, 32)], tb[1].close(h), 32)
        for h in range(2):
            add_into(rows_out.at[r, pl.ds(32 * h, 32)], ta.close(h), 32)
        zb.wait_recv()
        add_into(rows_out.at[r, pl.ds(64, 64)], [v_rows.at[r, 0], land_zb.at[r]], 32)

    def down_mid(e):
        for copy in own_loads[4 + e]:
            copy.wait()
        for d in (2, 1, 3, 0):
            down_z[e, d].wait_recv()
            add_into(t_down.at[e, d], [t_down.at[e, d], land_dz.at[e, d]], 64)
        half = H_ROWS // 2
        tree = Tree(
            sends, place.col,
            lambda d, h: t_down.at[e, d % NY, pl.ds(half * h, half)],
            lambda k, h: land_d.at[e, k, pl.ds(half * h, half)],
            lambda h: out_d.at[e, pl.ds(half * h, half)],
            32,
        )
        tree.open()
        return tree

    def down_end(e, tree):
        half = H_ROWS // 2
        for h in range(2):
            add_into(grads_out.at[2, e, pl.ds(half * h, half)], tree.close(h), 32)

    def y_relay(me):
        for copy in own_loads[me]:
            copy.wait()
        trees[me].relay()

    def y_end(me):
        tree = trees[me]
        for h in range(2):
            terms = tree.close(h)

            @pl.when(place.zh != h)
            def _():
                add_into(out_z.at[me], terms, 64)

            @pl.when(place.zh == h)
            def _():
                add_into(grads_out.at[me // 2, me % 2], terms, 64)

        return sends.start(out_z.at[me], land_z.at[me], place.col(0, 1))

    def z_end(me, copy):
        copy.wait_recv()
        dst = grads_out.at[me // 2, me % 2]
        add_into(dst, [dst, land_z.at[me]], 64)

    ta0 = rows_mid(0)
    y_relay(0)
    ta1 = rows_mid(1)
    y_relay(1)
    rows_end(0, ta0)
    d0 = down_mid(0)
    y_relay(2)
    rows_end(1, ta1)
    d1 = down_mid(1)
    y_relay(3)
    z0 = y_end(0)
    d0.relay()
    z1 = y_end(1)
    d1.relay()
    z2 = y_end(2)
    z_end(0, z0)
    down_end(0, d0)
    z3 = y_end(3)
    z_end(1, z1)
    down_end(1, d1)
    z_end(2, z2)
    for copy in gate_sends:
        copy.wait_recv()
    total = gates_in[0]
    for i in range(1, 16):
        total = total + gates_land[i]
    gates_out[...] = total
    z_end(3, z3)
    sends.drain()


def reduce_all(p_all, o_all, gates_in):
    d = o_all.shape[-1]
    n = 192
    hbm = pl.BlockSpec(memory_space=pl.ANY)
    vmem = pl.BlockSpec(memory_space=pltpu.VMEM)
    slab = (H_ROWS, W_COLS)

    def buf(*shape):
        return pltpu.VMEM(shape, BF16)

    return pl.pallas_call(
        reduce_kernel,
        out_shape=(
            jax.ShapeDtypeStruct((2, 128, d), BF16),
            jax.ShapeDtypeStruct((8, 128), F32),
            jax.ShapeDtypeStruct((3, 2) + slab, F32),
        ),
        in_specs=[hbm, hbm, vmem],
        out_specs=(vmem, vmem, vmem),
        scratch_shapes=[
            buf(4, 4, *slab), buf(4, 3, 2, *slab), buf(4, *slab), buf(4, 2, *slab),
            buf(4, *slab), buf(2, 4, *slab), buf(2, 3, *slab), buf(2, 4, *slab), buf(2, *slab),
            buf(2, 8, 128, d), buf(2, 8, 128, d), buf(2, 4, 64, d), buf(2, 4, 64, d),
            buf(2, 3, 2, 32, d), buf(2, 2, 32, d), buf(2, 2, 3, 2, 32, d), buf(2, 2, 2, 32, d),
            buf(2, 2, 64, d), buf(2, 64, d),
            pltpu.VMEM((16, 8, 128), F32),
            pltpu.SemaphoreType.DMA((n,)),
            pltpu.SemaphoreType.DMA((n,)),
            pltpu.SemaphoreType.DMA((64,)),
        ],
        compiler_params=pltpu.CompilerParams(
            collective_id=1, has_side_effects=True, vmem_limit_bytes=62 * 2**20
        ),
    )(p_all, o_all, gates_in)


def dot(spec, a, b):
    return jnp.einsum(spec, a, b, preferred_element_type=F32)


def shards(tokens, cotangent, route_gates, expert_ids, slot_index, w_gate, w_up, w_down):
    d = tokens.shape[1]
    target = (expert_ids * 32 + slot_index).astype(F32).T
    meta = jnp.zeros((16, 128), F32).at[0:6].set(target).at[8:14].set(route_gates.T)
    tok_all, cot_all, meta_all = dispatch(tokens, cotangent, meta)
    first = lax.axis_index("expert") * 64
    slots = (first + jnp.arange(64)).astype(F32)
    hit = meta_all[:, 0:6, None, :] == slots[None, None, :, None]
    pick = jnp.sum(hit, axis=1).astype(BF16)
    gate = jnp.sum(jnp.where(hit, meta_all[:, 8:14, None, :], 0.0), axis=(1, 3))

    def rows(block):
        return dot("bit,btd->bid", pick, block)

    def by_expert(v):
        return v.reshape(16, 2, 32, -1).transpose(1, 0, 2, 3).reshape(2, 512, -1)

    def by_block(v):
        return v.reshape(2, 16, 32, -1).transpose(1, 0, 2, 3).reshape(16, 64, -1)

    routed = by_expert(rows(tok_all).astype(BF16))
    cots = rows(cot_all)
    grad_rows = by_expert((gate[:, :, None] * cots).astype(BF16))
    gate_pre = dot("ecd,edh->ech", routed, w_gate)
    up_pre = dot("ecd,edh->ech", routed, w_up)
    hidden = (jax.nn.silu(gate_pre) * up_pre).astype(BF16)
    out_rows = by_block(dot("ech,ehd->ecd", hidden, w_down).astype(BF16)).astype(F32)
    o_out = dot("bit,bid->btd", pick, (gate[:, :, None] * out_rows).astype(BF16)).astype(BF16)
    gate_grad = jnp.sum(cots * out_rows, axis=2)
    gates_in = jnp.sum(jnp.where(hit, gate_grad[:, None, :, None], 0.0), axis=2)
    gates_in = jnp.pad(gates_in, ((0, 0), (0, 2), (0, 0)))
    grad_hidden = dot("ecd,ehd->ech", grad_rows, w_down)
    s = jax.nn.sigmoid(gate_pre)
    d_gate = (grad_hidden * up_pre * s * (1.0 + gate_pre * (1.0 - s))).astype(BF16)
    d_up = (grad_hidden * gate_pre * s).astype(BF16)
    d_in = dot("ech,edh->ecd", d_gate, w_gate) + dot("ech,edh->ecd", d_up, w_up)
    o_grad = dot("bit,bid->btd", pick, by_block(d_in.astype(BF16))).astype(BF16)
    p_all = jnp.stack(
        [
            dot("ech,ecd->ehd", d_gate, routed).astype(BF16),
            dot("ech,ecd->ehd", d_up, routed).astype(BF16),
            dot("ech,ecd->ehd", hidden, grad_rows).astype(BF16),
        ]
    )
    out, gates, grads = reduce_all(p_all, jnp.stack([o_out, o_grad]), gates_in)
    return (
        out[0],
        out[1],
        gates[0:6].T,
        grads[0].transpose(0, 2, 1),
        grads[1].transpose(0, 2, 1),
        grads[2],
    )


def solution(mesh):
    row = P(("expert", "dp"), None)
    weight = P("expert", None, None)
    return jax.shard_map(
        shards,
        mesh=mesh,
        in_specs=(row, row, row, row, row, weight, weight, weight),
        out_specs=(row, row, row, P("expert", "dp", None), P("expert", "dp", None), P("expert", None, "dp")),
        check_vma=False,
    )
```

```python
import functools

import jax
import jax.numpy as jnp
from jax import lax
from jax.experimental import pallas as pl
from jax.experimental.pallas import tpu as pltpu
from jax.sharding import PartitionSpec as P

MESH = pl.DeviceIdType.MESH
F32 = jnp.float32
BF16 = jnp.bfloat16
NX = 4
NY = 4
H_ROWS = 704
W_COLS = 256


def slot_of(dx, dz, dc):
    return (dx % NX) * 4 + (dz % 2) * 2 + (dc % 2)


class Place:
    def __init__(self):
        e = lax.axis_index("expert")
        q = lax.axis_index("dp")
        self.e, self.q = e, q
        self.x, self.zl, self.c = e // 4, (e // 2) % 2, e % 2
        self.y, self.zh = q // 2, q % 2

    def group(self, dx=0, dz=0, dc=0):
        x = lax.rem(self.x + (dx % NX), NX) if dx % NX else self.x
        z = 1 - self.zl if dz % 2 else self.zl
        c = 1 - self.c if dc % 2 else self.c
        return (x * 4 + z * 2 + c, self.q)

    def col(self, dy=0, dz=0):
        y = lax.rem(self.y + (dy % NY), NY) if dy % NY else self.y
        z = 1 - self.zh if dz % 2 else self.zh
        return (self.e, y * 2 + z)


def enter(peers):
    barrier = pltpu.get_barrier_semaphore()
    for peer in peers:
        pl.semaphore_signal(barrier, inc=1, device_id=peer, device_id_type=MESH)
    pl.semaphore_wait(barrier, len(peers))


class Sends:
    def __init__(self, send_sem, recv_sem):
        self.send_sem, self.recv_sem = send_sem, recv_sem
        self.made = []

    def start(self, src, dst, peer):
        i = len(self.made)
        copy = pltpu.make_async_remote_copy(
            src_ref=src,
            dst_ref=dst,
            send_sem=self.send_sem.at[i],
            recv_sem=self.recv_sem.at[i],
            device_id=peer,
            device_id_type=MESH,
        )
        copy.start()
        self.made.append(copy)
        return copy

    def drain(self):
        for copy in self.made:
            copy.wait_send()


GROUP = [(dx, dz, dc) for dx in range(NX) for dz in range(2) for dc in range(2)]
A = (0, 64)
B = (64, 128)
A0, A1, B0, B1 = (0, 32), (32, 64), (64, 96), (96, 128)


def gather_rows(sends, place, own, buf):
    arrived = {}

    def push(dx, dz, dc, rows, ddx=0, ddz=0, ddc=0):
        lo, hi = rows
        here = own if (dx, dz, dc) == (0, 0, 0) else buf.at[slot_of(dx, dz, dc)]
        there = ((dx - ddx) % NX, (dz - ddz) % 2, (dc - ddc) % 2)
        arrived[there + (rows,)] = sends.start(
            here.at[pl.ds(lo, hi - lo)],
            buf.at[slot_of(*there), pl.ds(lo, hi - lo)],
            place.group(ddx, ddz, ddc),
        )

    def take(dx, dz, rows):
        arrived[(dx % NX, dz % 2, 0, rows)].wait_recv()
        push(dx % NX, dz % 2, 0, rows, ddc=1)

    yield
    push(0, 0, 0, B, ddz=1)
    push(0, 0, 0, A, ddx=1)
    push(0, 0, 0, A, ddx=-1)
    push(0, 0, 0, B, ddx=1)
    push(0, 0, 0, B, ddx=-1)
    push(0, 0, 0, A, ddz=1)
    push(0, 0, 0, (0, 128), ddc=1)
    yield
    take(0, 1, B)
    push(0, 1, 0, B, ddx=1)
    push(0, 1, 0, B, ddx=-1)
    yield
    take(1, 0, A)
    push(1, 0, 0, A0, ddx=-1)
    push(1, 0, 0, A, ddz=1)
    take(-1, 0, A)
    push(3, 0, 0, A1, ddx=1)
    push(3, 0, 0, A, ddz=1)
    yield
    take(1, 0, B)
    push(1, 0, 0, B0, ddx=-1)
    take(-1, 0, B)
    push(3, 0, 0, B1, ddx=1)
    take(0, 1, A)
    yield
    take(1, 1, B)
    push(1, 1, 0, B0, ddx=-1)
    take(-1, 1, B)
    push(3, 1, 0, B1, ddx=1)
    take(2, 0, A0)
    push(2, 0, 0, A0, ddz=1)
    take(2, 0, A1)
    push(2, 0, 0, A1, ddz=1)
    yield
    take(1, 1, A)
    take(3, 1, A)
    take(2, 0, B0)
    take(2, 0, B1)
    take(2, 1, B0)
    take(2, 1, B1)
    take(2, 1, A0)
    take(2, 1, A1)
    yield
    for key in list(arrived):
        if key[2] == 1:
            arrived[key].wait_recv()
    yield


def forward_kernel(
    tok, cot, meta, wg_hbm, wu_hbm, wd_hbm,
    routed_o, dy_o, pre_o, hidden_o, rows_o, gates_o, pick,
    tok_all, cot_all, meta_all, wg, wu, wd, routed, y_rows, dy, pre, hidden, hidden_t, gate_col,
    send_sem, recv_sem, copy_sem,
):
    place = Place()
    enter([place.group(*r) for r in GROUP[1:]])
    copies = []

    def local(src, dst):
        copy = pltpu.make_async_copy(src, dst, copy_sem.at[len(copies)])
        copy.start()
        copies.append(copy)
        return copy

    tok_sends = Sends(send_sem.at[pl.ds(0, 48)], recv_sem.at[pl.ds(0, 48)])
    cot_sends = Sends(send_sem.at[pl.ds(48, 48)], recv_sem.at[pl.ds(48, 48)])
    sends = Sends(send_sem.at[pl.ds(96, 16)], recv_sem.at[pl.ds(96, 16)])
    metas = []
    for r in GROUP[1:]:
        dst = meta_all.at[slot_of(-r[0], r[1], r[2])]
        metas.append(sends.start(meta, dst, place.group(*r)))
    first = gather_rows(tok_sends, place, tok, tok_all)
    second = gather_rows(cot_sends, place, cot, cot_all)
    next(first)
    next(second)
    next(first)
    own = [local(tok, tok_all.at[0]), local(cot, cot_all.at[0]), local(meta, meta_all.at[0])]
    weights = [local(wg_hbm, wg), local(wu_hbm, wu), local(wd_hbm, wd)]
    next(first)
    for copy in metas:
        copy.wait_recv()
    for copy in own:
        copy.wait()
    slot = (lax.broadcasted_iota(jnp.int32, (64, 128), 0) + place.e * 64).astype(F32)

    @pl.loop(0, 16)
    def _(j):
        total = jnp.zeros((64, 128), F32)
        gate = jnp.zeros((64, 128), F32)
        for k in range(6):
            hit = slot == jnp.broadcast_to(meta_all[j, k : k + 1], (64, 128))
            total = total + jnp.where(hit, 1.0, 0.0)
            row = jnp.broadcast_to(meta_all[j, 8 + k : 9 + k], (64, 128))
            gate = gate + jnp.where(hit, row, 0.0)
        pick[j] = total.astype(BF16)
        gate_col[j] = jnp.broadcast_to(jnp.sum(gate, axis=1, keepdims=True), (64, 128))

    next(first)
    next(first)
    next(first)
    next(second)
    for _ in first:
        pass
    next(second)

    def rows32(j):
        return pl.ds(pl.multiple_of(j * 32, 32), 32)

    @pl.loop(0, 16)
    def _(j):
        got = jnp.dot(pick[j], tok_all[j], preferred_element_type=F32).astype(BF16)
        routed[0, rows32(j)] = got[0:32]
        routed[1, rows32(j)] = got[32:64]

    routed_out = local(routed, routed_o)
    next(second)
    for copy in weights:
        copy.wait()

    def up(e):
        pre[e, 0] = jnp.dot(routed[e], wg[e], preferred_element_type=F32)
        pre[e, 1] = jnp.dot(routed[e], wu[e], preferred_element_type=F32)

        @pl.loop(0, 16)
        def _(i):
            at = rows32(i)
            gate = pre[e, 0, at]
            hidden[e, at] = (gate * jax.nn.sigmoid(gate) * pre[e, 1, at]).astype(BF16)

        local(pre.at[e], pre_o.at[e])

    def down(e):
        hidden_t[e] = hidden[e].T
        local(hidden_t.at[e], hidden_o.at[e])
        for n in range(2):
            at = pl.ds(n * 1024, 1024)
            y_rows[e, :, at] = jnp.dot(
                hidden[e], wd[e, :, at], preferred_element_type=F32
            ).astype(BF16)

    up(0)
    next(second)
    up(1)
    next(second)
    down(0)
    next(second)
    down(1)
    tok_sends.drain()

    def both(ref, j):
        return jnp.concatenate([ref[0, rows32(j)], ref[1, rows32(j)]], axis=0)

    @pl.loop(0, 16)
    def _(j):
        scaled = (both(y_rows, j).astype(F32) * gate_col[j, :, 0:1]).astype(BF16)
        tok_all[j] = lax.dot_general(
            pick[j], scaled, (((0,), (0,)), ((), ())), preferred_element_type=F32
        ).astype(BF16)

    local(tok_all, rows_o)
    for _ in second:
        pass

    @pl.loop(0, 16)
    def _(j):
        got = jnp.dot(pick[j], cot_all[j], preferred_element_type=F32)
        by_slot = jnp.sum(got * both(y_rows, j).astype(F32), axis=1, keepdims=True)
        scaled = (got * gate_col[j, :, 0:1]).astype(BF16)
        dy[0, rows32(j)] = scaled[0:32]
        dy[1, rows32(j)] = scaled[32:64]
        by_slot = jnp.broadcast_to(by_slot, (64, 128))
        parts = []
        for k in range(6):
            hit = slot == jnp.broadcast_to(meta_all[j, k : k + 1], (64, 128))
            parts.append(jnp.sum(jnp.where(hit, by_slot, 0.0), axis=0, keepdims=True))
        parts.append(jnp.zeros((2, 128), F32))
        gates_o[j] = jnp.concatenate(parts, axis=0)

    local(dy, dy_o)
    for copy in copies[6:]:
        copy.wait()
    cot_sends.drain()
    sends.drain()


def forward(tok, cot, meta, w_gate, w_up, w_down):
    d = tok.shape[1]
    hbm = pl.BlockSpec(memory_space=pl.ANY)
    vmem = pl.BlockSpec(memory_space=pltpu.VMEM)
    return pl.pallas_call(
        forward_kernel,
        out_shape=(
            jax.ShapeDtypeStruct((2, 512, d), BF16),
            jax.ShapeDtypeStruct((2, 512, d), BF16),
            jax.ShapeDtypeStruct((2, 2, 512, H_ROWS), F32),
            jax.ShapeDtypeStruct((2, H_ROWS, 512), BF16),
            jax.ShapeDtypeStruct((16, 128, d), BF16),
            jax.ShapeDtypeStruct((16, 8, 128), F32),
            jax.ShapeDtypeStruct((16, 64, 128), BF16),
        ),
        in_specs=[hbm] * 6,
        out_specs=(hbm, hbm, hbm, hbm, hbm, vmem, vmem),
        scratch_shapes=[
            pltpu.VMEM((16, 128, d), BF16),
            pltpu.VMEM((16, 128, d), BF16),
            pltpu.VMEM((16,) + meta.shape, F32),
            pltpu.VMEM(w_gate.shape, BF16),
            pltpu.VMEM(w_up.shape, BF16),
            pltpu.VMEM(w_down.shape, BF16),
            pltpu.VMEM((2, 512, d), BF16),
            pltpu.VMEM((2, 512, d), BF16),
            pltpu.VMEM((2, 512, d), BF16),
            pltpu.VMEM((2, 2, 512, H_ROWS), F32),
            pltpu.VMEM((2, 512, H_ROWS), BF16),
            pltpu.VMEM((2, H_ROWS, 512), BF16),
            pltpu.VMEM((16, 64, 128), F32),
            pltpu.SemaphoreType.DMA((112,)),
            pltpu.SemaphoreType.DMA((112,)),
            pltpu.SemaphoreType.DMA((16,)),
        ],
        compiler_params=pltpu.CompilerParams(
            collective_id=0, has_side_effects=True, vmem_limit_bytes=62 * 2**20
        ),
    )(tok, cot, meta, w_gate, w_up, w_down)


def add_into(dst, terms, chunk):
    rows = dst.shape[0]

    @pl.loop(0, rows // chunk)
    def _(i):
        at = pl.ds(pl.multiple_of(i * chunk, chunk), chunk)
        total = terms[0][at].astype(F32)
        for term in terms[1:]:
            total = total + term[at].astype(F32)
        dst[at] = total.astype(dst.dtype)


class Tree:
    def __init__(self, sends, peer, part, land, out, chunk):
        self.sends, self.peer, self.part = sends, peer, part
        self.land, self.out, self.chunk = land, out, chunk

    def open(self):
        s, p, peer = self.sends, self.part, self.peer
        self.far = [
            s.start(p(2, 0), self.land(0, 0), peer(-1)),
            s.start(p(2, 1), self.land(0, 1), peer(1)),
        ]
        self.near = [
            s.start(p(1, 0), self.land(1, 0), peer(1)),
            s.start(p(-1, 1), self.land(1, 1), peer(-1)),
        ]

    def relay(self):
        self.via = []
        for h, d in ((0, -1), (1, 1)):
            self.far[h].wait_recv()
            add_into(self.out(h), [self.part(d, h), self.land(0, h)], self.chunk)
            self.via.append(self.sends.start(self.out(h), self.land(2, h), self.peer(d)))

    def close(self, h):
        self.near[h].wait_recv()
        self.via[h].wait_recv()
        return [self.part(0, h), self.land(1, h), self.land(2, h)]


def reduce_kernel(
    p_gate, p_up, p_down, o_first, o_second, gates_in,
    out_first, out_second, gates_out, grads_out,
    own_p, land_y, land_z, out_y, out_z, t_down, land_d, land_dz, out_d,
    t_rows, land_s, land_xb, out_xb, v_rows, land_zb,
    gates_land, send_sem, recv_sem, load_sem,
):
    place = Place()
    peers = [place.group(*r) for r in GROUP[1:]] + [place.col(1), place.col(-1), place.col(0, 1)]
    enter(peers)
    sends = Sends(send_sem, recv_sem)
    o_hbm = (o_first, o_second)
    p_hbm = (p_gate, p_up, p_down)
    rows_out = (out_first, out_second)
    loads = []

    def load(src, dst):
        copy = pltpu.make_async_copy(src, dst, load_sem.at[len(loads)])
        copy.start()
        loads.append(copy)
        return copy

    def yy(d):
        return lax.rem(place.y + (d % NY), NY) if d % NY else place.y

    def p_slice(m, e, d, z):
        at = pl.multiple_of((yy(d) * 2 + z) * W_COLS, W_COLS)
        return p_hbm[m].at[e, :, pl.ds(at, W_COLS)]

    shares = []
    for r in range(2):
        got = []
        for dx in range(NX):
            for dz in range(2):
                got.append(
                    sends.start(
                        o_hbm[r].at[slot_of(dx, dz, 1)], land_s.at[r, dx * 2 + dz],
                        place.group(0, 0, 1),
                    )
                )
        shares.append(got)
    down_z = {}
    own_loads = {}
    for e in range(2):
        for d in (2, 1, 3, 0):
            down_z[e, d] = sends.start(
                p_slice(2, e, d, 1 - place.zh), land_dz.at[e, d], place.col(0, 1)
            )
    trees = []
    for m in range(2):
        for e in range(2):
            me = m * 2 + e

            def part(d, h, m=m, e=e, me=me):
                return own_part(m, e, me, d, h)

            def own_part(m, e, me, d, h):
                return p_slice(m, e, d, h)

            def held(d, h, me=me):
                return own_p.at[me, {-1: 0, 1: 1, 0: 2 + h}[d]]

            def land(k, h, me=me):
                return land_y.at[me, k, h]

            def out(h, me=me):
                return out_y.at[me, h]

            tree = Tree(sends, place.col, part, land, out, 64)
            tree.open()
            tree.part = held
            own_loads[me] = [
                load(p_slice(m, e, -1, 0), own_p.at[me, 0]),
                load(p_slice(m, e, 1, 1), own_p.at[me, 1]),
                load(p_slice(m, e, 0, 0), own_p.at[me, 2]),
                load(p_slice(m, e, 0, 1), own_p.at[me, 3]),
            ]
            trees.append(tree)
    for e in range(2):
        own_loads[4 + e] = [
            load(p_slice(2, e, d, place.zh), t_down.at[e, d]) for d in range(NY)
        ]
    own_rows = [
        load(o_hbm[r].at[slot_of(dx, dz, 0)], t_rows.at[r, dx * 2 + dz])
        for r in range(2) for dx in range(NX) for dz in range(2)
    ]
    gate_sends = []
    for r in GROUP[1:]:
        gate_sends.append(
            sends.start(
                gates_in.at[slot_of(*r)], gates_land.at[slot_of(-r[0], r[1], r[2])],
                place.group(*r),
            )
        )

    row_state = []
    for r in range(2):
        for i in range(8):
            shares[r][i].wait_recv()
            own_rows[r * 8 + i].wait()
            add_into(t_rows.at[r, i], [t_rows.at[r, i], land_s.at[r, i]], 32)
        trees_x = []
        for dz in (1, 0):
            tree = Tree(
                sends, place.group,
                lambda d, h, r=r, dz=dz: t_rows.at[r, (d % NX) * 2 + dz, pl.ds(64 * h, 64)],
                lambda k, h, r=r, dz=dz: land_xb.at[r, dz, k, h],
                lambda h, r=r, dz=dz: out_xb.at[r, dz, h],
                32,
            )
            tree.open()
            trees_x.append(tree)
        row_state.append(trees_x)

    def rows_mid(r):
        for tree in row_state[r]:
            tree.relay()

    def rows_end(r):
        for h in range(2):
            add_into(v_rows.at[r, 1, pl.ds(64 * h, 64)], row_state[r][0].close(h), 32)
        copy = sends.start(v_rows.at[r, 1], land_zb.at[r], place.group(0, 1, 0))
        for h in range(2):
            add_into(v_rows.at[r, 0, pl.ds(64 * h, 64)], row_state[r][1].close(h), 32)
        return copy

    def rows_last(r, copy):
        copy.wait_recv()
        add_into(rows_out[r], [v_rows.at[r, 0], land_zb.at[r]], 32)

    def down_mid(e):
        for copy in own_loads[4 + e]:
            copy.wait()
        for d in (2, 1, 3, 0):
            down_z[e, d].wait_recv()
            add_into(t_down.at[e, d], [t_down.at[e, d], land_dz.at[e, d]], 64)
        half = H_ROWS // 2
        tree = Tree(
            sends, place.col,
            lambda d, h: t_down.at[e, d % NY, pl.ds(half * h, half)],
            lambda k, h: land_d.at[e, k, pl.ds(half * h, half)],
            lambda h: out_d.at[e, pl.ds(half * h, half)],
            32,
        )
        tree.open()
        return tree

    def down_end(e, tree):
        half = H_ROWS // 2
        for h in range(2):
            add_into(grads_out.at[2, e, pl.ds(half * h, half)], tree.close(h), 32)

    def y_relay(me):
        for copy in own_loads[me]:
            copy.wait()
        trees[me].relay()

    def y_end(me):
        tree = trees[me]
        for h in range(2):
            terms = tree.close(h)

            @pl.when(place.zh != h)
            def _():
                add_into(out_z.at[me], terms, 64)

            @pl.when(place.zh == h)
            def _():
                add_into(grads_out.at[me // 2, me % 2], terms, 64)

        return sends.start(out_z.at[me], land_z.at[me], place.col(0, 1))

    def z_end(me, copy):
        copy.wait_recv()
        dst = grads_out.at[me // 2, me % 2]
        add_into(dst, [dst, land_z.at[me]], 64)

    y_relay(0)
    rows_mid(0)
    y_relay(1)
    d0 = down_mid(0)
    rows_mid(1)
    y_relay(2)
    r0 = rows_end(0)
    d1 = down_mid(1)
    y_relay(3)
    z0 = y_end(0)
    r1 = rows_end(1)
    d0.relay()
    z1 = y_end(1)
    rows_last(0, r0)
    d1.relay()
    z2 = y_end(2)
    rows_last(1, r1)
    z_end(0, z0)
    down_end(0, d0)
    z3 = y_end(3)
    z_end(1, z1)
    down_end(1, d1)
    z_end(2, z2)
    for copy in gate_sends:
        copy.wait_recv()
    total = gates_in[0]
    for i in range(1, 16):
        total = total + gates_land[i]
    gates_out[...] = total
    z_end(3, z3)
    sends.drain()


def reduce_all(p_gate, p_up, p_down, o_first, o_second, gates_in):
    d = o_first.shape[-1]
    n = 192
    hbm = pl.BlockSpec(memory_space=pl.ANY)
    vmem = pl.BlockSpec(memory_space=pltpu.VMEM)
    slab = (H_ROWS, W_COLS)

    def buf(*shape):
        return pltpu.VMEM(shape, BF16)

    return pl.pallas_call(
        reduce_kernel,
        out_shape=(
            jax.ShapeDtypeStruct((128, d), BF16),
            jax.ShapeDtypeStruct((128, d), BF16),
            jax.ShapeDtypeStruct((8, 128), F32),
            jax.ShapeDtypeStruct((3, 2) + slab, F32),
        ),
        in_specs=[hbm] * 5 + [vmem],
        out_specs=(vmem,) * 4,
        scratch_shapes=[
            buf(4, 4, *slab), buf(4, 3, 2, *slab), buf(4, *slab), buf(4, 2, *slab),
            buf(4, *slab), buf(2, 4, *slab), buf(2, 3, *slab), buf(2, 4, *slab), buf(2, *slab),
            buf(2, 8, 128, d), buf(2, 8, 128, d), buf(2, 2, 3, 2, 64, d), buf(2, 2, 2, 64, d),
            buf(2, 2, 128, d), buf(2, 128, d),
            pltpu.VMEM((16, 8, 128), F32),
            pltpu.SemaphoreType.DMA((n,)),
            pltpu.SemaphoreType.DMA((n,)),
            pltpu.SemaphoreType.DMA((64,)),
        ],
        compiler_params=pltpu.CompilerParams(
            collective_id=1, has_side_effects=True, vmem_limit_bytes=62 * 2**20
        ),
    )(p_gate, p_up, p_down, o_first, o_second, gates_in)


def dot(spec, a, b):
    return jnp.einsum(spec, a, b, preferred_element_type=F32)


def shards(tokens, cotangent, route_gates, expert_ids, slot_index, w_gate, w_up, w_down):
    d = tokens.shape[1]
    target = (expert_ids * 32 + slot_index).astype(F32).T
    meta = jnp.zeros((16, 128), F32).at[0:6].set(target).at[8:14].set(route_gates.T)
    routed, grad_rows, pre, hidden_t, o_out, gates_in, pick = forward(
        tokens, cotangent, meta, w_gate, w_up, w_down
    )

    def by_block(v):
        return v.reshape(2, 16, 32, -1).transpose(1, 0, 2, 3).reshape(16, 64, -1)

    gate_pre, up_pre = pre[:, 0], pre[:, 1]
    grad_hidden = dot("ecd,ehd->ech", grad_rows, w_down)
    s = jax.nn.sigmoid(gate_pre)
    d_gate = (grad_hidden * up_pre * s * (1.0 + gate_pre * (1.0 - s))).astype(BF16)
    d_up = (grad_hidden * gate_pre * s).astype(BF16)
    d_in = dot("ech,edh->ecd", d_gate, w_gate) + dot("ech,edh->ecd", d_up, w_up)
    o_grad = dot("bit,bid->btd", pick, by_block(d_in.astype(BF16))).astype(BF16)
    out, grad, gates, grads = reduce_all(
        dot("ech,ecd->ehd", d_gate, routed).astype(BF16),
        dot("ech,ecd->ehd", d_up, routed).astype(BF16),
        dot("ehc,ecd->ehd", hidden_t, grad_rows).astype(BF16),
        o_out, o_grad, gates_in,
    )
    return (
        out,
        grad,
        gates[0:6].T,
        grads[0].transpose(0, 2, 1),
        grads[1].transpose(0, 2, 1),
        grads[2],
    )


def solution(mesh):
    row = P(("expert", "dp"), None)
    weight = P("expert", None, None)
    return jax.shard_map(
        shards,
        mesh=mesh,
        in_specs=(row, row, row, row, row, weight, weight, weight),
        out_specs=(row, row, row, P("expert", "dp", None), P("expert", "dp", None), P("expert", None, "dp")),
        check_vma=False,
    )
```

```python
import functools

import jax
import jax.numpy as jnp
from jax import lax
from jax.experimental import pallas as pl
from jax.experimental.pallas import tpu as pltpu
from jax.sharding import PartitionSpec as P

MESH = pl.DeviceIdType.MESH
F32 = jnp.float32
BF16 = jnp.bfloat16
NX = 4
NY = 4
H_ROWS = 704
W_COLS = 256


def slot_of(dx, dz, dc):
    return (dx % NX) * 4 + (dz % 2) * 2 + (dc % 2)


class Place:
    def __init__(self):
        e = lax.axis_index("expert")
        q = lax.axis_index("dp")
        self.e, self.q = e, q
        self.x, self.zl, self.c = e // 4, (e // 2) % 2, e % 2
        self.y, self.zh = q // 2, q % 2

    def group(self, dx=0, dz=0, dc=0):
        x = lax.rem(self.x + (dx % NX), NX) if dx % NX else self.x
        z = 1 - self.zl if dz % 2 else self.zl
        c = 1 - self.c if dc % 2 else self.c
        return (x * 4 + z * 2 + c, self.q)

    def col(self, dy=0, dz=0):
        y = lax.rem(self.y + (dy % NY), NY) if dy % NY else self.y
        z = 1 - self.zh if dz % 2 else self.zh
        return (self.e, y * 2 + z)


def enter(peers):
    barrier = pltpu.get_barrier_semaphore()
    for peer in peers:
        pl.semaphore_signal(barrier, inc=1, device_id=peer, device_id_type=MESH)
    pl.semaphore_wait(barrier, len(peers))


class Sent:
    def __init__(self, owner, i, dst):
        self.owner, self.i, self.dst = owner, i, dst

    def again(self):
        dst = self.dst()
        return pltpu.make_async_remote_copy(
            src_ref=dst,
            dst_ref=dst,
            send_sem=self.owner.send_sem.at[self.i],
            recv_sem=self.owner.recv_sem.at[self.i],
            device_id=self.owner.home,
            device_id_type=MESH,
        )

    def wait_recv(self):
        self.again().wait_recv()

    def wait_send(self):
        self.again().wait_send()


class Sends:
    def __init__(self, send_sem, recv_sem, place):
        self.send_sem, self.recv_sem = send_sem, recv_sem
        self.home = (place.e, place.q)
        self.made = []

    def start(self, src, dst, peer):
        i = len(self.made)
        pltpu.make_async_remote_copy(
            src_ref=src,
            dst_ref=dst(),
            send_sem=self.send_sem.at[i],
            recv_sem=self.recv_sem.at[i],
            device_id=peer,
            device_id_type=MESH,
        ).start()
        copy = Sent(self, i, dst)
        self.made.append(copy)
        return copy

    def drain(self):
        for copy in self.made:
            copy.wait_send()


def dot_nn(a, b):
    return jnp.dot(a, b, preferred_element_type=F32)


def dot_nt(a, b):
    return lax.dot_general(a, b, (((1,), (1,)), ((), ())), preferred_element_type=F32)


def dot_tn(a, b):
    return lax.dot_general(a, b, (((0,), (0,)), ((), ())), preferred_element_type=F32)


GROUP = [(dx, dz, dc) for dx in range(NX) for dz in range(2) for dc in range(2)]
A = (0, 64)
B = (64, 128)
A0, A1, B0, B1 = (0, 32), (32, 64), (64, 96), (96, 128)


def gather_rows(sends, place, own, buf):
    arrived = {}

    def push(dx, dz, dc, rows, ddx=0, ddz=0, ddc=0):
        lo, hi = rows
        here = own if (dx, dz, dc) == (0, 0, 0) else buf.at[slot_of(dx, dz, dc)]
        there = ((dx - ddx) % NX, (dz - ddz) % 2, (dc - ddc) % 2)
        arrived[there + (rows,)] = sends.start(
            here.at[pl.ds(lo, hi - lo)],
            lambda: buf.at[slot_of(*there), pl.ds(lo, hi - lo)],
            place.group(ddx, ddz, ddc),
        )

    def take(dx, dz, rows):
        arrived[(dx % NX, dz % 2, 0, rows)].wait_recv()
        push(dx % NX, dz % 2, 0, rows, ddc=1)

    yield
    push(0, 0, 0, B, ddz=1)
    push(0, 0, 0, A, ddx=1)
    push(0, 0, 0, A, ddx=-1)
    push(0, 0, 0, B, ddx=1)
    push(0, 0, 0, B, ddx=-1)
    push(0, 0, 0, A, ddz=1)
    push(0, 0, 0, (0, 128), ddc=1)
    yield
    take(0, 1, B)
    push(0, 1, 0, B, ddx=1)
    push(0, 1, 0, B, ddx=-1)
    yield
    take(1, 0, A)
    push(1, 0, 0, A0, ddx=-1)
    push(1, 0, 0, A, ddz=1)
    take(-1, 0, A)
    push(3, 0, 0, A1, ddx=1)
    push(3, 0, 0, A, ddz=1)
    yield
    take(1, 0, B)
    push(1, 0, 0, B0, ddx=-1)
    take(-1, 0, B)
    push(3, 0, 0, B1, ddx=1)
    take(0, 1, A)
    yield
    take(1, 1, B)
    push(1, 1, 0, B0, ddx=-1)
    take(-1, 1, B)
    push(3, 1, 0, B1, ddx=1)
    take(2, 0, A0)
    push(2, 0, 0, A0, ddz=1)
    take(2, 0, A1)
    push(2, 0, 0, A1, ddz=1)
    yield
    take(1, 1, A)
    take(3, 1, A)
    take(2, 0, B0)
    take(2, 0, B1)
    take(2, 1, B0)
    take(2, 1, B1)
    take(2, 1, A0)
    take(2, 1, A1)
    yield
    for key in list(arrived):
        if key[2] == 1:
            arrived[key].wait_recv()
    yield


def forward_kernel(
    tok, cot, meta, wg_hbm, wu_hbm, wd_hbm,
    routed_o, dy_o, pre_o, hidden_o, rows_o, gates_o, pick,
    tok_all, cot_all, meta_all, wg, wu, wd, routed, y_rows, dy, pre, hidden, hidden_t, gate_col,
    send_sem, recv_sem, copy_sem,
):
    place = Place()
    enter([place.group(*r) for r in GROUP[1:]])
    copies = []

    def local(src, dst):
        copy = pltpu.make_async_copy(src, dst, copy_sem.at[len(copies)])
        copy.start()
        copies.append(copy)
        return copy

    tok_sends = Sends(send_sem.at[pl.ds(0, 48)], recv_sem.at[pl.ds(0, 48)], place)
    cot_sends = Sends(send_sem.at[pl.ds(48, 48)], recv_sem.at[pl.ds(48, 48)], place)
    sends = Sends(send_sem.at[pl.ds(96, 16)], recv_sem.at[pl.ds(96, 16)], place)
    metas = []
    for r in GROUP[1:]:
        to = slot_of(-r[0], r[1], r[2])
        metas.append(sends.start(meta, lambda to=to: meta_all.at[to], place.group(*r)))
    first = gather_rows(tok_sends, place, tok, tok_all)
    second = gather_rows(cot_sends, place, cot, cot_all)
    next(first)
    next(second)
    next(first)
    own = [local(tok, tok_all.at[0]), local(cot, cot_all.at[0]), local(meta, meta_all.at[0])]
    weights = [local(wg_hbm, wg), local(wu_hbm, wu), local(wd_hbm, wd)]
    next(first)
    for copy in metas:
        copy.wait_recv()
    for copy in own:
        copy.wait()
    slot = (lax.broadcasted_iota(jnp.int32, (64, 128), 0) + place.e * 64).astype(F32)

    @pl.loop(0, 16)
    def _(j):
        total = jnp.zeros((64, 128), F32)
        gate = jnp.zeros((64, 128), F32)
        for k in range(6):
            hit = slot == jnp.broadcast_to(meta_all[j, k : k + 1], (64, 128))
            total = total + jnp.where(hit, 1.0, 0.0)
            row = jnp.broadcast_to(meta_all[j, 8 + k : 9 + k], (64, 128))
            gate = gate + jnp.where(hit, row, 0.0)
        pick[j] = total.astype(BF16)
        gate_col[j] = jnp.broadcast_to(jnp.sum(gate, axis=1, keepdims=True), (64, 128))

    next(first)
    next(first)
    next(first)
    next(second)
    for _ in first:
        pass
    next(second)

    def rows32(j):
        return pl.ds(pl.multiple_of(j * 32, 32), 32)

    @pl.loop(0, 16)
    def _(j):
        got = jnp.dot(pick[j], tok_all[j], preferred_element_type=F32).astype(BF16)
        routed[0, rows32(j)] = got[0:32]
        routed[1, rows32(j)] = got[32:64]

    routed_out = local(routed, routed_o)
    next(second)
    for copy in weights:
        copy.wait()

    def up(e):
        pre[e, 0] = dot_nt(routed[e], wg[e])
        pre[e, 1] = dot_nt(routed[e], wu[e])

        @pl.loop(0, 16)
        def _(i):
            at = rows32(i)
            gate = pre[e, 0, at]
            hidden[e, at] = (gate * jax.nn.sigmoid(gate) * pre[e, 1, at]).astype(BF16)

        local(pre.at[e], pre_o.at[e])

    def down(e):
        hidden_t[e] = hidden[e].T
        local(hidden_t.at[e], hidden_o.at[e])
        for n in range(2):
            at = pl.ds(n * 1024, 1024)
            y_rows[e, :, at] = jnp.dot(
                hidden[e], wd[e, :, at], preferred_element_type=F32
            ).astype(BF16)

    up(0)
    next(second)
    up(1)
    next(second)
    down(0)
    next(second)
    down(1)
    tok_sends.drain()

    def both(ref, j):
        return jnp.concatenate([ref[0, rows32(j)], ref[1, rows32(j)]], axis=0)

    @pl.loop(0, 16)
    def _(j):
        scaled = (both(y_rows, j).astype(F32) * gate_col[j, :, 0:1]).astype(BF16)
        tok_all[j] = lax.dot_general(
            pick[j], scaled, (((0,), (0,)), ((), ())), preferred_element_type=F32
        ).astype(BF16)

    local(tok_all, rows_o)
    for _ in second:
        pass

    @pl.loop(0, 16)
    def _(j):
        got = jnp.dot(pick[j], cot_all[j], preferred_element_type=F32)
        by_slot = jnp.sum(got * both(y_rows, j).astype(F32), axis=1, keepdims=True)
        scaled = (got * gate_col[j, :, 0:1]).astype(BF16)
        dy[0, rows32(j)] = scaled[0:32]
        dy[1, rows32(j)] = scaled[32:64]
        by_slot = jnp.broadcast_to(by_slot, (64, 128))
        parts = []
        for k in range(6):
            hit = slot == jnp.broadcast_to(meta_all[j, k : k + 1], (64, 128))
            parts.append(jnp.sum(jnp.where(hit, by_slot, 0.0), axis=0, keepdims=True))
        parts.append(jnp.zeros((2, 128), F32))
        gates_o[j] = jnp.concatenate(parts, axis=0)

    local(dy, dy_o)
    for copy in copies[6:]:
        copy.wait()
    cot_sends.drain()
    sends.drain()


def forward(tok, cot, meta, w_gate, w_up, w_down):
    d = tok.shape[1]
    hbm = pl.BlockSpec(memory_space=pl.ANY)
    vmem = pl.BlockSpec(memory_space=pltpu.VMEM)
    return pl.pallas_call(
        forward_kernel,
        out_shape=(
            jax.ShapeDtypeStruct((2, 512, d), BF16),
            jax.ShapeDtypeStruct((2, 512, d), BF16),
            jax.ShapeDtypeStruct((2, 2, 512, H_ROWS), F32),
            jax.ShapeDtypeStruct((2, H_ROWS, 512), BF16),
            jax.ShapeDtypeStruct((16, 128, d), BF16),
            jax.ShapeDtypeStruct((16, 8, 128), F32),
            jax.ShapeDtypeStruct((16, 64, 128), BF16),
        ),
        in_specs=[hbm] * 6,
        out_specs=(hbm, hbm, hbm, hbm, hbm, vmem, vmem),
        scratch_shapes=[
            pltpu.VMEM((16, 128, d), BF16),
            pltpu.VMEM((16, 128, d), BF16),
            pltpu.VMEM((16,) + meta.shape, F32),
            pltpu.VMEM(w_gate.shape, BF16),
            pltpu.VMEM(w_up.shape, BF16),
            pltpu.VMEM(w_down.shape, BF16),
            pltpu.VMEM((2, 512, d), BF16),
            pltpu.VMEM((2, 512, d), BF16),
            pltpu.VMEM((2, 512, d), BF16),
            pltpu.VMEM((2, 2, 512, H_ROWS), F32),
            pltpu.VMEM((2, 512, H_ROWS), BF16),
            pltpu.VMEM((2, H_ROWS, 512), BF16),
            pltpu.VMEM((16, 64, 128), F32),
            pltpu.SemaphoreType.DMA((112,)),
            pltpu.SemaphoreType.DMA((112,)),
            pltpu.SemaphoreType.DMA((16,)),
        ],
        compiler_params=pltpu.CompilerParams(
            collective_id=0, has_side_effects=True, vmem_limit_bytes=62 * 2**20
        ),
    )(tok, cot, meta, w_gate, w_up, w_down)


def add_into(dst, terms, chunk):
    rows = dst.shape[0]

    @pl.loop(0, rows // chunk)
    def _(i):
        at = pl.ds(pl.multiple_of(i * chunk, chunk), chunk)
        total = terms[0][at].astype(F32)
        for term in terms[1:]:
            total = total + term[at].astype(F32)
        dst[at] = total.astype(dst.dtype)


class Tree:
    def __init__(self, sends, peer, part, land, out, chunk):
        self.sends, self.peer, self.part = sends, peer, part
        self.land, self.out, self.chunk = land, out, chunk

    def open(self):
        s, p, peer = self.sends, self.part, self.peer
        self.far = [
            s.start(p(2, 0), lambda: self.land(0, 0), peer(-1)),
            s.start(p(2, 1), lambda: self.land(0, 1), peer(1)),
        ]
        self.near = [
            s.start(p(1, 0), lambda: self.land(1, 0), peer(1)),
            s.start(p(-1, 1), lambda: self.land(1, 1), peer(-1)),
        ]

    def relay(self):
        self.via = []
        for h, d in ((0, -1), (1, 1)):
            self.far[h].wait_recv()
            add_into(self.out(h), [self.part(d, h), self.land(0, h)], self.chunk)
            self.via.append(self.sends.start(self.out(h), lambda h=h: self.land(2, h), self.peer(d)))

    def close(self, h):
        self.near[h].wait_recv()
        self.via[h].wait_recv()
        return [self.part(0, h), self.land(1, h), self.land(2, h)]


Y_FIRST = ((2, 0), (0, 0), (0, 1), (1, 1))
Z_FIRST = ((2, 1), (1, 0))


def backward_kernel(
    routed_hbm, dy_hbm, pre_hbm, hidden_hbm, wg_hbm, wu_hbm, wd_hbm, o_first, gates_in, pick,
    out_first, out_second, gates_out, grads_out, p_hbm, o_own, land_s,
    land_y, land_z, land_d, land_dz, land_xb, land_zb, gates_land,
    send_sem, recv_sem, load_sem,
):
    place = Place()
    loads = []

    def load(src, dst):
        copy = pltpu.make_async_copy(src, dst, load_sem.at[len(loads)])
        copy.start()
        loads.append(copy)
        return copy

    rows_out = (out_first, out_second)
    sends = Sends(send_sem, recv_sem, place)

    def yy(d):
        return lax.rem(place.y + (d % NY), NY) if d % NY else place.y

    def p_slice(m, e, d, z):
        at = pl.multiple_of((yy(d) * 2 + z) * W_COLS, W_COLS)
        return p_hbm.at[m, e, :, pl.ds(at, W_COLS)]

    trees = {}
    down_z = {}

    def open_partial(m, e):
        if (m, e) in Y_FIRST:
            i = Y_FIRST.index((m, e))
            tree = Tree(
                sends, place.col,
                lambda d, h: p_slice(m, e, d, h),
                lambda k, h: land_y.at[i, k, h],
                None, 64,
            )
            tree.open()
            trees[i] = tree
        else:
            i = Z_FIRST.index((m, e))
            for d in (2, 1, 3, 0):
                down_z[i, d] = sends.start(
                    p_slice(m, e, d, 1 - place.zh), lambda d=d: land_dz.at[i, d], place.col(0, 1)
                )

    shares = {}

    def first_phase(
        routed, dy, pre, hidden_t, wg, wu, wd, dhd, dg, du, dg_t, du_t, stage, o_stage
    ):
        ld = [
            load(hidden_hbm, hidden_t), load(dy_hbm, dy), load(wd_hbm.at[0], wd),
            load(pre_hbm.at[0], pre), load(routed_hbm, routed),
            load(wg_hbm.at[0], wg), load(wu_hbm.at[0], wu),
        ]
        peers = [place.group(*r) for r in GROUP[1:]]
        enter(peers + [place.col(1), place.col(-1), place.col(0, 1)])
        for dx in range(NX):
            for dz in range(2):
                i = dx * 2 + dz
                shares[0, i] = sends.start(
                    o_first.at[slot_of(dx, dz, 1)], lambda i=i: land_s.at[0, i],
                    place.group(0, 0, 1),
                )
        gate_sends = []
        for r in GROUP[1:]:
            to = slot_of(-r[0], r[1], r[2])
            gate_sends.append(
                sends.start(
                    gates_in.at[slot_of(*r)], lambda to=to: gates_land.at[to], place.group(*r)
                )
            )
        pending = []

        def flush():
            for copies, m, e in pending:
                for copy in copies:
                    copy.wait()
                open_partial(m, e)
            pending.clear()

        def partial(m, e, left, right):
            copies = []
            before = list(pending)
            for n in range(2):
                for entry in before:
                    entry[0][n].wait()

                @pl.loop(0, 2)
                def _(k):
                    at = pl.ds(pl.multiple_of(k * 512, 512), 512)
                    src = pl.ds(pl.multiple_of(n * 1024 + k * 512, 512), 512)
                    stage[n, :, at] = dot_nn(left[...], right[:, src]).astype(BF16)

                copies.append(
                    load(stage.at[n], p_hbm.at[m, e, :, pl.ds(n * 1024, 1024)])
                )
            for entry in before:
                open_partial(entry[1], entry[2])
                pending.remove(entry)
            pending.append((copies, m, e))

        ld[0].wait()
        ld[1].wait()
        partial(2, 0, hidden_t.at[0], dy.at[0])
        partial(2, 1, hidden_t.at[1], dy.at[1])
        for e in range(2):
            if e == 0:
                ld[2].wait()
                ld[3].wait()
                ld[4].wait()
                ld[5].wait()
                ld[6].wait()
            else:
                next_wd.wait()
                next_pre.wait()
            dhd[...] = dot_nt(dy[e], wd[...])
            if e == 0:
                next_wd = load(wd_hbm.at[1], wd)

            @pl.loop(0, 16)
            def _(i):
                at = pl.ds(pl.multiple_of(i * 32, 32), 32)
                gate = pre[0, at]
                s = jax.nn.sigmoid(gate)
                back = dhd[at]
                dg[at] = (back * pre[1, at] * s * (1.0 + gate * (1.0 - s))).astype(BF16)
                du[at] = (back * gate * s).astype(BF16)

            if e == 0:
                next_pre = load(pre_hbm.at[1], pre)
            dg_t[...] = dg[...].T
            du_t[...] = du[...].T
            partial(0, e, dg_t, routed.at[e])
            partial(1, e, du_t, routed.at[e])
            if e == 1:
                for copy in next_w:
                    copy.wait()

            @pl.loop(0, 4)
            def _(n):
                at = pl.ds(pl.multiple_of(n * 512, 512), 512)
                total = dot_nn(dg[...], wg[:, at]) + dot_nn(du[...], wu[:, at])
                routed[e, :, at] = total.astype(BF16)

            if e == 0:
                next_w = [load(wg_hbm.at[1], wg), load(wu_hbm.at[1], wu)]
        for entry in pending:
            for copy in entry[0]:
                copy.wait()
            open_partial(entry[1], entry[2])

        def back_rows(j):
            at = pl.ds(pl.multiple_of(j * 32, 32), 32)
            rows = jnp.concatenate([routed[0, at], routed[1, at]], axis=0)
            return dot_tn(pick[j], rows).astype(BF16)

        @pl.loop(0, 8)
        def _(i):
            at = pl.ds(pl.multiple_of(lax.rem(i, 4) * 128, 128), 128)
            dy[i // 4, at] = back_rows(i * 2 + 1)

        for i in range(8):
            shares[1, i] = sends.start(
                dy.at[i // 4, pl.ds((i % 4) * 128, 128)], lambda i=i: land_s.at[1, i],
                place.group(0, 0, 1),
            )
        outs = []
        for i in range(8):
            if i >= 2:
                outs[i - 2].wait()
            o_stage[i % 2] = back_rows(i * 2)
            outs.append(load(o_stage.at[i % 2], o_own.at[i]))
        for copy in outs[6:]:
            copy.wait()
        for i in range(8):
            shares[1, i].wait_send()
        for copy in gate_sends:
            copy.wait_recv()
        total = gates_in[0]
        for i in range(1, 16):
            total = total + gates_land[i]
        gates_out[...] = total

    def second_phase(own_p, out_y, out_z, t_down, out_d, t_rows, s_stage, out_xb, v_rows):
        own_rows = []
        for r in range(2):
            for i in range(8):
                src = o_first.at[i * 2] if r == 0 else o_own.at[i]
                own_rows.append(load(src, t_rows.at[r, i]))
        own_loads = {}
        for i, (m, e) in enumerate(Y_FIRST):
            own_loads[i] = [
                load(p_slice(m, e, -1, 0), own_p.at[i, 0]),
                load(p_slice(m, e, 1, 1), own_p.at[i, 1]),
                load(p_slice(m, e, 0, 0), own_p.at[i, 2]),
                load(p_slice(m, e, 0, 1), own_p.at[i, 3]),
            ]
        down_loads = {}
        for i, (m, e) in enumerate(Z_FIRST):
            down_loads[i] = [load(p_slice(m, e, d, place.zh), t_down.at[i, d]) for d in range(NY)]

        row_state = {}

        def rows_start(r):
            gets = []
            for i in range(8):
                shares[r, i].wait_recv()
            for i in range(9):
                if i < 8:
                    gets.append(load(land_s.at[r, i], s_stage.at[i % 2]))
                if i > 0:
                    gets[i - 1].wait()
                    own_rows[r * 8 + i - 1].wait()
                    dst = t_rows.at[r, i - 1]
                    add_into(dst, [dst, s_stage.at[(i - 1) % 2]], 32)
            made = []
            for dz in (1, 0):
                tree = Tree(
                    sends, place.group,
                    lambda d, h, dz=dz: t_rows.at[r, (d % NX) * 2 + dz, pl.ds(64 * h, 64)],
                    lambda k, h, dz=dz: land_xb.at[r, dz, k, h],
                    lambda h, dz=dz: out_xb.at[r, dz, h],
                    32,
                )
                tree.open()
                made.append(tree)
            row_state[r] = made

        def rows_mid(r):
            for tree in row_state[r]:
                tree.relay()

        def rows_end(r):
            for h in range(2):
                add_into(v_rows.at[r, 1, pl.ds(64 * h, 64)], row_state[r][0].close(h), 32)
            copy = sends.start(v_rows.at[r, 1], lambda: land_zb.at[r], place.group(0, 1, 0))
            for h in range(2):
                add_into(v_rows.at[r, 0, pl.ds(64 * h, 64)], row_state[r][1].close(h), 32)
            return copy

        def rows_last(r, copy):
            copy.wait_recv()
            add_into(rows_out[r], [v_rows.at[r, 0], land_zb.at[r]], 32)

        def down_mid(i):
            for copy in down_loads[i]:
                copy.wait()
            for d in (2, 1, 3, 0):
                down_z[i, d].wait_recv()
                add_into(t_down.at[i, d], [t_down.at[i, d], land_dz.at[i, d]], 64)
            half = H_ROWS // 2
            tree = Tree(
                sends, place.col,
                lambda d, h: t_down.at[i, d % NY, pl.ds(half * h, half)],
                lambda k, h: land_d.at[i, k, pl.ds(half * h, half)],
                lambda h: out_d.at[i, pl.ds(half * h, half)],
                32,
            )
            tree.open()
            return tree

        def down_end(i, tree):
            m, e = Z_FIRST[i]
            half = H_ROWS // 2
            for h in range(2):
                add_into(grads_out.at[m, e, pl.ds(half * h, half)], tree.close(h), 32)

        def y_relay(i):
            for copy in own_loads[i]:
                copy.wait()
            trees[i].part = lambda d, h: own_p.at[i, {-1: 0, 1: 1, 0: 2 + h}[d]]
            trees[i].out = lambda h: out_y.at[i, h]
            trees[i].relay()

        def y_end(i):
            m, e = Y_FIRST[i]
            for h in range(2):
                terms = trees[i].close(h)

                @pl.when(place.zh != h)
                def _():
                    add_into(out_z.at[i], terms, 64)

                @pl.when(place.zh == h)
                def _():
                    add_into(grads_out.at[m, e], terms, 64)

            return sends.start(out_z.at[i], lambda: land_z.at[i], place.col(0, 1))

        def z_end(i, copy):
            m, e = Y_FIRST[i]
            copy.wait_recv()
            dst = grads_out.at[m, e]
            add_into(dst, [dst, land_z.at[i]], 64)

        rows_start(0)
        y_relay(0)
        rows_start(1)
        d0 = down_mid(0)
        rows_mid(0)
        y_relay(1)
        rows_mid(1)
        y_relay(2)
        r0 = rows_end(0)
        d1 = down_mid(1)
        y_relay(3)
        z0 = y_end(0)
        r1 = rows_end(1)
        d0.relay()
        z1 = y_end(1)
        rows_last(0, r0)
        d1.relay()
        z2 = y_end(2)
        rows_last(1, r1)
        z_end(0, z0)
        down_end(0, d0)
        z3 = y_end(3)
        z_end(1, z1)
        down_end(1, d1)
        z_end(2, z2)
        z_end(3, z3)
        for copy in sends.made:
            if all(copy is not c for (r, _), c in shares.items() if r == 1):
                copy.wait_send()

    def buf(*shape):
        return pltpu.VMEM(shape, BF16)

    d = o_first.shape[-1]
    slab = (H_ROWS, W_COLS)
    pl.run_scoped(
        first_phase,
        buf(2, 512, d), buf(2, 512, d), pltpu.VMEM((2, 512, H_ROWS), F32), buf(2, H_ROWS, 512),
        buf(H_ROWS, d), buf(H_ROWS, d), buf(H_ROWS, d), pltpu.VMEM((512, H_ROWS), F32),
        buf(512, H_ROWS), buf(512, H_ROWS), buf(H_ROWS, 512), buf(H_ROWS, 512),
        buf(2, H_ROWS, 1024), buf(2, 128, d),
    )
    pl.run_scoped(
        second_phase,
        buf(4, 4, *slab), buf(4, 2, *slab), buf(4, *slab), buf(2, 4, *slab), buf(2, *slab),
        buf(2, 8, 128, d), buf(2, 128, d), buf(2, 2, 2, 64, d), buf(2, 2, 128, d),
    )


def backward(*operands):
    d = operands[0].shape[-1]
    n = 192
    hbm = pl.BlockSpec(memory_space=pl.ANY)
    vmem = pl.BlockSpec(memory_space=pltpu.VMEM)
    slab = (H_ROWS, W_COLS)

    def buf(*shape):
        return pltpu.VMEM(shape, BF16)

    return pl.pallas_call(
        backward_kernel,
        out_shape=(
            jax.ShapeDtypeStruct((128, d), BF16),
            jax.ShapeDtypeStruct((128, d), BF16),
            jax.ShapeDtypeStruct((8, 128), F32),
            jax.ShapeDtypeStruct((3, 2) + slab, F32),
            jax.ShapeDtypeStruct((3, 2, H_ROWS, d), BF16),
            jax.ShapeDtypeStruct((8, 128, d), BF16),
            jax.ShapeDtypeStruct((2, 8, 128, d), BF16),
        ),
        in_specs=[hbm] * 8 + [vmem] * 2,
        out_specs=(vmem,) * 4 + (hbm,) * 3,
        scratch_shapes=[
            buf(4, 3, 2, *slab), buf(4, *slab), buf(2, 3, *slab), buf(2, 4, *slab),
            buf(2, 2, 3, 2, 64, d), buf(2, 128, d),
            pltpu.VMEM((16, 8, 128), F32),
            pltpu.SemaphoreType.DMA((n,)),
            pltpu.SemaphoreType.DMA((n,)),
            pltpu.SemaphoreType.DMA((112,)),
        ],
        compiler_params=pltpu.CompilerParams(
            collective_id=1, has_side_effects=True, vmem_limit_bytes=63 * 2**20
        ),
    )(*operands)[:4]


def shards(tokens, cotangent, route_gates, expert_ids, slot_index, w_gate, w_up, w_down):
    target = (expert_ids * 32 + slot_index).astype(F32).T
    meta = jnp.zeros((16, 128), F32).at[0:6].set(target).at[8:14].set(route_gates.T)
    wg, wu = w_gate.transpose(0, 2, 1), w_up.transpose(0, 2, 1)
    routed, grad_rows, pre, hidden_t, o_out, gates_in, pick = forward(
        tokens, cotangent, meta, wg, wu, w_down
    )
    out, grad, gates, grads = backward(
        routed, grad_rows, pre, hidden_t, wg, wu, w_down, o_out, gates_in, pick
    )
    return (
        out,
        grad,
        gates[0:6].T,
        grads[0].transpose(0, 2, 1),
        grads[1].transpose(0, 2, 1),
        grads[2],
    )


def solution(mesh):
    row = P(("expert", "dp"), None)
    weight = P("expert", None, None)
    return jax.shard_map(
        shards,
        mesh=mesh,
        in_specs=(row, row, row, row, row, weight, weight, weight),
        out_specs=(row, row, row, P("expert", "dp", None), P("expert", "dp", None), P("expert", None, "dp")),
        check_vma=False,
    )
```

```python
import functools

import jax
import jax.numpy as jnp
from jax import lax
from jax.experimental import pallas as pl
from jax.experimental.pallas import tpu as pltpu
from jax.sharding import PartitionSpec as P

MESH = pl.DeviceIdType.MESH
F32 = jnp.float32
BF16 = jnp.bfloat16
NX = 4
NY = 4
H_ROWS = 704
W_COLS = 256


def slot_of(dx, dz, dc):
    return (dx % NX) * 4 + (dz % 2) * 2 + (dc % 2)


class Place:
    def __init__(self):
        e = lax.axis_index("expert")
        q = lax.axis_index("dp")
        self.e, self.q = e, q
        self.x, self.zl, self.c = e // 4, (e // 2) % 2, e % 2
        self.y, self.zh = q // 2, q % 2

    def group(self, dx=0, dz=0, dc=0):
        x = lax.rem(self.x + (dx % NX), NX) if dx % NX else self.x
        z = 1 - self.zl if dz % 2 else self.zl
        c = 1 - self.c if dc % 2 else self.c
        return (x * 4 + z * 2 + c, self.q)

    def col(self, dy=0, dz=0):
        y = lax.rem(self.y + (dy % NY), NY) if dy % NY else self.y
        z = 1 - self.zh if dz % 2 else self.zh
        return (self.e, y * 2 + z)


def enter(peers):
    barrier = pltpu.get_barrier_semaphore()
    for peer in peers:
        pl.semaphore_signal(barrier, inc=1, device_id=peer, device_id_type=MESH)
    pl.semaphore_wait(barrier, len(peers))


class Sent:
    def __init__(self, owner, i, dst):
        self.owner, self.i, self.dst = owner, i, dst

    def again(self):
        dst = self.dst()
        return pltpu.make_async_remote_copy(
            src_ref=dst,
            dst_ref=dst,
            send_sem=self.owner.send_sem.at[self.i],
            recv_sem=self.owner.recv_sem.at[self.i],
            device_id=self.owner.home,
            device_id_type=MESH,
        )

    def wait_recv(self):
        self.again().wait_recv()

    def wait_send(self):
        self.again().wait_send()


class Sends:
    def __init__(self, send_sem, recv_sem, place):
        self.send_sem, self.recv_sem = send_sem, recv_sem
        self.home = (place.e, place.q)
        self.made = []

    def start(self, src, dst, peer):
        i = len(self.made)
        pltpu.make_async_remote_copy(
            src_ref=src,
            dst_ref=dst(),
            send_sem=self.send_sem.at[i],
            recv_sem=self.recv_sem.at[i],
            device_id=peer,
            device_id_type=MESH,
        ).start()
        copy = Sent(self, i, dst)
        self.made.append(copy)
        return copy

    def drain(self):
        for copy in self.made:
            copy.wait_send()


def dot_nn(a, b):
    return jnp.dot(a, b, preferred_element_type=F32)


def dot_nt(a, b):
    return lax.dot_general(a, b, (((1,), (1,)), ((), ())), preferred_element_type=F32)


def dot_tn(a, b):
    return lax.dot_general(a, b, (((0,), (0,)), ((), ())), preferred_element_type=F32)


GROUP = [(dx, dz, dc) for dx in range(NX) for dz in range(2) for dc in range(2)]
A = (0, 64)
B = (64, 128)
A0, A1, B0, B1 = (0, 32), (32, 64), (64, 96), (96, 128)


def gather_rows(sends, place, own, buf):
    arrived = {}

    def push(dx, dz, dc, rows, ddx=0, ddz=0, ddc=0):
        lo, hi = rows
        here = own if (dx, dz, dc) == (0, 0, 0) else buf.at[slot_of(dx, dz, dc)]
        there = ((dx - ddx) % NX, (dz - ddz) % 2, (dc - ddc) % 2)
        arrived[there + (rows,)] = sends.start(
            here.at[pl.ds(lo, hi - lo)],
            lambda: buf.at[slot_of(*there), pl.ds(lo, hi - lo)],
            place.group(ddx, ddz, ddc),
        )

    def take(dx, dz, rows):
        arrived[(dx % NX, dz % 2, 0, rows)].wait_recv()
        push(dx % NX, dz % 2, 0, rows, ddc=1)

    yield
    push(0, 0, 0, B, ddz=1)
    push(0, 0, 0, A, ddx=1)
    push(0, 0, 0, A, ddx=-1)
    push(0, 0, 0, B, ddx=1)
    push(0, 0, 0, B, ddx=-1)
    push(0, 0, 0, A, ddz=1)
    push(0, 0, 0, (0, 128), ddc=1)
    yield
    take(0, 1, B)
    push(0, 1, 0, B, ddx=1)
    push(0, 1, 0, B, ddx=-1)
    yield
    take(1, 0, A)
    push(1, 0, 0, A0, ddx=-1)
    push(1, 0, 0, A, ddz=1)
    take(-1, 0, A)
    push(3, 0, 0, A1, ddx=1)
    push(3, 0, 0, A, ddz=1)
    yield
    take(1, 0, B)
    push(1, 0, 0, B0, ddx=-1)
    take(-1, 0, B)
    push(3, 0, 0, B1, ddx=1)
    take(0, 1, A)
    yield
    take(1, 1, B)
    push(1, 1, 0, B0, ddx=-1)
    take(-1, 1, B)
    push(3, 1, 0, B1, ddx=1)
    take(2, 0, A0)
    push(2, 0, 0, A0, ddz=1)
    take(2, 0, A1)
    push(2, 0, 0, A1, ddz=1)
    yield
    take(1, 1, A)
    take(3, 1, A)
    take(2, 0, B0)
    take(2, 0, B1)
    take(2, 1, B0)
    take(2, 1, B1)
    take(2, 1, A0)
    take(2, 1, A1)
    yield
    near = ((0, 0), (0, 1), (1, 0), (3, 0))
    for first in (True, False):
        for key in list(arrived):
            if key[2] == 1 and (key[0:2] in near) == first:
                arrived[key].wait_recv()
        yield


def forward_kernel(
    tok, cot, meta, wg_hbm, wu_hbm, wd_hbm,
    routed_o, dy_o, pre_o, hidden_o, totals_o, gates_o, pick,
    tok_all, cot_all, meta_all, wg, wu, wd, routed, y_rows, dy, pre, hidden, hidden_t, gate_col, land_s,
    send_sem, recv_sem, copy_sem,
):
    place = Place()
    enter([place.group(*r) for r in GROUP[1:]])
    copies = []

    def local(src, dst):
        copy = pltpu.make_async_copy(src, dst, copy_sem.at[len(copies)])
        copy.start()
        copies.append(copy)
        return copy

    tok_sends = Sends(send_sem.at[pl.ds(0, 48)], recv_sem.at[pl.ds(0, 48)], place)
    cot_sends = Sends(send_sem.at[pl.ds(48, 48)], recv_sem.at[pl.ds(48, 48)], place)
    sends = Sends(send_sem.at[pl.ds(96, 32)], recv_sem.at[pl.ds(96, 32)], place)
    metas = []
    for r in GROUP[1:]:
        to = slot_of(-r[0], r[1], r[2])
        metas.append(sends.start(meta, lambda to=to: meta_all.at[to], place.group(*r)))
    first = gather_rows(tok_sends, place, tok, tok_all)
    second = gather_rows(cot_sends, place, cot, cot_all)
    next(first)
    next(second)
    next(first)
    own = [local(tok, tok_all.at[0]), local(cot, cot_all.at[0]), local(meta, meta_all.at[0])]
    weights = [local(wg_hbm, wg), local(wu_hbm, wu), local(wd_hbm, wd)]
    next(first)
    for copy in metas:
        copy.wait_recv()
    for copy in own:
        copy.wait()
    slot = (lax.broadcasted_iota(jnp.int32, (64, 128), 0) + place.e * 64).astype(F32)

    @pl.loop(0, 16)
    def _(j):
        total = jnp.zeros((64, 128), F32)
        gate = jnp.zeros((64, 128), F32)
        for k in range(6):
            hit = slot == jnp.broadcast_to(meta_all[j, k : k + 1], (64, 128))
            total = total + jnp.where(hit, 1.0, 0.0)
            row = jnp.broadcast_to(meta_all[j, 8 + k : 9 + k], (64, 128))
            gate = gate + jnp.where(hit, row, 0.0)
        pick[j] = total.astype(BF16)
        gate_col[j] = jnp.broadcast_to(jnp.sum(gate, axis=1, keepdims=True), (64, 128))

    next(first)
    next(first)
    next(first)
    next(second)
    for _ in first:
        pass
    next(second)

    def rows32(j):
        return pl.ds(pl.multiple_of(j * 32, 32), 32)

    @pl.loop(0, 16)
    def _(j):
        got = jnp.dot(pick[j], tok_all[j], preferred_element_type=F32).astype(BF16)
        routed[0, rows32(j)] = got[0:32]
        routed[1, rows32(j)] = got[32:64]

    routed_out = local(routed, routed_o)
    next(second)
    for copy in weights:
        copy.wait()

    def up(e):
        pre[e, 0] = dot_nt(routed[e], wg[e])
        pre[e, 1] = dot_nt(routed[e], wu[e])

        @pl.loop(0, 16)
        def _(i):
            at = rows32(i)
            gate = pre[e, 0, at]
            hidden[e, at] = (gate * jax.nn.sigmoid(gate) * pre[e, 1, at]).astype(BF16)

        local(pre.at[e], pre_o.at[e])

    def down(e):
        hidden_t[e] = hidden[e].T
        local(hidden_t.at[e], hidden_o.at[e])
        for n in range(2):
            at = pl.ds(n * 1024, 1024)
            y_rows[e, :, at] = jnp.dot(
                hidden[e], wd[e, :, at], preferred_element_type=F32
            ).astype(BF16)

    def both(ref, j):
        return jnp.concatenate([ref[0, rows32(j)], ref[1, rows32(j)]], axis=0)

    def gated(j):
        scaled = (both(y_rows, j).astype(F32) * gate_col[j, :, 0:1]).astype(BF16)
        return dot_tn(pick[j], scaled)

    def pick_cot(j):
        got = jnp.dot(pick[j], cot_all[j], preferred_element_type=F32)
        by_slot = jnp.sum(got * both(y_rows, j).astype(F32), axis=1, keepdims=True)
        scaled = (got * gate_col[j, :, 0:1]).astype(BF16)
        dy[0, rows32(j)] = scaled[0:32]
        dy[1, rows32(j)] = scaled[32:64]
        by_slot = jnp.broadcast_to(by_slot, (64, 128))
        parts = []
        for k in range(6):
            hit = slot == jnp.broadcast_to(meta_all[j, k : k + 1], (64, 128))
            parts.append(jnp.sum(jnp.where(hit, by_slot, 0.0), axis=0, keepdims=True))
        parts.append(jnp.zeros((2, 128), F32))
        gates_o[j] = jnp.concatenate(parts, axis=0)

    up(0)
    next(second)
    up(1)
    next(second)
    down(0)
    down(1)
    tok_sends.drain()

    @pl.loop(0, 8)
    def _(i):
        tok_all[i * 2 + 1] = gated(i * 2 + 1).astype(BF16)

    shares = [
        sends.start(tok_all.at[i * 2 + 1], lambda i=i: land_s.at[i], place.group(0, 0, 1))
        for i in range(8)
    ]
    next(second)
    next(second)

    @pl.loop(0, 8)
    def _(i):
        pick_cot(i + 6 * (i // 6))

    for copy in shares:
        copy.wait_recv()

    @pl.loop(0, 8)
    def _(i):
        tok_all[i * 2] = (gated(i * 2) + land_s[i].astype(F32)).astype(BF16)

    for i in range(8):
        local(tok_all.at[i * 2], totals_o.at[i])
    for _ in second:
        pass

    @pl.loop(0, 8)
    def _(i):
        pick_cot(6 + i + 2 * (i // 6))

    local(dy, dy_o)
    for copy in copies[6:]:
        copy.wait()
    cot_sends.drain()
    sends.drain()


def forward(tok, cot, meta, w_gate, w_up, w_down):
    d = tok.shape[1]
    hbm = pl.BlockSpec(memory_space=pl.ANY)
    vmem = pl.BlockSpec(memory_space=pltpu.VMEM)
    return pl.pallas_call(
        forward_kernel,
        out_shape=(
            jax.ShapeDtypeStruct((2, 512, d), BF16),
            jax.ShapeDtypeStruct((2, 512, d), BF16),
            jax.ShapeDtypeStruct((2, 2, 512, H_ROWS), F32),
            jax.ShapeDtypeStruct((2, H_ROWS, 512), BF16),
            jax.ShapeDtypeStruct((8, 128, d), BF16),
            jax.ShapeDtypeStruct((16, 8, 128), F32),
            jax.ShapeDtypeStruct((16, 64, 128), BF16),
        ),
        in_specs=[hbm] * 6,
        out_specs=(hbm, hbm, hbm, hbm, hbm, vmem, vmem),
        scratch_shapes=[
            pltpu.VMEM((16, 128, d), BF16),
            pltpu.VMEM((16, 128, d), BF16),
            pltpu.VMEM((16,) + meta.shape, F32),
            pltpu.VMEM(w_gate.shape, BF16),
            pltpu.VMEM(w_up.shape, BF16),
            pltpu.VMEM(w_down.shape, BF16),
            pltpu.VMEM((2, 512, d), BF16),
            pltpu.VMEM((2, 512, d), BF16),
            pltpu.VMEM((2, 512, d), BF16),
            pltpu.VMEM((2, 2, 512, H_ROWS), F32),
            pltpu.VMEM((2, 512, H_ROWS), BF16),
            pltpu.VMEM((2, H_ROWS, 512), BF16),
            pltpu.VMEM((16, 64, 128), F32),
            pltpu.VMEM((8, 128, d), BF16),
            pltpu.SemaphoreType.DMA((128,)),
            pltpu.SemaphoreType.DMA((128,)),
            pltpu.SemaphoreType.DMA((32,)),
        ],
        compiler_params=pltpu.CompilerParams(
            collective_id=0, has_side_effects=True, vmem_limit_bytes=63 * 2**20
        ),
    )(tok, cot, meta, w_gate, w_up, w_down)


def add_into(dst, terms, chunk):
    rows = dst.shape[0]

    @pl.loop(0, rows // chunk)
    def _(i):
        at = pl.ds(pl.multiple_of(i * chunk, chunk), chunk)
        total = terms[0][at].astype(F32)
        for term in terms[1:]:
            total = total + term[at].astype(F32)
        dst[at] = total.astype(dst.dtype)


class Tree:
    def __init__(self, sends, peer, part, land, out, chunk):
        self.sends, self.peer, self.part = sends, peer, part
        self.land, self.out, self.chunk = land, out, chunk

    def open(self):
        s, p, peer = self.sends, self.part, self.peer
        self.far = [
            s.start(p(2, 0), lambda: self.land(0, 0), peer(-1)),
            s.start(p(2, 1), lambda: self.land(0, 1), peer(1)),
        ]
        self.near = [
            s.start(p(1, 0), lambda: self.land(1, 0), peer(1)),
            s.start(p(-1, 1), lambda: self.land(1, 1), peer(-1)),
        ]

    def relay(self):
        self.via = []
        for h, d in ((0, -1), (1, 1)):
            self.far[h].wait_recv()
            add_into(self.out(h), [self.part(d, h), self.land(0, h)], self.chunk)
            self.via.append(self.sends.start(self.out(h), lambda h=h: self.land(2, h), self.peer(d)))

    def close(self, h):
        self.near[h].wait_recv()
        self.via[h].wait_recv()
        return [self.part(0, h), self.land(1, h), self.land(2, h)]


Y_FIRST = ((2, 0), (0, 0), (0, 1), (1, 1))
Z_FIRST = ((2, 1), (1, 0))


def backward_kernel(
    routed_hbm, dy_hbm, pre_hbm, hidden_hbm, wg_hbm, wu_hbm, wd_hbm, t_first, gates_in, pick,
    out_first, out_second, gates_out, grads_out, p_hbm, o_own, land_s,
    land_y, land_z, land_d, land_dz, land_xb, land_zb, gates_land, early_x, early_y,
    send_sem, recv_sem, load_sem,
):
    place = Place()
    loads = []

    def load(src, dst):
        copy = pltpu.make_async_copy(src, dst, load_sem.at[len(loads)])
        copy.start()
        loads.append(copy)
        return copy

    rows_out = (out_first, out_second)
    sends = Sends(send_sem, recv_sem, place)

    def yy(d):
        return lax.rem(place.y + (d % NY), NY) if d % NY else place.y

    def p_slice(m, e, d, z):
        at = pl.multiple_of((yy(d) * 2 + z) * W_COLS, W_COLS)
        return p_hbm.at[m, e, :, pl.ds(at, W_COLS)]

    trees = {}
    down_z = {}

    def open_partial(m, e):
        if (m, e) in Y_FIRST:
            i = Y_FIRST.index((m, e))
            tree = Tree(
                sends, place.col,
                lambda d, h: p_slice(m, e, d, h),
                lambda k, h: land_y.at[i, k, h],
                None, 64,
            )
            tree.open()
            trees[i] = tree
        else:
            i = Z_FIRST.index((m, e))
            for d in (2, 1, 3, 0):
                down_z[i, d] = sends.start(
                    p_slice(m, e, d, 1 - place.zh), lambda d=d: land_dz.at[i, d], place.col(0, 1)
                )

    shares = {}
    row_state = {}

    def first_phase(
        routed, dy, pre, hidden_t, wg, wu, wd, dhd, dg, du, dg_t, du_t, stage, o_stage
    ):
        ld = [
            load(hidden_hbm, hidden_t), load(dy_hbm, dy), load(wd_hbm.at[0], wd),
            load(pre_hbm.at[0], pre), load(routed_hbm, routed),
            load(wg_hbm.at[0], wg), load(wu_hbm.at[0], wu),
        ]
        peers = [place.group(*r) for r in GROUP[1:]]
        enter(peers + [place.col(1), place.col(-1), place.col(0, 1)])
        for dz in (1, 0):
            tree = Tree(
                sends, place.group,
                lambda d, h, dz=dz: t_first.at[(d % NX) * 2 + dz, pl.ds(64 * h, 64)],
                lambda k, h, dz=dz: land_xb.at[0, dz, k, h],
                None, 32,
            )
            tree.open()
            row_state.setdefault(0, []).append(tree)
        x_loads = [
            load(t_first.at[6 + dz, pl.ds(0, 64)], early_x.at[dz, 0]) for dz in range(2)
        ] + [
            load(t_first.at[2 + dz, pl.ds(64, 64)], early_x.at[dz, 1]) for dz in range(2)
        ]

        def early_rows():
            for copy in x_loads:
                copy.wait()
            for tree, dz in zip(row_state[0], (1, 0)):
                tree.part = lambda d, h, dz=dz: early_x.at[dz, h]
                tree.out = lambda h, dz=dz: early_x.at[dz, h]
                tree.relay()

        def early_partial():
            y_loads = [
                load(p_slice(*Y_FIRST[0], -1, 0), early_y.at[0]),
                load(p_slice(*Y_FIRST[0], 1, 1), early_y.at[1]),
            ]
            for copy in y_loads:
                copy.wait()
            trees[0].part = lambda d, h: early_y.at[h]
            trees[0].out = lambda h: early_y.at[h]
            trees[0].relay()

        gate_sends = []
        for r in GROUP[1:]:
            to = slot_of(-r[0], r[1], r[2])
            gate_sends.append(
                sends.start(
                    gates_in.at[slot_of(*r)], lambda to=to: gates_land.at[to], place.group(*r)
                )
            )
        pending = []

        def flush():
            for copies, m, e in pending:
                for copy in copies:
                    copy.wait()
                open_partial(m, e)
            pending.clear()

        def partial(m, e, left, right):
            copies = []
            before = list(pending)
            for n in range(2):
                for entry in before:
                    entry[0][n].wait()

                @pl.loop(0, 2)
                def _(k):
                    at = pl.ds(pl.multiple_of(k * 512, 512), 512)
                    src = pl.ds(pl.multiple_of(n * 1024 + k * 512, 512), 512)
                    stage[n, :, at] = dot_nn(left[...], right[:, src]).astype(BF16)

                copies.append(
                    load(stage.at[n], p_hbm.at[m, e, :, pl.ds(n * 1024, 1024)])
                )
            for entry in before:
                open_partial(entry[1], entry[2])
                pending.remove(entry)
            pending.append((copies, m, e))

        ld[0].wait()
        ld[1].wait()
        partial(2, 0, hidden_t.at[0], dy.at[0])
        partial(2, 1, hidden_t.at[1], dy.at[1])
        for e in range(2):
            if e == 0:
                ld[2].wait()
                ld[3].wait()
                ld[4].wait()
                ld[5].wait()
                ld[6].wait()
            else:
                next_wd.wait()
                next_pre.wait()
            dhd[...] = dot_nt(dy[e], wd[...])
            if e == 0:
                next_wd = load(wd_hbm.at[1], wd)

            @pl.loop(0, 16)
            def _(i):
                at = pl.ds(pl.multiple_of(i * 32, 32), 32)
                gate = pre[0, at]
                s = jax.nn.sigmoid(gate)
                back = dhd[at]
                dg[at] = (back * pre[1, at] * s * (1.0 + gate * (1.0 - s))).astype(BF16)
                du[at] = (back * gate * s).astype(BF16)

            if e == 0:
                next_pre = load(pre_hbm.at[1], pre)
            dg_t[...] = dg[...].T
            du_t[...] = du[...].T
            partial(0, e, dg_t, routed.at[e])
            partial(1, e, du_t, routed.at[e])
            if e == 1:
                for copy in next_w:
                    copy.wait()

            @pl.loop(0, 4)
            def _(n):
                at = pl.ds(pl.multiple_of(n * 512, 512), 512)
                total = dot_nn(dg[...], wg[:, at]) + dot_nn(du[...], wu[:, at])
                routed[e, :, at] = total.astype(BF16)

            if e == 0:
                early_rows()
                next_w = [load(wg_hbm.at[1], wg), load(wu_hbm.at[1], wu)]
        for entry in pending:
            for copy in entry[0]:
                copy.wait()
            open_partial(entry[1], entry[2])
        early_partial()

        def back_rows(j):
            at = pl.ds(pl.multiple_of(j * 32, 32), 32)
            rows = jnp.concatenate([routed[0, at], routed[1, at]], axis=0)
            return dot_tn(pick[j], rows).astype(BF16)

        @pl.loop(0, 8)
        def _(i):
            at = pl.ds(pl.multiple_of(lax.rem(i, 4) * 128, 128), 128)
            dy[i // 4, at] = back_rows(i * 2 + 1)

        for i in range(8):
            shares[i] = sends.start(
                dy.at[i // 4, pl.ds((i % 4) * 128, 128)], lambda i=i: land_s.at[i],
                place.group(0, 0, 1),
            )
        outs = []
        for i in range(8):
            if i >= 2:
                outs[i - 2].wait()
            o_stage[i % 2] = back_rows(i * 2)
            outs.append(load(o_stage.at[i % 2], o_own.at[i]))
        for copy in outs[6:]:
            copy.wait()
        for i in range(8):
            shares[i].wait_send()
        for copy in gate_sends:
            copy.wait_recv()
        total = gates_in[0]
        for i in range(1, 16):
            total = total + gates_land[i]
        gates_out[...] = total

    def second_phase(own_p, out_z, t_down, out_d, t_rows, own_x, s_stage, out_xb, v_rows):
        own_rows = [load(o_own.at[i], t_rows.at[i]) for i in range(8)]
        x_own = [load(t_first.at[dz], own_x.at[dz]) for dz in range(2)]
        own_loads = {}
        for i, (m, e) in enumerate(Y_FIRST):
            own_loads[i] = [
                load(p_slice(m, e, -1, 0), own_p.at[i, 0]),
                load(p_slice(m, e, 1, 1), own_p.at[i, 1]),
                load(p_slice(m, e, 0, 0), own_p.at[i, 2]),
                load(p_slice(m, e, 0, 1), own_p.at[i, 3]),
            ]
        down_loads = {}
        for i, (m, e) in enumerate(Z_FIRST):
            down_loads[i] = [load(p_slice(m, e, d, place.zh), t_down.at[i, d]) for d in range(NY)]

        def rows_start():
            gets = []
            for i in range(8):
                shares[i].wait_recv()
            for i in range(9):
                if i < 8:
                    gets.append(load(land_s.at[i], s_stage.at[i % 2]))
                if i > 0:
                    gets[i - 1].wait()
                    own_rows[i - 1].wait()
                    dst = t_rows.at[i - 1]
                    add_into(dst, [dst, s_stage.at[(i - 1) % 2]], 32)
            made = []
            for dz in (1, 0):
                tree = Tree(
                    sends, place.group,
                    lambda d, h, dz=dz: t_rows.at[(d % NX) * 2 + dz, pl.ds(64 * h, 64)],
                    lambda k, h, dz=dz: land_xb.at[1, dz, k, h],
                    lambda h, dz=dz: out_xb.at[dz, h],
                    32,
                )
                tree.open()
                made.append(tree)
            row_state[1] = made

        def rows_mid():
            for tree in row_state[1]:
                tree.relay()

        def rows_end(r):
            if r == 0:
                for copy in x_own:
                    copy.wait()
                for tree, dz in zip(row_state[0], (1, 0)):
                    tree.part = lambda d, h, dz=dz: own_x.at[dz, pl.ds(64 * h, 64)]
            for h in range(2):
                add_into(v_rows.at[r, 1, pl.ds(64 * h, 64)], row_state[r][0].close(h), 32)
            copy = sends.start(v_rows.at[r, 1], lambda: land_zb.at[r], place.group(0, 1, 0))
            for h in range(2):
                add_into(v_rows.at[r, 0, pl.ds(64 * h, 64)], row_state[r][1].close(h), 32)
            return copy

        def rows_last(r, copy):
            copy.wait_recv()
            add_into(rows_out[r], [v_rows.at[r, 0], land_zb.at[r]], 32)

        def down_mid(i):
            for copy in down_loads[i]:
                copy.wait()
            for d in (2, 1, 3, 0):
                down_z[i, d].wait_recv()
                add_into(t_down.at[i, d], [t_down.at[i, d], land_dz.at[i, d]], 64)
            half = H_ROWS // 2
            tree = Tree(
                sends, place.col,
                lambda d, h: t_down.at[i, d % NY, pl.ds(half * h, half)],
                lambda k, h: land_d.at[i, k, pl.ds(half * h, half)],
                lambda h: out_d.at[i, pl.ds(half * h, half)],
                32,
            )
            tree.open()
            return tree

        def down_end(i, tree):
            m, e = Z_FIRST[i]
            half = H_ROWS // 2
            for h in range(2):
                add_into(grads_out.at[m, e, pl.ds(half * h, half)], tree.close(h), 32)

        def y_relay(i):
            for copy in own_loads[i]:
                copy.wait()
            trees[i].part = lambda d, h: own_p.at[i, {-1: 0, 1: 1, 0: 2 + h}[d]]
            trees[i].out = lambda h: own_p.at[i, h]
            if i > 0:
                trees[i].relay()

        def y_end(i):
            m, e = Y_FIRST[i]
            for h in range(2):
                terms = trees[i].close(h)

                @pl.when(place.zh != h)
                def _():
                    add_into(out_z.at[i], terms, 64)

                @pl.when(place.zh == h)
                def _():
                    add_into(grads_out.at[m, e], terms, 64)

            return sends.start(out_z.at[i], lambda: land_z.at[i], place.col(0, 1))

        def z_end(i, copy):
            m, e = Y_FIRST[i]
            copy.wait_recv()
            dst = grads_out.at[m, e]
            add_into(dst, [dst, land_z.at[i]], 64)

        rows_start()
        y_relay(0)
        y_relay(1)
        r0 = rows_end(0)
        d0 = down_mid(0)
        y_relay(2)
        rows_mid()
        z0 = y_end(0)
        y_relay(3)
        d1 = down_mid(1)
        rows_last(0, r0)
        r1 = rows_end(1)
        d0.relay()
        z1 = y_end(1)
        d1.relay()
        z2 = y_end(2)
        rows_last(1, r1)
        z_end(0, z0)
        down_end(0, d0)
        z3 = y_end(3)
        z_end(1, z1)
        down_end(1, d1)
        z_end(2, z2)
        z_end(3, z3)
        for copy in sends.made:
            if all(copy is not c for c in shares.values()):
                copy.wait_send()

    def buf(*shape):
        return pltpu.VMEM(shape, BF16)

    d = t_first.shape[-1]
    slab = (H_ROWS, W_COLS)
    pl.run_scoped(
        first_phase,
        buf(2, 512, d), buf(2, 512, d), pltpu.VMEM((2, 512, H_ROWS), F32), buf(2, H_ROWS, 512),
        buf(H_ROWS, d), buf(H_ROWS, d), buf(H_ROWS, d), pltpu.VMEM((512, H_ROWS), F32),
        buf(512, H_ROWS), buf(512, H_ROWS), buf(H_ROWS, 512), buf(H_ROWS, 512),
        buf(2, H_ROWS, 1024), buf(2, 128, d),
    )
    pl.run_scoped(
        second_phase,
        buf(4, 4, *slab), buf(4, *slab), buf(2, 4, *slab), buf(2, *slab),
        buf(8, 128, d), buf(2, 128, d), buf(2, 128, d), buf(2, 2, 64, d), buf(2, 2, 128, d),
    )


def backward(*operands):
    d = operands[0].shape[-1]
    n = 192
    hbm = pl.BlockSpec(memory_space=pl.ANY)
    vmem = pl.BlockSpec(memory_space=pltpu.VMEM)
    slab = (H_ROWS, W_COLS)

    def buf(*shape):
        return pltpu.VMEM(shape, BF16)

    return pl.pallas_call(
        backward_kernel,
        out_shape=(
            jax.ShapeDtypeStruct((128, d), BF16),
            jax.ShapeDtypeStruct((128, d), BF16),
            jax.ShapeDtypeStruct((8, 128), F32),
            jax.ShapeDtypeStruct((3, 2) + slab, F32),
            jax.ShapeDtypeStruct((3, 2, H_ROWS, d), BF16),
            jax.ShapeDtypeStruct((8, 128, d), BF16),
            jax.ShapeDtypeStruct((8, 128, d), BF16),
        ),
        in_specs=[hbm] * 8 + [vmem] * 2,
        out_specs=(vmem,) * 4 + (hbm,) * 3,
        scratch_shapes=[
            buf(4, 3, 2, *slab), buf(4, *slab), buf(2, 3, *slab), buf(2, 4, *slab),
            buf(2, 2, 3, 2, 64, d), buf(2, 128, d),
            pltpu.VMEM((16, 8, 128), F32),
            buf(2, 2, 64, d), buf(2, *slab),
            pltpu.SemaphoreType.DMA((n,)),
            pltpu.SemaphoreType.DMA((n,)),
            pltpu.SemaphoreType.DMA((112,)),
        ],
        compiler_params=pltpu.CompilerParams(
            collective_id=1, has_side_effects=True, vmem_limit_bytes=63 * 2**20
        ),
    )(*operands)[:4]


def shards(tokens, cotangent, route_gates, expert_ids, slot_index, w_gate, w_up, w_down):
    target = (expert_ids * 32 + slot_index).astype(F32).T
    meta = jnp.zeros((16, 128), F32).at[0:6].set(target).at[8:14].set(route_gates.T)
    wg, wu = w_gate.transpose(0, 2, 1), w_up.transpose(0, 2, 1)
    routed, grad_rows, pre, hidden_t, o_out, gates_in, pick = forward(
        tokens, cotangent, meta, wg, wu, w_down
    )
    out, grad, gates, grads = backward(
        routed, grad_rows, pre, hidden_t, wg, wu, w_down, o_out, gates_in, pick
    )
    return (
        out,
        grad,
        gates[0:6].T,
        grads[0].transpose(0, 2, 1),
        grads[1].transpose(0, 2, 1),
        grads[2],
    )


def solution(mesh):
    row = P(("expert", "dp"), None)
    weight = P("expert", None, None)
    return jax.shard_map(
        shards,
        mesh=mesh,
        in_specs=(row, row, row, row, row, weight, weight, weight),
        out_specs=(row, row, row, P("expert", "dp", None), P("expert", "dp", None), P("expert", None, "dp")),
        check_vma=False,
    )
```

```python
import functools

import jax
import jax.numpy as jnp
from jax import lax
from jax.experimental import pallas as pl
from jax.experimental.pallas import tpu as pltpu
from jax.sharding import PartitionSpec as P

MESH = pl.DeviceIdType.MESH
F32 = jnp.float32
BF16 = jnp.bfloat16
NX = 4
NY = 4
H_ROWS = 704
W_COLS = 256


def slot_of(dx, dz, dc):
    return (dx % NX) * 4 + (dz % 2) * 2 + (dc % 2)


class Place:
    def __init__(self):
        e = lax.axis_index("expert")
        q = lax.axis_index("dp")
        self.e, self.q = e, q
        self.x, self.zl, self.c = e // 4, (e // 2) % 2, e % 2
        self.y, self.zh = q // 2, q % 2

    def group(self, dx=0, dz=0, dc=0):
        x = lax.rem(self.x + (dx % NX), NX) if dx % NX else self.x
        z = 1 - self.zl if dz % 2 else self.zl
        c = 1 - self.c if dc % 2 else self.c
        return (x * 4 + z * 2 + c, self.q)

    def col(self, dy=0, dz=0):
        y = lax.rem(self.y + (dy % NY), NY) if dy % NY else self.y
        z = 1 - self.zh if dz % 2 else self.zh
        return (self.e, y * 2 + z)


def enter(peers):
    barrier = pltpu.get_barrier_semaphore()
    for peer in peers:
        pl.semaphore_signal(barrier, inc=1, device_id=peer, device_id_type=MESH)
    pl.semaphore_wait(barrier, len(peers))


class Sent:
    def __init__(self, owner, i, dst):
        self.owner, self.i, self.dst = owner, i, dst

    def again(self):
        dst = self.dst()
        return pltpu.make_async_remote_copy(
            src_ref=dst,
            dst_ref=dst,
            send_sem=self.owner.send_sem.at[self.i],
            recv_sem=self.owner.recv_sem.at[self.i],
            device_id=self.owner.home,
            device_id_type=MESH,
        )

    def wait_recv(self):
        self.again().wait_recv()

    def wait_send(self):
        self.again().wait_send()


class Sends:
    def __init__(self, send_sem, recv_sem, place):
        self.send_sem, self.recv_sem = send_sem, recv_sem
        self.home = (place.e, place.q)
        self.made = []

    def start(self, src, dst, peer):
        i = len(self.made)
        pltpu.make_async_remote_copy(
            src_ref=src,
            dst_ref=dst(),
            send_sem=self.send_sem.at[i],
            recv_sem=self.recv_sem.at[i],
            device_id=peer,
            device_id_type=MESH,
        ).start()
        copy = Sent(self, i, dst)
        self.made.append(copy)
        return copy

    def drain(self):
        for copy in self.made:
            copy.wait_send()


def dot_nn(a, b):
    return jnp.dot(a, b, preferred_element_type=F32)


def dot_nt(a, b):
    return lax.dot_general(a, b, (((1,), (1,)), ((), ())), preferred_element_type=F32)


def dot_tn(a, b):
    return lax.dot_general(a, b, (((0,), (0,)), ((), ())), preferred_element_type=F32)


GROUP = [(dx, dz, dc) for dx in range(NX) for dz in range(2) for dc in range(2)]
A = (0, 64)
B = (64, 128)
A0, A1, B0, B1 = (0, 32), (32, 64), (64, 96), (96, 128)


def gather_rows(sends, place, own, buf):
    arrived = {}

    def push(dx, dz, dc, rows, ddx=0, ddz=0, ddc=0):
        lo, hi = rows
        here = own if (dx, dz, dc) == (0, 0, 0) else buf.at[slot_of(dx, dz, dc)]
        there = ((dx - ddx) % NX, (dz - ddz) % 2, (dc - ddc) % 2)
        arrived[there + (rows,)] = sends.start(
            here.at[pl.ds(lo, hi - lo)],
            lambda: buf.at[slot_of(*there), pl.ds(lo, hi - lo)],
            place.group(ddx, ddz, ddc),
        )

    def take(dx, dz, rows):
        arrived[(dx % NX, dz % 2, 0, rows)].wait_recv()
        push(dx % NX, dz % 2, 0, rows, ddc=1)

    yield
    push(0, 0, 0, B, ddz=1)
    push(0, 0, 0, A, ddx=1)
    push(0, 0, 0, A, ddx=-1)
    push(0, 0, 0, B, ddx=1)
    push(0, 0, 0, B, ddx=-1)
    push(0, 0, 0, A, ddz=1)
    push(0, 0, 0, (0, 128), ddc=1)
    yield
    take(0, 1, B)
    push(0, 1, 0, B, ddx=1)
    push(0, 1, 0, B, ddx=-1)
    yield
    take(1, 0, A)
    push(1, 0, 0, A0, ddx=-1)
    push(1, 0, 0, A, ddz=1)
    take(-1, 0, A)
    push(3, 0, 0, A1, ddx=1)
    push(3, 0, 0, A, ddz=1)
    yield
    take(1, 0, B)
    push(1, 0, 0, B0, ddx=-1)
    take(-1, 0, B)
    push(3, 0, 0, B1, ddx=1)
    take(0, 1, A)
    yield
    take(1, 1, B)
    push(1, 1, 0, B0, ddx=-1)
    take(-1, 1, B)
    push(3, 1, 0, B1, ddx=1)
    take(2, 0, A0)
    push(2, 0, 0, A0, ddz=1)
    take(2, 0, A1)
    push(2, 0, 0, A1, ddz=1)
    yield
    take(1, 1, A)
    take(3, 1, A)
    take(2, 0, B0)
    take(2, 0, B1)
    take(2, 1, B0)
    take(2, 1, B1)
    take(2, 1, A0)
    take(2, 1, A1)
    yield
    near = ((0, 0), (0, 1), (1, 0), (3, 0))
    for first in (True, False):
        for key in list(arrived):
            if key[2] == 1 and (key[0:2] in near) == first:
                arrived[key].wait_recv()
        yield


def forward_kernel(
    tok, cot, meta, wg_hbm, wu_hbm, wd_hbm,
    routed_o, dy_o, pre_o, hidden_o, totals_o, gates_o, pick,
    tok_all, cot_all, meta_all, wg, wu, wd, routed, y_rows, dy, pre, hidden, hidden_t, gate_col, land_s,
    send_sem, recv_sem, copy_sem,
):
    place = Place()
    enter([place.group(*r) for r in GROUP[1:]])
    copies = []

    def local(src, dst):
        copy = pltpu.make_async_copy(src, dst, copy_sem.at[len(copies)])
        copy.start()
        copies.append(copy)
        return copy

    tok_sends = Sends(send_sem.at[pl.ds(0, 48)], recv_sem.at[pl.ds(0, 48)], place)
    cot_sends = Sends(send_sem.at[pl.ds(48, 48)], recv_sem.at[pl.ds(48, 48)], place)
    sends = Sends(send_sem.at[pl.ds(96, 32)], recv_sem.at[pl.ds(96, 32)], place)
    metas = []
    for r in GROUP[1:]:
        to = slot_of(-r[0], r[1], r[2])
        metas.append(sends.start(meta, lambda to=to: meta_all.at[to], place.group(*r)))
    first = gather_rows(tok_sends, place, tok, tok_all)
    second = gather_rows(cot_sends, place, cot, cot_all)
    next(first)
    next(second)
    next(first)
    own = [local(tok, tok_all.at[0]), local(cot, cot_all.at[0]), local(meta, meta_all.at[0])]
    weights = [local(wg_hbm, wg), local(wu_hbm, wu), local(wd_hbm, wd)]
    next(first)
    for copy in metas:
        copy.wait_recv()
    for copy in own:
        copy.wait()
    slot = (lax.broadcasted_iota(jnp.int32, (64, 128), 0) + place.e * 64).astype(F32)

    @pl.loop(0, 16)
    def _(j):
        total = jnp.zeros((64, 128), F32)
        gate = jnp.zeros((64, 128), F32)
        for k in range(6):
            hit = slot == jnp.broadcast_to(meta_all[j, k : k + 1], (64, 128))
            total = total + jnp.where(hit, 1.0, 0.0)
            row = jnp.broadcast_to(meta_all[j, 8 + k : 9 + k], (64, 128))
            gate = gate + jnp.where(hit, row, 0.0)
        pick[j] = total.astype(BF16)
        gate_col[j] = jnp.broadcast_to(jnp.sum(gate, axis=1, keepdims=True), (64, 128))

    next(first)
    next(first)
    next(first)
    next(second)
    for _ in first:
        pass
    next(second)

    def rows32(j):
        return pl.ds(pl.multiple_of(j * 32, 32), 32)

    @pl.loop(0, 16)
    def _(j):
        got = jnp.dot(pick[j], tok_all[j], preferred_element_type=F32).astype(BF16)
        routed[0, rows32(j)] = got[0:32]
        routed[1, rows32(j)] = got[32:64]

    routed_out = local(routed, routed_o)
    next(second)
    for copy in weights:
        copy.wait()

    def up(e):
        pre[e, 0] = dot_nt(routed[e], wg[e])
        pre[e, 1] = dot_nt(routed[e], wu[e])

        @pl.loop(0, 16)
        def _(i):
            at = rows32(i)
            gate = pre[e, 0, at]
            hidden[e, at] = (gate * jax.nn.sigmoid(gate) * pre[e, 1, at]).astype(BF16)

        local(pre.at[e], pre_o.at[e])

    def down(e):
        hidden_t[e] = hidden[e].T
        local(hidden_t.at[e], hidden_o.at[e])
        for n in range(2):
            at = pl.ds(n * 1024, 1024)
            y_rows[e, :, at] = jnp.dot(
                hidden[e], wd[e, :, at], preferred_element_type=F32
            ).astype(BF16)

    def both(ref, j):
        return jnp.concatenate([ref[0, rows32(j)], ref[1, rows32(j)]], axis=0)

    def gated(j):
        scaled = (both(y_rows, j).astype(F32) * gate_col[j, :, 0:1]).astype(BF16)
        return dot_tn(pick[j], scaled)

    def pick_cot(j):
        got = jnp.dot(pick[j], cot_all[j], preferred_element_type=F32)
        by_slot = jnp.sum(got * both(y_rows, j).astype(F32), axis=1, keepdims=True)
        scaled = (got * gate_col[j, :, 0:1]).astype(BF16)
        dy[0, rows32(j)] = scaled[0:32]
        dy[1, rows32(j)] = scaled[32:64]
        by_slot = jnp.broadcast_to(by_slot, (64, 128))
        parts = []
        for k in range(6):
            hit = slot == jnp.broadcast_to(meta_all[j, k : k + 1], (64, 128))
            parts.append(jnp.sum(jnp.where(hit, by_slot, 0.0), axis=0, keepdims=True))
        parts.append(jnp.zeros((2, 128), F32))
        gates_o[j] = jnp.concatenate(parts, axis=0)

    up(0)
    next(second)
    up(1)
    next(second)
    down(0)
    down(1)
    tok_sends.drain()

    @pl.loop(0, 8)
    def _(i):
        tok_all[i * 2 + 1] = gated(i * 2 + 1).astype(BF16)

    shares = [
        sends.start(tok_all.at[i * 2 + 1], lambda i=i: land_s.at[i], place.group(0, 0, 1))
        for i in range(8)
    ]
    next(second)
    next(second)

    @pl.loop(0, 8)
    def _(i):
        pick_cot(i + 6 * (i // 6))

    for copy in shares:
        copy.wait_recv()

    @pl.loop(0, 8)
    def _(i):
        tok_all[i * 2] = (gated(i * 2) + land_s[i].astype(F32)).astype(BF16)

    for i in range(8):
        local(tok_all.at[i * 2], totals_o.at[i])
    for _ in second:
        pass

    @pl.loop(0, 8)
    def _(i):
        pick_cot(6 + i + 2 * (i // 6))

    local(dy, dy_o)
    for copy in copies[6:]:
        copy.wait()
    cot_sends.drain()
    sends.drain()


def forward(tok, cot, meta, w_gate, w_up, w_down):
    d = tok.shape[1]
    hbm = pl.BlockSpec(memory_space=pl.ANY)
    vmem = pl.BlockSpec(memory_space=pltpu.VMEM)
    return pl.pallas_call(
        forward_kernel,
        out_shape=(
            jax.ShapeDtypeStruct((2, 512, d), BF16),
            jax.ShapeDtypeStruct((2, 512, d), BF16),
            jax.ShapeDtypeStruct((2, 2, 512, H_ROWS), F32),
            jax.ShapeDtypeStruct((2, H_ROWS, 512), BF16),
            jax.ShapeDtypeStruct((8, 128, d), BF16),
            jax.ShapeDtypeStruct((16, 8, 128), F32),
            jax.ShapeDtypeStruct((16, 64, 128), BF16),
        ),
        in_specs=[hbm] * 6,
        out_specs=(hbm, hbm, hbm, hbm, hbm, vmem, vmem),
        scratch_shapes=[
            pltpu.VMEM((16, 128, d), BF16),
            pltpu.VMEM((16, 128, d), BF16),
            pltpu.VMEM((16,) + meta.shape, F32),
            pltpu.VMEM(w_gate.shape, BF16),
            pltpu.VMEM(w_up.shape, BF16),
            pltpu.VMEM(w_down.shape, BF16),
            pltpu.VMEM((2, 512, d), BF16),
            pltpu.VMEM((2, 512, d), BF16),
            pltpu.VMEM((2, 512, d), BF16),
            pltpu.VMEM((2, 2, 512, H_ROWS), F32),
            pltpu.VMEM((2, 512, H_ROWS), BF16),
            pltpu.VMEM((2, H_ROWS, 512), BF16),
            pltpu.VMEM((16, 64, 128), F32),
            pltpu.VMEM((8, 128, d), BF16),
            pltpu.SemaphoreType.DMA((128,)),
            pltpu.SemaphoreType.DMA((128,)),
            pltpu.SemaphoreType.DMA((32,)),
        ],
        compiler_params=pltpu.CompilerParams(
            collective_id=0, has_side_effects=True, vmem_limit_bytes=63 * 2**20
        ),
    )(tok, cot, meta, w_gate, w_up, w_down)


def add_into(dst, terms, chunk):
    rows = dst.shape[0]

    @pl.loop(0, rows // chunk)
    def _(i):
        at = pl.ds(pl.multiple_of(i * chunk, chunk), chunk)
        total = terms[0][at].astype(F32)
        for term in terms[1:]:
            total = total + term[at].astype(F32)
        dst[at] = total.astype(dst.dtype)


class Tree:
    def __init__(self, sends, peer, part, land, out, chunk):
        self.sends, self.peer, self.part = sends, peer, part
        self.land, self.out, self.chunk = land, out, chunk

    def open(self):
        s, p, peer = self.sends, self.part, self.peer
        self.far = [
            s.start(p(2, 0), lambda: self.land(0, 0), peer(-1)),
            s.start(p(2, 1), lambda: self.land(0, 1), peer(1)),
        ]
        self.near = [
            s.start(p(1, 0), lambda: self.land(1, 0), peer(1)),
            s.start(p(-1, 1), lambda: self.land(1, 1), peer(-1)),
        ]

    def relay(self):
        self.via = []
        for h, d in ((0, -1), (1, 1)):
            self.far[h].wait_recv()
            add_into(self.out(h), [self.part(d, h), self.land(0, h)], self.chunk)
            self.via.append(self.sends.start(self.out(h), lambda h=h: self.land(2, h), self.peer(d)))

    def close(self, h):
        self.near[h].wait_recv()
        self.via[h].wait_recv()
        return [self.part(0, h), self.land(1, h), self.land(2, h)]


Y_FIRST = ((2, 0), (0, 0), (0, 1), (1, 1))
Z_FIRST = ((2, 1), (1, 0))


def backward_kernel(
    routed_hbm, dy_hbm, pre_hbm, hidden_hbm, wg_hbm, wu_hbm, wd_hbm, t_first, gates_in, pick,
    out_first, out_second, gates_out, grads_gate, grads_up, grads_down, p_hbm,
    land_s, land_y, land_z, land_d, land_dz, land_xb, land_zb, gates_land, early_x, early_y,
    send_sem, recv_sem, load_sem,
):
    place = Place()
    loads = []

    def load(src, dst):
        copy = pltpu.make_async_copy(src, dst, load_sem.at[len(loads)])
        copy.start()
        loads.append(copy)
        return copy

    rows_out = (out_first, out_second)
    grads_out = (grads_gate, grads_up, grads_down)
    sends = Sends(send_sem, recv_sem, place)

    def yy(d):
        return lax.rem(place.y + (d % NY), NY) if d % NY else place.y

    def p_slice(m, e, d, z):
        at = pl.multiple_of((yy(d) * 2 + z) * W_COLS, W_COLS)
        return p_hbm.at[m, e, :, pl.ds(at, W_COLS)]

    trees = {}
    down_z = {}

    def open_partial(m, e):
        if (m, e) in Y_FIRST:
            i = Y_FIRST.index((m, e))
            tree = Tree(
                sends, place.col,
                lambda d, h: p_slice(m, e, d, h),
                lambda k, h: land_y.at[i, k, h],
                None, 64,
            )
            tree.open()
            trees[i] = tree
        else:
            i = Z_FIRST.index((m, e))
            for d in (2, 1, 3, 0):
                down_z[i, d] = sends.start(
                    p_slice(m, e, d, 1 - place.zh), lambda d=d: land_dz.at[i, d], place.col(0, 1)
                )

    shares = {}
    row_state = {}

    def first_phase(
        routed, dy, pre, hidden_t, wg, wu, wd, dhd, dg, du, dg_t, du_t, stage
    ):
        ld = [
            load(hidden_hbm, hidden_t), load(dy_hbm, dy), load(wd_hbm.at[0], wd),
            load(pre_hbm.at[0], pre), load(routed_hbm, routed),
            load(wg_hbm.at[0], wg), load(wu_hbm.at[0], wu),
        ]
        peers = [place.group(*r) for r in GROUP[1:]]
        enter(peers + [place.col(1), place.col(-1), place.col(0, 1)])
        for dz in (1, 0):
            tree = Tree(
                sends, place.group,
                lambda d, h, dz=dz: t_first.at[(d % NX) * 2 + dz, pl.ds(64 * h, 64)],
                lambda k, h, dz=dz: land_xb.at[0, dz, k, h],
                None, 32,
            )
            tree.open()
            row_state.setdefault(0, []).append(tree)
        x_loads = [
            load(t_first.at[6 + dz, pl.ds(0, 64)], early_x.at[dz, 0]) for dz in range(2)
        ] + [
            load(t_first.at[2 + dz, pl.ds(64, 64)], early_x.at[dz, 1]) for dz in range(2)
        ]

        def early_rows():
            for copy in x_loads:
                copy.wait()
            for tree, dz in zip(row_state[0], (1, 0)):
                tree.part = lambda d, h, dz=dz: early_x.at[dz, h]
                tree.out = lambda h, dz=dz: early_x.at[dz, h]
                tree.relay()

        def early_partial():
            y_loads = [
                load(p_slice(*Y_FIRST[0], -1, 0), early_y.at[0]),
                load(p_slice(*Y_FIRST[0], 1, 1), early_y.at[1]),
            ]
            for copy in y_loads:
                copy.wait()
            trees[0].part = lambda d, h: early_y.at[h]
            trees[0].out = lambda h: early_y.at[h]
            trees[0].relay()

        gate_sends = []
        for r in GROUP[1:]:
            to = slot_of(-r[0], r[1], r[2])
            gate_sends.append(
                sends.start(
                    gates_in.at[slot_of(*r)], lambda to=to: gates_land.at[to], place.group(*r)
                )
            )
        pending = []

        def flush():
            for copies, m, e in pending:
                for copy in copies:
                    copy.wait()
                open_partial(m, e)
            pending.clear()

        def partial(m, e, left, right):
            copies = []
            before = list(pending)
            for n in range(2):
                for entry in before:
                    entry[0][n].wait()

                @pl.loop(0, 2)
                def _(k):
                    at = pl.ds(pl.multiple_of(k * 512, 512), 512)
                    src = pl.ds(pl.multiple_of(n * 1024 + k * 512, 512), 512)
                    stage[n, :, at] = dot_nn(left[...], right[:, src]).astype(BF16)

                copies.append(
                    load(stage.at[n], p_hbm.at[m, e, :, pl.ds(n * 1024, 1024)])
                )
            for entry in before:
                open_partial(entry[1], entry[2])
                pending.remove(entry)
            pending.append((copies, m, e))

        ld[0].wait()
        ld[1].wait()
        partial(2, 0, hidden_t.at[0], dy.at[0])
        partial(2, 1, hidden_t.at[1], dy.at[1])
        for e in range(2):
            if e == 0:
                ld[2].wait()
                ld[3].wait()
                ld[4].wait()
                ld[5].wait()
                ld[6].wait()
            else:
                next_wd.wait()
                next_pre.wait()
            dhd[...] = dot_nt(dy[e], wd[...])
            flush()
            if e == 0:
                next_wd = load(wd_hbm.at[1], wd)

            @pl.loop(0, 16)
            def _(i):
                at = pl.ds(pl.multiple_of(i * 32, 32), 32)
                gate = pre[0, at]
                s = jax.nn.sigmoid(gate)
                back = dhd[at]
                dg[at] = (back * pre[1, at] * s * (1.0 + gate * (1.0 - s))).astype(BF16)
                du[at] = (back * gate * s).astype(BF16)

            if e == 0:
                next_pre = load(pre_hbm.at[1], pre)
            dg_t[...] = dg[...].T
            du_t[...] = du[...].T
            if e == 0:
                partial(0, e, dg_t, routed.at[e])
                partial(1, e, du_t, routed.at[e])
            else:
                for copy in next_w:
                    copy.wait()

            def back(n):
                at = pl.ds(pl.multiple_of(n * 512, 512), 512)
                total = dot_nn(dg[...], wg[:, at]) + dot_nn(du[...], wu[:, at])
                dy[e, :, at] = total.astype(BF16)

            pl.loop(0, 1)(back)
            flush()
            pl.loop(1, 4)(back)

            if e == 0:
                next_w = [load(wg_hbm.at[1], wg), load(wu_hbm.at[1], wu)]
                early_rows()

        def back_rows(j):
            at = pl.ds(pl.multiple_of(j * 32, 32), 32)
            rows = jnp.concatenate([dy[0, at], dy[1, at]], axis=0)
            return dot_tn(pick[j], rows)

        @pl.loop(0, 4)
        def _(i):
            at = pl.ds(pl.multiple_of(i * 128, 128), 128)
            wg[at] = back_rows(i * 2 + 1).astype(BF16)
            wu[at] = back_rows(i * 2 + 9).astype(BF16)

        for i in range(8):
            shares[i] = sends.start(
                (wg, wu)[i // 4].at[pl.ds((i % 4) * 128, 128)], lambda i=i: land_s.at[i],
                place.group(0, 0, 1),
            )
        partial(0, 1, dg_t, routed.at[1])
        partial(1, 1, du_t, routed.at[1])
        flush()
        early_partial()
        for i in range(8):
            shares[i].wait_recv()

        @pl.loop(0, 8)
        def _(i):
            land_s[i] = (back_rows(i * 2) + land_s[i].astype(F32)).astype(BF16)

        for dz in (1, 0):

            def part(d, h, dz=dz):
                return land_s.at[(d % NX) * 2 + dz, pl.ds(64 * h, 64)]

            tree = Tree(
                sends, place.group, part,
                lambda k, h, dz=dz: land_xb.at[1, dz, k, h],
                lambda h, part=part: part((-1, 1)[h], h),
                32,
            )
            tree.open()
            row_state.setdefault(1, []).append(tree)
        for i in range(8):
            shares[i].wait_send()
        for copy in gate_sends:
            copy.wait_recv()
        total = gates_in[0]
        for i in range(1, 16):
            total = total + gates_land[i]
        gates_out[...] = total

    def second_phase(own_p, out_z, t_down, out_d, own_x, v_rows):
        x_own = [load(t_first.at[dz], own_x.at[dz]) for dz in range(2)]
        own_loads = {}
        for i, (m, e) in enumerate(Y_FIRST):
            own_loads[i] = [
                load(p_slice(m, e, -1, 0), own_p.at[i, 0]),
                load(p_slice(m, e, 1, 1), own_p.at[i, 1]),
                load(p_slice(m, e, 0, 0), own_p.at[i, 2]),
                load(p_slice(m, e, 0, 1), own_p.at[i, 3]),
            ]
        down_loads = {}
        for i, (m, e) in enumerate(Z_FIRST):
            down_loads[i] = [load(p_slice(m, e, d, place.zh), t_down.at[i, d]) for d in range(NY)]

        def rows_mid():
            for tree in row_state[1]:
                tree.relay()

        def rows_end(r):
            if r == 0:
                for copy in x_own:
                    copy.wait()
                for tree, dz in zip(row_state[0], (1, 0)):
                    tree.part = lambda d, h, dz=dz: own_x.at[dz, pl.ds(64 * h, 64)]
            for h in range(2):
                add_into(v_rows.at[r, 1, pl.ds(64 * h, 64)], row_state[r][0].close(h), 32)
            copy = sends.start(v_rows.at[r, 1], lambda: land_zb.at[r], place.group(0, 1, 0))
            for h in range(2):
                add_into(v_rows.at[r, 0, pl.ds(64 * h, 64)], row_state[r][1].close(h), 32)
            return copy

        def rows_last(r, copy):
            copy.wait_recv()
            add_into(rows_out[r], [v_rows.at[r, 0], land_zb.at[r]], 32)

        def down_mid(i):
            for copy in down_loads[i]:
                copy.wait()
            for d in (2, 1, 3, 0):
                down_z[i, d].wait_recv()
                add_into(t_down.at[i, d], [t_down.at[i, d], land_dz.at[i, d]], 64)
            half = H_ROWS // 2
            tree = Tree(
                sends, place.col,
                lambda d, h: t_down.at[i, d % NY, pl.ds(half * h, half)],
                lambda k, h: land_d.at[i, k, pl.ds(half * h, half)],
                lambda h: out_d.at[i, pl.ds(half * h, half)],
                32,
            )
            tree.open()
            return tree

        def down_end(i, tree):
            m, e = Z_FIRST[i]
            half = H_ROWS // 2
            for h in range(2):
                add_into(grads_out[m].at[e, pl.ds(half * h, half)], tree.close(h), 32)

        def y_relay(i):
            for copy in own_loads[i]:
                copy.wait()
            trees[i].part = lambda d, h: own_p.at[i, {-1: 0, 1: 1, 0: 2 + h}[d]]
            trees[i].out = lambda h: own_p.at[i, h]
            if i > 0:
                trees[i].relay()

        def y_end(i):
            m, e = Y_FIRST[i]
            for h in range(2):
                terms = trees[i].close(h)

                @pl.when(place.zh != h)
                def _():
                    add_into(out_z.at[i], terms, 64)

                @pl.when(place.zh == h)
                def _():
                    add_into(grads_out[m].at[e], terms, 64)

            return sends.start(out_z.at[i], lambda: land_z.at[i], place.col(0, 1))

        def z_end(i, copy):
            m, e = Y_FIRST[i]
            copy.wait_recv()
            dst = grads_out[m].at[e]
            add_into(dst, [dst, land_z.at[i]], 64)

        y_relay(0)
        y_relay(1)
        d0 = down_mid(0)
        r0 = rows_end(0)
        z0 = y_end(0)
        rows_mid()
        z1 = y_end(1)
        y_relay(2)
        y_relay(3)
        d1 = down_mid(1)
        rows_last(0, r0)
        d0.relay()
        z_end(0, z0)
        z2 = y_end(2)
        r1 = rows_end(1)
        d1.relay()
        z_end(1, z1)
        z3 = y_end(3)
        down_end(0, d0)
        rows_last(1, r1)
        down_end(1, d1)
        z_end(2, z2)
        z_end(3, z3)
        for copy in sends.made:
            if all(copy is not c for c in shares.values()):
                copy.wait_send()

    def buf(*shape):
        return pltpu.VMEM(shape, BF16)

    d = t_first.shape[-1]
    slab = (H_ROWS, W_COLS)
    pl.run_scoped(
        first_phase,
        buf(2, 512, d), buf(2, 512, d), pltpu.VMEM((2, 512, H_ROWS), F32), buf(2, H_ROWS, 512),
        buf(H_ROWS, d), buf(H_ROWS, d), buf(H_ROWS, d), pltpu.VMEM((512, H_ROWS), F32),
        buf(512, H_ROWS), buf(512, H_ROWS), buf(H_ROWS, 512), buf(H_ROWS, 512),
        buf(2, H_ROWS, 1024),
    )
    pl.run_scoped(
        second_phase,
        buf(4, 4, *slab), buf(4, *slab), buf(2, 4, *slab), buf(2, *slab),
        buf(2, 128, d), buf(2, 2, 128, d),
    )


def backward(*operands):
    d = operands[0].shape[-1]
    n = 192
    hbm = pl.BlockSpec(memory_space=pl.ANY)
    vmem = pl.BlockSpec(memory_space=pltpu.VMEM)
    slab = (H_ROWS, W_COLS)

    def buf(*shape):
        return pltpu.VMEM(shape, BF16)

    return pl.pallas_call(
        backward_kernel,
        out_shape=(
            jax.ShapeDtypeStruct((128, d), BF16),
            jax.ShapeDtypeStruct((128, d), BF16),
            jax.ShapeDtypeStruct((8, 128), F32),
            jax.ShapeDtypeStruct((2,) + slab, F32),
            jax.ShapeDtypeStruct((2,) + slab, F32),
            jax.ShapeDtypeStruct((2,) + slab, F32),
            jax.ShapeDtypeStruct((3, 2, H_ROWS, d), BF16),
        ),
        in_specs=[hbm] * 8 + [vmem] * 2,
        out_specs=(vmem,) * 6 + (hbm,),
        scratch_shapes=[
            buf(8, 128, d), buf(4, 3, 2, *slab), buf(4, *slab), buf(2, 3, *slab), buf(2, 4, *slab),
            buf(2, 2, 3, 2, 64, d), buf(2, 128, d),
            pltpu.VMEM((16, 8, 128), F32),
            buf(2, 2, 64, d), buf(2, *slab),
            pltpu.SemaphoreType.DMA((n,)),
            pltpu.SemaphoreType.DMA((n,)),
            pltpu.SemaphoreType.DMA((112,)),
        ],
        compiler_params=pltpu.CompilerParams(
            collective_id=1, has_side_effects=True, vmem_limit_bytes=63 * 2**20
        ),
    )(*operands)[:6]


def shards(tokens, cotangent, route_gates, expert_ids, slot_index, w_gate, w_up, w_down):
    target = (expert_ids * 32 + slot_index).astype(F32).T
    meta = jnp.zeros((16, 128), F32).at[0:6].set(target).at[8:14].set(route_gates.T)
    wg, wu = w_gate.transpose(0, 2, 1), w_up.transpose(0, 2, 1)
    routed, grad_rows, pre, hidden_t, o_out, gates_in, pick = forward(
        tokens, cotangent, meta, wg, wu, w_down
    )
    out, grad, gates, grad_gate, grad_up, grad_down = backward(
        routed, grad_rows, pre, hidden_t, wg, wu, w_down, o_out, gates_in, pick
    )
    return (
        out,
        grad,
        gates[0:6].T,
        grad_gate.transpose(0, 2, 1),
        grad_up.transpose(0, 2, 1),
        grad_down,
    )


def solution(mesh):
    row = P(("expert", "dp"), None)
    weight = P("expert", None, None)
    return jax.shard_map(
        shards,
        mesh=mesh,
        in_specs=(row, row, row, row, row, weight, weight, weight),
        out_specs=(row, row, row, P("expert", "dp", None), P("expert", "dp", None), P("expert", None, "dp")),
        check_vma=False,
    )
```

```python
import functools

import jax
import jax.numpy as jnp
from jax import lax
from jax.experimental import pallas as pl
from jax.experimental.pallas import tpu as pltpu
from jax.sharding import PartitionSpec as P

MESH = pl.DeviceIdType.MESH
F32 = jnp.float32
BF16 = jnp.bfloat16
NX = 4
NY = 4
H_ROWS = 704
W_COLS = 256


def slot_of(dx, dz, dc):
    return (dx % NX) * 4 + (dz % 2) * 2 + (dc % 2)


class Place:
    def __init__(self):
        e = lax.axis_index("expert")
        q = lax.axis_index("dp")
        self.e, self.q = e, q
        self.x, self.zl, self.c = e // 4, (e // 2) % 2, e % 2
        self.y, self.zh = q // 2, q % 2

    def group(self, dx=0, dz=0, dc=0):
        x = lax.rem(self.x + (dx % NX), NX) if dx % NX else self.x
        z = 1 - self.zl if dz % 2 else self.zl
        c = 1 - self.c if dc % 2 else self.c
        return (x * 4 + z * 2 + c, self.q)

    def col(self, dy=0, dz=0):
        y = lax.rem(self.y + (dy % NY), NY) if dy % NY else self.y
        z = 1 - self.zh if dz % 2 else self.zh
        return (self.e, y * 2 + z)


def enter(peers):
    barrier = pltpu.get_barrier_semaphore()
    for peer in peers:
        pl.semaphore_signal(barrier, inc=1, device_id=peer, device_id_type=MESH)
    pl.semaphore_wait(barrier, len(peers))


class Sent:
    def __init__(self, owner, i, dst):
        self.owner, self.i, self.dst = owner, i, dst

    def again(self):
        dst = self.dst()
        return pltpu.make_async_remote_copy(
            src_ref=dst,
            dst_ref=dst,
            send_sem=self.owner.send_sem.at[self.i],
            recv_sem=self.owner.recv_sem.at[self.i],
            device_id=self.owner.home,
            device_id_type=MESH,
        )

    def wait_recv(self):
        self.again().wait_recv()

    def wait_send(self):
        self.again().wait_send()


class Sends:
    def __init__(self, send_sem, recv_sem, place):
        self.send_sem, self.recv_sem = send_sem, recv_sem
        self.home = (place.e, place.q)
        self.made = []

    def start(self, src, dst, peer):
        i = len(self.made)
        pltpu.make_async_remote_copy(
            src_ref=src,
            dst_ref=dst(),
            send_sem=self.send_sem.at[i],
            recv_sem=self.recv_sem.at[i],
            device_id=peer,
            device_id_type=MESH,
        ).start()
        copy = Sent(self, i, dst)
        self.made.append(copy)
        return copy

    def drain(self):
        for copy in self.made:
            copy.wait_send()


def dot_nn(a, b):
    return jnp.dot(a, b, preferred_element_type=F32)


def dot_nt(a, b):
    return lax.dot_general(a, b, (((1,), (1,)), ((), ())), preferred_element_type=F32)


def dot_tn(a, b):
    return lax.dot_general(a, b, (((0,), (0,)), ((), ())), preferred_element_type=F32)


GROUP = [(dx, dz, dc) for dx in range(NX) for dz in range(2) for dc in range(2)]
A = (0, 64)
B = (64, 128)
A0, A1, B0, B1 = (0, 32), (32, 64), (64, 96), (96, 128)


def gather_rows(sends, place, own, buf):
    arrived = {}

    def push(dx, dz, dc, rows, ddx=0, ddz=0, ddc=0):
        lo, hi = rows
        here = own if (dx, dz, dc) == (0, 0, 0) else buf.at[slot_of(dx, dz, dc)]
        there = ((dx - ddx) % NX, (dz - ddz) % 2, (dc - ddc) % 2)
        arrived[there + (rows,)] = sends.start(
            here.at[pl.ds(lo, hi - lo)],
            lambda: buf.at[slot_of(*there), pl.ds(lo, hi - lo)],
            place.group(ddx, ddz, ddc),
        )

    def take(dx, dz, rows):
        arrived[(dx % NX, dz % 2, 0, rows)].wait_recv()
        push(dx % NX, dz % 2, 0, rows, ddc=1)

    yield
    push(0, 0, 0, B, ddz=1)
    push(0, 0, 0, A, ddx=1)
    push(0, 0, 0, A, ddx=-1)
    push(0, 0, 0, B, ddx=1)
    push(0, 0, 0, B, ddx=-1)
    push(0, 0, 0, A, ddz=1)
    push(0, 0, 0, (0, 128), ddc=1)
    yield
    take(0, 1, B)
    push(0, 1, 0, B, ddx=1)
    push(0, 1, 0, B, ddx=-1)
    yield
    take(1, 0, A)
    push(1, 0, 0, A0, ddx=-1)
    push(1, 0, 0, A, ddz=1)
    take(-1, 0, A)
    push(3, 0, 0, A1, ddx=1)
    push(3, 0, 0, A, ddz=1)
    yield
    take(1, 0, B)
    push(1, 0, 0, B0, ddx=-1)
    take(-1, 0, B)
    push(3, 0, 0, B1, ddx=1)
    take(0, 1, A)
    yield
    take(1, 1, B)
    push(1, 1, 0, B0, ddx=-1)
    take(-1, 1, B)
    push(3, 1, 0, B1, ddx=1)
    take(2, 0, A0)
    push(2, 0, 0, A0, ddz=1)
    take(2, 0, A1)
    push(2, 0, 0, A1, ddz=1)
    yield
    take(1, 1, A)
    take(3, 1, A)
    take(2, 0, B0)
    take(2, 0, B1)
    take(2, 1, B0)
    take(2, 1, B1)
    take(2, 1, A0)
    take(2, 1, A1)
    yield
    near = ((0, 0), (0, 1), (1, 0), (3, 0))
    for first in (True, False):
        for key in list(arrived):
            if key[2] == 1 and (key[0:2] in near) == first:
                arrived[key].wait_recv()
        yield


def forward_kernel(
    tok, cot, meta, wg_hbm, wu_hbm, wd_hbm,
    routed_o, dy_o, pre_o, hidden_o, totals_o, gates_o, pick,
    tok_all, cot_all, meta_all, wg, wu, wd, routed, y_rows, dy, pre, hidden, hidden_t, gate_col, land_s,
    send_sem, recv_sem, copy_sem,
):
    place = Place()
    enter([place.group(*r) for r in GROUP[1:]])
    copies = []

    def local(src, dst):
        copy = pltpu.make_async_copy(src, dst, copy_sem.at[len(copies)])
        copy.start()
        copies.append(copy)
        return copy

    tok_sends = Sends(send_sem.at[pl.ds(0, 48)], recv_sem.at[pl.ds(0, 48)], place)
    cot_sends = Sends(send_sem.at[pl.ds(48, 48)], recv_sem.at[pl.ds(48, 48)], place)
    sends = Sends(send_sem.at[pl.ds(96, 32)], recv_sem.at[pl.ds(96, 32)], place)
    metas = []
    for r in GROUP[1:]:
        to = slot_of(-r[0], r[1], r[2])
        metas.append(sends.start(meta, lambda to=to: meta_all.at[to], place.group(*r)))
    first = gather_rows(tok_sends, place, tok, tok_all)
    second = gather_rows(cot_sends, place, cot, cot_all)
    next(first)
    next(second)
    next(first)
    own = [local(tok, tok_all.at[0]), local(cot, cot_all.at[0]), local(meta, meta_all.at[0])]
    weights = [local(wg_hbm, wg), local(wu_hbm, wu), local(wd_hbm, wd)]
    next(first)
    for copy in metas:
        copy.wait_recv()
    for copy in own:
        copy.wait()
    slot = (lax.broadcasted_iota(jnp.int32, (64, 128), 0) + place.e * 64).astype(F32)

    @pl.loop(0, 16)
    def _(j):
        total = jnp.zeros((64, 128), F32)
        gate = jnp.zeros((64, 128), F32)
        for k in range(6):
            hit = slot == jnp.broadcast_to(meta_all[j, k : k + 1], (64, 128))
            total = total + jnp.where(hit, 1.0, 0.0)
            row = jnp.broadcast_to(meta_all[j, 8 + k : 9 + k], (64, 128))
            gate = gate + jnp.where(hit, row, 0.0)
        pick[j] = total.astype(BF16)
        gate_col[j] = jnp.broadcast_to(jnp.sum(gate, axis=1, keepdims=True), (64, 128))

    next(first)
    next(first)
    next(first)
    next(second)
    for _ in first:
        pass
    next(second)

    def rows32(j):
        return pl.ds(pl.multiple_of(j * 32, 32), 32)

    @pl.loop(0, 16)
    def _(j):
        got = jnp.dot(pick[j], tok_all[j], preferred_element_type=F32).astype(BF16)
        routed[0, rows32(j)] = got[0:32]
        routed[1, rows32(j)] = got[32:64]

    routed_out = local(routed, routed_o)
    next(second)
    for copy in weights:
        copy.wait()

    def up(e):
        pre[e, 0] = dot_nt(routed[e], wg[e])
        pre[e, 1] = dot_nt(routed[e], wu[e])

        @pl.loop(0, 16)
        def _(i):
            at = rows32(i)
            gate = pre[e, 0, at]
            hidden[e, at] = (gate * jax.nn.sigmoid(gate) * pre[e, 1, at]).astype(BF16)

        local(pre.at[e], pre_o.at[e])

    def down(e):
        hidden_t[e] = hidden[e].T
        local(hidden_t.at[e], hidden_o.at[e])
        for n in range(2):
            at = pl.ds(n * 1024, 1024)
            y_rows[e, :, at] = jnp.dot(
                hidden[e], wd[e, :, at], preferred_element_type=F32
            ).astype(BF16)

    def both(ref, j):
        return jnp.concatenate([ref[0, rows32(j)], ref[1, rows32(j)]], axis=0)

    def gated(j):
        scaled = (both(y_rows, j).astype(F32) * gate_col[j, :, 0:1]).astype(BF16)
        return dot_tn(pick[j], scaled)

    def pick_cot(j):
        got = jnp.dot(pick[j], cot_all[j], preferred_element_type=F32)
        by_slot = jnp.sum(got * both(y_rows, j).astype(F32), axis=1, keepdims=True)
        scaled = (got * gate_col[j, :, 0:1]).astype(BF16)
        dy[0, rows32(j)] = scaled[0:32]
        dy[1, rows32(j)] = scaled[32:64]
        by_slot = jnp.broadcast_to(by_slot, (64, 128))
        parts = []
        for k in range(6):
            hit = slot == jnp.broadcast_to(meta_all[j, k : k + 1], (64, 128))
            parts.append(jnp.sum(jnp.where(hit, by_slot, 0.0), axis=0, keepdims=True))
        parts.append(jnp.zeros((2, 128), F32))
        gates_o[j] = jnp.concatenate(parts, axis=0)

    up(0)
    next(second)
    up(1)
    next(second)
    down(0)
    down(1)
    tok_sends.drain()

    @pl.loop(0, 8)
    def _(i):
        tok_all[i * 2 + 1] = gated(i * 2 + 1).astype(BF16)

    shares = [
        sends.start(tok_all.at[i * 2 + 1], lambda i=i: land_s.at[i], place.group(0, 0, 1))
        for i in range(8)
    ]
    next(second)
    next(second)

    @pl.loop(0, 8)
    def _(i):
        pick_cot(i + 6 * (i // 6))

    for copy in shares:
        copy.wait_recv()

    @pl.loop(0, 8)
    def _(i):
        tok_all[i * 2] = (gated(i * 2) + land_s[i].astype(F32)).astype(BF16)

    for i in range(8):
        local(tok_all.at[i * 2], totals_o.at[i])
    for _ in second:
        pass

    @pl.loop(0, 8)
    def _(i):
        pick_cot(6 + i + 2 * (i // 6))

    local(dy, dy_o)
    for copy in copies[6:]:
        copy.wait()
    cot_sends.drain()
    sends.drain()


def forward(tok, cot, meta, w_gate, w_up, w_down):
    d = tok.shape[1]
    hbm = pl.BlockSpec(memory_space=pl.ANY)
    vmem = pl.BlockSpec(memory_space=pltpu.VMEM)
    return pl.pallas_call(
        forward_kernel,
        out_shape=(
            jax.ShapeDtypeStruct((2, 512, d), BF16),
            jax.ShapeDtypeStruct((2, 512, d), BF16),
            jax.ShapeDtypeStruct((2, 2, 512, H_ROWS), F32),
            jax.ShapeDtypeStruct((2, H_ROWS, 512), BF16),
            jax.ShapeDtypeStruct((8, 128, d), BF16),
            jax.ShapeDtypeStruct((16, 8, 128), F32),
            jax.ShapeDtypeStruct((16, 64, 128), BF16),
        ),
        in_specs=[hbm] * 6,
        out_specs=(hbm, hbm, hbm, hbm, hbm, vmem, vmem),
        scratch_shapes=[
            pltpu.VMEM((16, 128, d), BF16),
            pltpu.VMEM((16, 128, d), BF16),
            pltpu.VMEM((16,) + meta.shape, F32),
            pltpu.VMEM(w_gate.shape, BF16),
            pltpu.VMEM(w_up.shape, BF16),
            pltpu.VMEM(w_down.shape, BF16),
            pltpu.VMEM((2, 512, d), BF16),
            pltpu.VMEM((2, 512, d), BF16),
            pltpu.VMEM((2, 512, d), BF16),
            pltpu.VMEM((2, 2, 512, H_ROWS), F32),
            pltpu.VMEM((2, 512, H_ROWS), BF16),
            pltpu.VMEM((2, H_ROWS, 512), BF16),
            pltpu.VMEM((16, 64, 128), F32),
            pltpu.VMEM((8, 128, d), BF16),
            pltpu.SemaphoreType.DMA((128,)),
            pltpu.SemaphoreType.DMA((128,)),
            pltpu.SemaphoreType.DMA((32,)),
        ],
        compiler_params=pltpu.CompilerParams(
            collective_id=0, has_side_effects=True, vmem_limit_bytes=63 * 2**20
        ),
    )(tok, cot, meta, w_gate, w_up, w_down)


def add_into(dst, terms, chunk):
    rows = dst.shape[0]

    @pl.loop(0, rows // chunk)
    def _(i):
        at = pl.ds(pl.multiple_of(i * chunk, chunk), chunk)
        total = terms[0][at].astype(F32)
        for term in terms[1:]:
            total = total + term[at].astype(F32)
        dst[at] = total.astype(dst.dtype)


class Tree:
    def __init__(self, sends, peer, part, land, out, chunk):
        self.sends, self.peer, self.part = sends, peer, part
        self.land, self.out, self.chunk = land, out, chunk

    def open(self):
        s, p, peer = self.sends, self.part, self.peer
        self.far = [
            s.start(p(2, 0), lambda: self.land(0, 0), peer(-1)),
            s.start(p(2, 1), lambda: self.land(0, 1), peer(1)),
        ]
        self.near = [
            s.start(p(1, 0), lambda: self.land(1, 0), peer(1)),
            s.start(p(-1, 1), lambda: self.land(1, 1), peer(-1)),
        ]

    def relay(self):
        self.via = []
        for h, d in ((0, -1), (1, 1)):
            self.far[h].wait_recv()
            add_into(self.out(h), [self.part(d, h), self.land(0, h)], self.chunk)
            self.via.append(self.sends.start(self.out(h), lambda h=h: self.land(2, h), self.peer(d)))

    def close(self, h):
        self.near[h].wait_recv()
        self.via[h].wait_recv()
        return [self.part(0, h), self.land(1, h), self.land(2, h)]


Y_FIRST = ((2, 0), (0, 0), (0, 1), (1, 1))
Z_FIRST = ((2, 1), (1, 0))


def backward_kernel(
    routed_hbm, dy_hbm, pre_hbm, hidden_hbm, wg_hbm, wu_hbm, wd_hbm, t_first, gates_in, pick,
    out_first, out_second, gates_out, grads_hbm, p_hbm,
    land_s, land_y, land_z, land_d, land_dz, land_xb, land_zb, gates_land, early_x, early_y, grads,
    send_sem, recv_sem, load_sem,
):
    place = Place()
    loads = []

    def load(src, dst):
        copy = pltpu.make_async_copy(src, dst, load_sem.at[len(loads)])
        copy.start()
        loads.append(copy)
        return copy

    rows_out = (out_first, out_second)
    sends = Sends(send_sem, recv_sem, place)

    def yy(d):
        return lax.rem(place.y + (d % NY), NY) if d % NY else place.y

    def p_slice(m, e, d, z):
        at = pl.multiple_of((yy(d) * 2 + z) * W_COLS, W_COLS)
        return p_hbm.at[m, e, :, pl.ds(at, W_COLS)]

    trees = {}
    down_z = {}

    def open_partial(m, e):
        if (m, e) in Y_FIRST:
            i = Y_FIRST.index((m, e))
            tree = Tree(
                sends, place.col,
                lambda d, h: p_slice(m, e, d, h),
                lambda k, h: land_y.at[i, k, h],
                None, 64,
            )
            tree.open()
            trees[i] = tree
        else:
            i = Z_FIRST.index((m, e))
            for d in (2, 1, 3, 0):
                down_z[i, d] = sends.start(
                    p_slice(m, e, d, 1 - place.zh), lambda d=d: land_dz.at[i, d], place.col(0, 1)
                )

    shares = {}
    row_state = {}

    def first_phase(
        routed, dy, pre, hidden_t, wg, wu, wd, dhd, dg, du, dg_t, du_t, stage
    ):
        ld = [
            load(hidden_hbm, hidden_t), load(dy_hbm, dy), load(wd_hbm.at[0], wd),
            load(pre_hbm.at[0], pre), load(routed_hbm, routed),
            load(wg_hbm.at[0], wg), load(wu_hbm.at[0], wu),
        ]
        peers = [place.group(*r) for r in GROUP[1:]]
        enter(peers + [place.col(1), place.col(-1), place.col(0, 1)])
        for dz in (1, 0):
            tree = Tree(
                sends, place.group,
                lambda d, h, dz=dz: t_first.at[(d % NX) * 2 + dz, pl.ds(64 * h, 64)],
                lambda k, h, dz=dz: land_xb.at[0, dz, k, h],
                None, 32,
            )
            tree.open()
            row_state.setdefault(0, []).append(tree)
        x_loads = [
            load(t_first.at[6 + dz, pl.ds(0, 64)], early_x.at[dz, 0]) for dz in range(2)
        ] + [
            load(t_first.at[2 + dz, pl.ds(64, 64)], early_x.at[dz, 1]) for dz in range(2)
        ]

        def early_rows():
            for copy in x_loads:
                copy.wait()
            for tree, dz in zip(row_state[0], (1, 0)):
                tree.part = lambda d, h, dz=dz: early_x.at[dz, h]
                tree.out = lambda h, dz=dz: early_x.at[dz, h]
                tree.relay()

        def early_partial():
            y_loads = [
                load(p_slice(*Y_FIRST[0], -1, 0), early_y.at[0]),
                load(p_slice(*Y_FIRST[0], 1, 1), early_y.at[1]),
            ]
            for copy in y_loads:
                copy.wait()
            trees[0].part = lambda d, h: early_y.at[h]
            trees[0].out = lambda h: early_y.at[h]
            trees[0].relay()

        gate_sends = []
        for r in GROUP[1:]:
            to = slot_of(-r[0], r[1], r[2])
            gate_sends.append(
                sends.start(
                    gates_in.at[slot_of(*r)], lambda to=to: gates_land.at[to], place.group(*r)
                )
            )
        pending = []

        def flush():
            for copies, m, e in pending:
                for copy in copies:
                    copy.wait()
                open_partial(m, e)
            pending.clear()

        def partial(m, e, left, right):
            copies = []
            before = list(pending)
            for n in range(2):
                for entry in before:
                    entry[0][n].wait()

                @pl.loop(0, 2)
                def _(k):
                    at = pl.ds(pl.multiple_of(k * 512, 512), 512)
                    src = pl.ds(pl.multiple_of(n * 1024 + k * 512, 512), 512)
                    stage[n, :, at] = dot_nn(left[...], right[:, src]).astype(BF16)

                copies.append(
                    load(stage.at[n], p_hbm.at[m, e, :, pl.ds(n * 1024, 1024)])
                )
            for entry in before:
                open_partial(entry[1], entry[2])
                pending.remove(entry)
            pending.append((copies, m, e))

        ld[0].wait()
        ld[1].wait()
        partial(2, 0, hidden_t.at[0], dy.at[0])
        partial(2, 1, hidden_t.at[1], dy.at[1])
        for e in range(2):
            if e == 0:
                ld[2].wait()
                ld[3].wait()
                ld[4].wait()
                ld[5].wait()
                ld[6].wait()
            else:
                next_wd.wait()
                next_pre.wait()
            dhd[...] = dot_nt(dy[e], wd[...])
            flush()
            if e == 0:
                next_wd = load(wd_hbm.at[1], wd)

            @pl.loop(0, 16)
            def _(i):
                at = pl.ds(pl.multiple_of(i * 32, 32), 32)
                gate = pre[0, at]
                s = jax.nn.sigmoid(gate)
                back = dhd[at]
                dg[at] = (back * pre[1, at] * s * (1.0 + gate * (1.0 - s))).astype(BF16)
                du[at] = (back * gate * s).astype(BF16)

            if e == 0:
                next_pre = load(pre_hbm.at[1], pre)
            dg_t[...] = dg[...].T
            du_t[...] = du[...].T
            if e == 0:
                partial(0, e, dg_t, routed.at[e])
                partial(1, e, du_t, routed.at[e])
            else:
                for copy in next_w:
                    copy.wait()

            def back(n):
                at = pl.ds(pl.multiple_of(n * 512, 512), 512)
                total = dot_nn(dg[...], wg[:, at]) + dot_nn(du[...], wu[:, at])
                dy[e, :, at] = total.astype(BF16)

            pl.loop(0, 1)(back)
            flush()
            pl.loop(1, 4)(back)

            if e == 0:
                next_w = [load(wg_hbm.at[1], wg), load(wu_hbm.at[1], wu)]
                early_rows()

        def back_rows(j):
            at = pl.ds(pl.multiple_of(j * 32, 32), 32)
            rows = jnp.concatenate([dy[0, at], dy[1, at]], axis=0)
            return dot_tn(pick[j], rows)

        @pl.loop(0, 4)
        def _(i):
            at = pl.ds(pl.multiple_of(i * 128, 128), 128)
            wg[at] = back_rows(i * 2 + 1).astype(BF16)
            wu[at] = back_rows(i * 2 + 9).astype(BF16)

        for i in range(8):
            shares[i] = sends.start(
                (wg, wu)[i // 4].at[pl.ds((i % 4) * 128, 128)], lambda i=i: land_s.at[i],
                place.group(0, 0, 1),
            )
        partial(0, 1, dg_t, routed.at[1])
        partial(1, 1, du_t, routed.at[1])
        flush()
        early_partial()
        for i in range(8):
            shares[i].wait_recv()

        @pl.loop(0, 8)
        def _(i):
            land_s[i] = (back_rows(i * 2) + land_s[i].astype(F32)).astype(BF16)

        for dz in (1, 0):

            def part(d, h, dz=dz):
                return land_s.at[(d % NX) * 2 + dz, pl.ds(64 * h, 64)]

            tree = Tree(
                sends, place.group, part,
                lambda k, h, dz=dz: land_xb.at[1, dz, k, h],
                lambda h, part=part: part((-1, 1)[h], h),
                32,
            )
            tree.open()
            row_state.setdefault(1, []).append(tree)
        for i in range(8):
            shares[i].wait_send()
        for copy in gate_sends:
            copy.wait_recv()
        total = gates_in[0]
        for i in range(1, 16):
            total = total + gates_land[i]
        gates_out[...] = total

    def second_phase(own_p, out_z, t_down, out_d, own_x, v_rows):
        x_own = [load(t_first.at[dz], own_x.at[dz]) for dz in range(2)]
        own_loads = {}
        for i, (m, e) in enumerate(Y_FIRST):
            own_loads[i] = [
                load(p_slice(m, e, -1, 0), own_p.at[i, 0]),
                load(p_slice(m, e, 1, 1), own_p.at[i, 1]),
                load(p_slice(m, e, 0, 0), own_p.at[i, 2]),
                load(p_slice(m, e, 0, 1), own_p.at[i, 3]),
            ]
        down_loads = {}
        for i, (m, e) in enumerate(Z_FIRST):
            down_loads[i] = [load(p_slice(m, e, d, place.zh), t_down.at[i, d]) for d in range(NY)]

        def rows_mid():
            for tree in row_state[1]:
                tree.relay()

        def rows_end(r):
            if r == 0:
                for copy in x_own:
                    copy.wait()
                for tree, dz in zip(row_state[0], (1, 0)):
                    tree.part = lambda d, h, dz=dz: own_x.at[dz, pl.ds(64 * h, 64)]
            for h in range(2):
                add_into(v_rows.at[r, 1, pl.ds(64 * h, 64)], row_state[r][0].close(h), 32)
            copy = sends.start(v_rows.at[r, 1], lambda: land_zb.at[r], place.group(0, 1, 0))
            for h in range(2):
                add_into(v_rows.at[r, 0, pl.ds(64 * h, 64)], row_state[r][1].close(h), 32)
            return copy

        def rows_last(r, copy):
            copy.wait_recv()
            add_into(rows_out[r], [v_rows.at[r, 0], land_zb.at[r]], 32)

        def down_mid(i):
            for copy in down_loads[i]:
                copy.wait()
            for d in (2, 1, 3, 0):
                down_z[i, d].wait_recv()
                add_into(t_down.at[i, d], [t_down.at[i, d], land_dz.at[i, d]], 64)
            half = H_ROWS // 2
            tree = Tree(
                sends, place.col,
                lambda d, h: t_down.at[i, d % NY, pl.ds(half * h, half)],
                lambda k, h: land_d.at[i, k, pl.ds(half * h, half)],
                lambda h: out_d.at[i, pl.ds(half * h, half)],
                32,
            )
            tree.open()
            return tree

        def down_end(i, tree):
            m, e = Z_FIRST[i]
            half = H_ROWS // 2
            for h in range(2):
                add_into(grads.at[m, e, pl.ds(half * h, half)], tree.close(h), 32)
            finals.append(load(grads.at[m, e], grads_hbm.at[m, e]))

        def y_relay(i):
            for copy in own_loads[i]:
                copy.wait()
            trees[i].part = lambda d, h: own_p.at[i, {-1: 0, 1: 1, 0: 2 + h}[d]]
            trees[i].out = lambda h: own_p.at[i, h]
            if i > 0:
                trees[i].relay()

        def y_end(i):
            m, e = Y_FIRST[i]
            for h in range(2):
                terms = trees[i].close(h)

                @pl.when(place.zh != h)
                def _():
                    add_into(out_z.at[i], terms, 64)

                @pl.when(place.zh == h)
                def _():
                    add_into(grads.at[m, e], terms, 64)

            return sends.start(out_z.at[i], lambda: land_z.at[i], place.col(0, 1))

        def z_end(i, copy):
            m, e = Y_FIRST[i]
            copy.wait_recv()
            dst = grads.at[m, e]
            add_into(dst, [dst, land_z.at[i]], 64)
            finals.append(load(dst, grads_hbm.at[m, e]))

        y_relay(0)
        y_relay(1)
        d0 = down_mid(0)
        finals = []
        r0 = rows_end(0)
        z0 = y_end(0)
        rows_mid()
        z1 = y_end(1)
        y_relay(2)
        y_relay(3)
        d1 = down_mid(1)
        rows_last(0, r0)
        d0.relay()
        z_end(0, z0)
        z2 = y_end(2)
        r1 = rows_end(1)
        d1.relay()
        z_end(1, z1)
        z3 = y_end(3)
        down_end(0, d0)
        rows_last(1, r1)
        down_end(1, d1)
        z_end(2, z2)
        z_end(3, z3)
        for copy in finals:
            copy.wait()
        for copy in sends.made:
            if all(copy is not c for c in shares.values()):
                copy.wait_send()

    def buf(*shape):
        return pltpu.VMEM(shape, BF16)

    d = t_first.shape[-1]
    slab = (H_ROWS, W_COLS)
    pl.run_scoped(
        first_phase,
        buf(2, 512, d), buf(2, 512, d), pltpu.VMEM((2, 512, H_ROWS), F32), buf(2, H_ROWS, 512),
        buf(H_ROWS, d), buf(H_ROWS, d), buf(H_ROWS, d), pltpu.VMEM((512, H_ROWS), F32),
        buf(512, H_ROWS), buf(512, H_ROWS), buf(H_ROWS, 512), buf(H_ROWS, 512),
        buf(2, H_ROWS, 1024),
    )
    pl.run_scoped(
        second_phase,
        buf(4, 4, *slab), buf(4, *slab), buf(2, 4, *slab), buf(2, *slab),
        buf(2, 128, d), buf(2, 2, 128, d),
    )


def backward(*operands):
    d = operands[0].shape[-1]
    n = 192
    hbm = pl.BlockSpec(memory_space=pl.ANY)
    vmem = pl.BlockSpec(memory_space=pltpu.VMEM)
    slab = (H_ROWS, W_COLS)

    def buf(*shape):
        return pltpu.VMEM(shape, BF16)

    return pl.pallas_call(
        backward_kernel,
        out_shape=(
            jax.ShapeDtypeStruct((128, d), BF16),
            jax.ShapeDtypeStruct((128, d), BF16),
            jax.ShapeDtypeStruct((8, 128), F32),
            jax.ShapeDtypeStruct((3, 2) + slab, F32),
            jax.ShapeDtypeStruct((3, 2, H_ROWS, d), BF16),
        ),
        in_specs=[hbm] * 8 + [vmem] * 2,
        out_specs=(vmem,) * 3 + (hbm,) * 2,
        scratch_shapes=[
            buf(8, 128, d), buf(4, 3, 2, *slab), buf(4, *slab), buf(2, 3, *slab), buf(2, 4, *slab),
            buf(2, 2, 3, 2, 64, d), buf(2, 128, d),
            pltpu.VMEM((16, 8, 128), F32),
            buf(2, 2, 64, d), buf(2, *slab), pltpu.VMEM((3, 2) + slab, F32),
            pltpu.SemaphoreType.DMA((n,)),
            pltpu.SemaphoreType.DMA((n,)),
            pltpu.SemaphoreType.DMA((112,)),
        ],
        compiler_params=pltpu.CompilerParams(
            collective_id=1, has_side_effects=True, vmem_limit_bytes=63 * 2**20
        ),
    )(*operands)[:4]


def shards(tokens, cotangent, route_gates, expert_ids, slot_index, w_gate, w_up, w_down):
    target = (expert_ids * 32 + slot_index).astype(F32).T
    gap = jnp.zeros((2, 128), F32)
    meta = jnp.concatenate([target, gap, route_gates.T, gap])
    wg, wu = w_gate.transpose(0, 2, 1), w_up.transpose(0, 2, 1)
    routed, grad_rows, pre, hidden_t, o_out, gates_in, pick = forward(
        tokens, cotangent, meta, wg, wu, w_down
    )
    out, grad, gates, grads = backward(
        routed, grad_rows, pre, hidden_t, wg, wu, w_down, o_out, gates_in, pick
    )
    return (
        out,
        grad,
        gates[0:6].T,
        grads[0].transpose(0, 2, 1),
        grads[1].transpose(0, 2, 1),
        grads[2],
    )


def solution(mesh):
    row = P(("expert", "dp"), None)
    weight = P("expert", None, None)
    return jax.shard_map(
        shards,
        mesh=mesh,
        in_specs=(row, row, row, row, row, weight, weight, weight),
        out_specs=(row, row, row, P("expert", "dp", None), P("expert", "dp", None), P("expert", None, "dp")),
        check_vma=False,
    )
```

```python
import functools

import jax
import jax.numpy as jnp
from jax import lax
from jax.experimental import pallas as pl
from jax.experimental.pallas import tpu as pltpu
from jax.sharding import PartitionSpec as P

MESH = pl.DeviceIdType.MESH
F32 = jnp.float32
BF16 = jnp.bfloat16
NX = 4
NY = 4
H_ROWS = 704
W_COLS = 256


def slot_of(dx, dz, dc):
    return (dx % NX) * 4 + (dz % 2) * 2 + (dc % 2)


class Place:
    def __init__(self):
        e = lax.axis_index("expert")
        q = lax.axis_index("dp")
        self.e, self.q = e, q
        self.x, self.zl, self.c = e // 4, (e // 2) % 2, e % 2
        self.y, self.zh = q // 2, q % 2

    def group(self, dx=0, dz=0, dc=0):
        x = lax.rem(self.x + (dx % NX), NX) if dx % NX else self.x
        z = 1 - self.zl if dz % 2 else self.zl
        c = 1 - self.c if dc % 2 else self.c
        return (x * 4 + z * 2 + c, self.q)

    def col(self, dy=0, dz=0):
        y = lax.rem(self.y + (dy % NY), NY) if dy % NY else self.y
        z = 1 - self.zh if dz % 2 else self.zh
        return (self.e, y * 2 + z)


def enter(peers):
    barrier = pltpu.get_barrier_semaphore()
    for peer in peers:
        pl.semaphore_signal(barrier, inc=1, device_id=peer, device_id_type=MESH)
    pl.semaphore_wait(barrier, len(peers))


class Sent:
    def __init__(self, owner, i, dst):
        self.owner, self.i, self.dst = owner, i, dst

    def again(self):
        dst = self.dst()
        return pltpu.make_async_remote_copy(
            src_ref=dst,
            dst_ref=dst,
            send_sem=self.owner.send_sem.at[self.i],
            recv_sem=self.owner.recv_sem.at[self.i],
            device_id=self.owner.home,
            device_id_type=MESH,
        )

    def wait_recv(self):
        self.again().wait_recv()

    def wait_send(self):
        self.again().wait_send()


class Sends:
    def __init__(self, send_sem, recv_sem, place):
        self.send_sem, self.recv_sem = send_sem, recv_sem
        self.home = (place.e, place.q)
        self.made = []

    def start(self, src, dst, peer):
        i = len(self.made)
        pltpu.make_async_remote_copy(
            src_ref=src,
            dst_ref=dst(),
            send_sem=self.send_sem.at[i],
            recv_sem=self.recv_sem.at[i],
            device_id=peer,
            device_id_type=MESH,
        ).start()
        copy = Sent(self, i, dst)
        self.made.append(copy)
        return copy

    def drain(self):
        for copy in self.made:
            copy.wait_send()


def dot_nn(a, b):
    return jnp.dot(a, b, preferred_element_type=F32)


def dot_nt(a, b):
    return lax.dot_general(a, b, (((1,), (1,)), ((), ())), preferred_element_type=F32)


def dot_tn(a, b):
    return lax.dot_general(a, b, (((0,), (0,)), ((), ())), preferred_element_type=F32)


GROUP = [(dx, dz, dc) for dx in range(NX) for dz in range(2) for dc in range(2)]
A = (0, 64)
B = (64, 128)
A0, A1, B0, B1 = (0, 32), (32, 64), (64, 96), (96, 128)


def gather_rows(sends, place, own, buf):
    arrived = {}

    def push(dx, dz, dc, rows, ddx=0, ddz=0, ddc=0):
        lo, hi = rows
        here = own if (dx, dz, dc) == (0, 0, 0) else buf.at[slot_of(dx, dz, dc)]
        there = ((dx - ddx) % NX, (dz - ddz) % 2, (dc - ddc) % 2)
        arrived[there + (rows,)] = sends.start(
            here.at[pl.ds(lo, hi - lo)],
            lambda: buf.at[slot_of(*there), pl.ds(lo, hi - lo)],
            place.group(ddx, ddz, ddc),
        )

    def take(dx, dz, rows):
        arrived[(dx % NX, dz % 2, 0, rows)].wait_recv()
        push(dx % NX, dz % 2, 0, rows, ddc=1)

    yield
    push(0, 0, 0, B, ddz=1)
    push(0, 0, 0, A, ddx=1)
    push(0, 0, 0, A, ddx=-1)
    push(0, 0, 0, B, ddx=1)
    push(0, 0, 0, B, ddx=-1)
    push(0, 0, 0, A, ddz=1)
    push(0, 0, 0, (0, 128), ddc=1)
    yield
    take(0, 1, B)
    push(0, 1, 0, B, ddx=1)
    push(0, 1, 0, B, ddx=-1)
    yield
    take(1, 0, A)
    push(1, 0, 0, A0, ddx=-1)
    push(1, 0, 0, A, ddz=1)
    take(-1, 0, A)
    push(3, 0, 0, A1, ddx=1)
    push(3, 0, 0, A, ddz=1)
    yield
    take(1, 0, B)
    push(1, 0, 0, B0, ddx=-1)
    take(-1, 0, B)
    push(3, 0, 0, B1, ddx=1)
    take(0, 1, A)
    yield
    take(1, 1, B)
    push(1, 1, 0, B0, ddx=-1)
    take(-1, 1, B)
    push(3, 1, 0, B1, ddx=1)
    take(2, 0, A0)
    push(2, 0, 0, A0, ddz=1)
    take(2, 0, A1)
    push(2, 0, 0, A1, ddz=1)
    yield
    take(1, 1, A)
    take(3, 1, A)
    take(2, 0, B0)
    take(2, 0, B1)
    take(2, 1, B0)
    take(2, 1, B1)
    take(2, 1, A0)
    take(2, 1, A1)
    yield
    near = ((0, 0), (0, 1), (1, 0), (3, 0))
    for first in (True, False):
        for key in list(arrived):
            if key[2] == 1 and (key[0:2] in near) == first:
                arrived[key].wait_recv()
        yield


def forward_kernel(
    tok, cot, ids, slots, route, wg_hbm, wu_hbm, wd_hbm,
    routed_o, dy_o, pre_o, hidden_o, totals_o, gates_o, pick,
    tok_all, cot_all, meta_all, wg, wu, wd, routed, y_rows, dy, pre, hidden, hidden_t, gate_col, land_s, meta,
    send_sem, recv_sem, copy_sem,
):
    place = Place()
    enter([place.group(*r) for r in GROUP[1:]])
    copies = []
    meta[...] = jnp.zeros((16, 128), F32)
    meta[0:6] = (ids[...] * 32 + slots[...]).astype(F32)
    meta[8:14] = route[...]

    def local(src, dst):
        copy = pltpu.make_async_copy(src, dst, copy_sem.at[len(copies)])
        copy.start()
        copies.append(copy)
        return copy

    tok_sends = Sends(send_sem.at[pl.ds(0, 48)], recv_sem.at[pl.ds(0, 48)], place)
    cot_sends = Sends(send_sem.at[pl.ds(48, 48)], recv_sem.at[pl.ds(48, 48)], place)
    sends = Sends(send_sem.at[pl.ds(96, 32)], recv_sem.at[pl.ds(96, 32)], place)
    metas = []
    for r in GROUP[1:]:
        to = slot_of(-r[0], r[1], r[2])
        metas.append(sends.start(meta, lambda to=to: meta_all.at[to], place.group(*r)))
    first = gather_rows(tok_sends, place, tok, tok_all)
    second = gather_rows(cot_sends, place, cot, cot_all)
    next(first)
    next(second)
    next(first)
    own = [local(tok, tok_all.at[0]), local(cot, cot_all.at[0]), local(meta, meta_all.at[0])]
    weights = [local(wg_hbm, wg), local(wu_hbm, wu), local(wd_hbm, wd)]
    next(first)
    for copy in metas:
        copy.wait_recv()
    for copy in own:
        copy.wait()
    slot = (lax.broadcasted_iota(jnp.int32, (64, 128), 0) + place.e * 64).astype(F32)

    @pl.loop(0, 16)
    def _(j):
        total = jnp.zeros((64, 128), F32)
        gate = jnp.zeros((64, 128), F32)
        for k in range(6):
            hit = slot == jnp.broadcast_to(meta_all[j, k : k + 1], (64, 128))
            total = total + jnp.where(hit, 1.0, 0.0)
            row = jnp.broadcast_to(meta_all[j, 8 + k : 9 + k], (64, 128))
            gate = gate + jnp.where(hit, row, 0.0)
        pick[j] = total.astype(BF16)
        gate_col[j] = jnp.broadcast_to(jnp.sum(gate, axis=1, keepdims=True), (64, 128))

    next(first)
    next(first)
    next(first)
    next(second)
    for _ in first:
        pass
    next(second)

    def rows32(j):
        return pl.ds(pl.multiple_of(j * 32, 32), 32)

    @pl.loop(0, 16)
    def _(j):
        got = jnp.dot(pick[j], tok_all[j], preferred_element_type=F32).astype(BF16)
        routed[0, rows32(j)] = got[0:32]
        routed[1, rows32(j)] = got[32:64]

    routed_out = local(routed, routed_o)
    next(second)
    for copy in weights:
        copy.wait()

    def up(e):
        pre[e, 0] = dot_nt(routed[e], wg[e])
        pre[e, 1] = dot_nt(routed[e], wu[e])

        @pl.loop(0, 16)
        def _(i):
            at = rows32(i)
            gate = pre[e, 0, at]
            hidden[e, at] = (gate * jax.nn.sigmoid(gate) * pre[e, 1, at]).astype(BF16)

        local(pre.at[e], pre_o.at[e])

    def down(e):
        hidden_t[e] = hidden[e].T
        local(hidden_t.at[e], hidden_o.at[e])
        for n in range(2):
            at = pl.ds(n * 1024, 1024)
            y_rows[e, :, at] = jnp.dot(
                hidden[e], wd[e, :, at], preferred_element_type=F32
            ).astype(BF16)

    def both(ref, j):
        return jnp.concatenate([ref[0, rows32(j)], ref[1, rows32(j)]], axis=0)

    def gated(j):
        scaled = (both(y_rows, j).astype(F32) * gate_col[j, :, 0:1]).astype(BF16)
        return dot_tn(pick[j], scaled)

    def pick_cot(j):
        got = jnp.dot(pick[j], cot_all[j], preferred_element_type=F32)
        by_slot = jnp.sum(got * both(y_rows, j).astype(F32), axis=1, keepdims=True)
        scaled = (got * gate_col[j, :, 0:1]).astype(BF16)
        dy[0, rows32(j)] = scaled[0:32]
        dy[1, rows32(j)] = scaled[32:64]
        by_slot = jnp.broadcast_to(by_slot, (64, 128))
        parts = []
        for k in range(6):
            hit = slot == jnp.broadcast_to(meta_all[j, k : k + 1], (64, 128))
            parts.append(jnp.sum(jnp.where(hit, by_slot, 0.0), axis=0, keepdims=True))
        parts.append(jnp.zeros((2, 128), F32))
        gates_o[j] = jnp.concatenate(parts, axis=0)

    up(0)
    next(second)
    up(1)
    next(second)
    down(0)
    down(1)
    tok_sends.drain()

    @pl.loop(0, 8)
    def _(i):
        tok_all[i * 2 + 1] = gated(i * 2 + 1).astype(BF16)

    shares = [
        sends.start(tok_all.at[i * 2 + 1], lambda i=i: land_s.at[i], place.group(0, 0, 1))
        for i in range(8)
    ]
    next(second)
    next(second)

    @pl.loop(0, 8)
    def _(i):
        pick_cot(i + 6 * (i // 6))

    for copy in shares:
        copy.wait_recv()

    @pl.loop(0, 8)
    def _(i):
        tok_all[i * 2] = (gated(i * 2) + land_s[i].astype(F32)).astype(BF16)

    for i in range(8):
        local(tok_all.at[i * 2], totals_o.at[i])
    for _ in second:
        pass

    @pl.loop(0, 8)
    def _(i):
        pick_cot(6 + i + 2 * (i // 6))

    local(dy, dy_o)
    for copy in copies[6:]:
        copy.wait()
    cot_sends.drain()
    sends.drain()


def forward(tok, cot, ids, slots, route, w_gate, w_up, w_down):
    d = tok.shape[1]
    hbm = pl.BlockSpec(memory_space=pl.ANY)
    vmem = pl.BlockSpec(memory_space=pltpu.VMEM)
    return pl.pallas_call(
        forward_kernel,
        out_shape=(
            jax.ShapeDtypeStruct((2, 512, d), BF16),
            jax.ShapeDtypeStruct((2, 512, d), BF16),
            jax.ShapeDtypeStruct((2, 2, 512, H_ROWS), F32),
            jax.ShapeDtypeStruct((2, H_ROWS, 512), BF16),
            jax.ShapeDtypeStruct((8, 128, d), BF16),
            jax.ShapeDtypeStruct((16, 8, 128), F32),
            jax.ShapeDtypeStruct((16, 64, 128), BF16),
        ),
        in_specs=[hbm] * 2 + [vmem] * 3 + [hbm] * 3,
        out_specs=(hbm, hbm, hbm, hbm, hbm, vmem, vmem),
        scratch_shapes=[
            pltpu.VMEM((16, 128, d), BF16),
            pltpu.VMEM((16, 128, d), BF16),
            pltpu.VMEM((16, 16, 128), F32),
            pltpu.VMEM(w_gate.shape, BF16),
            pltpu.VMEM(w_up.shape, BF16),
            pltpu.VMEM(w_down.shape, BF16),
            pltpu.VMEM((2, 512, d), BF16),
            pltpu.VMEM((2, 512, d), BF16),
            pltpu.VMEM((2, 512, d), BF16),
            pltpu.VMEM((2, 2, 512, H_ROWS), F32),
            pltpu.VMEM((2, 512, H_ROWS), BF16),
            pltpu.VMEM((2, H_ROWS, 512), BF16),
            pltpu.VMEM((16, 64, 128), F32),
            pltpu.VMEM((8, 128, d), BF16),
            pltpu.VMEM((16, 128), F32),
            pltpu.SemaphoreType.DMA((128,)),
            pltpu.SemaphoreType.DMA((128,)),
            pltpu.SemaphoreType.DMA((32,)),
        ],
        compiler_params=pltpu.CompilerParams(
            collective_id=0, has_side_effects=True, vmem_limit_bytes=63 * 2**20
        ),
    )(tok, cot, ids, slots, route, w_gate, w_up, w_down)


def add_into(dst, terms, chunk):
    rows = dst.shape[0]

    @pl.loop(0, rows // chunk)
    def _(i):
        at = pl.ds(pl.multiple_of(i * chunk, chunk), chunk)
        total = terms[0][at].astype(F32)
        for term in terms[1:]:
            total = total + term[at].astype(F32)
        dst[at] = total.astype(dst.dtype)


class Tree:
    def __init__(self, sends, peer, part, land, out, chunk):
        self.sends, self.peer, self.part = sends, peer, part
        self.land, self.out, self.chunk = land, out, chunk

    def open(self):
        s, p, peer = self.sends, self.part, self.peer
        self.far = [
            s.start(p(2, 0), lambda: self.land(0, 0), peer(-1)),
            s.start(p(2, 1), lambda: self.land(0, 1), peer(1)),
        ]
        self.near = [
            s.start(p(1, 0), lambda: self.land(1, 0), peer(1)),
            s.start(p(-1, 1), lambda: self.land(1, 1), peer(-1)),
        ]

    def relay(self):
        self.via = []
        for h, d in ((0, -1), (1, 1)):
            self.far[h].wait_recv()
            add_into(self.out(h), [self.part(d, h), self.land(0, h)], self.chunk)
            self.via.append(self.sends.start(self.out(h), lambda h=h: self.land(2, h), self.peer(d)))

    def close(self, h):
        self.near[h].wait_recv()
        self.via[h].wait_recv()
        return [self.part(0, h), self.land(1, h), self.land(2, h)]


Y_FIRST = ((2, 0), (0, 0), (0, 1), (1, 1))
Z_FIRST = ((2, 1), (1, 0))


def backward_kernel(
    routed_hbm, dy_hbm, pre_hbm, hidden_hbm, wg_hbm, wu_hbm, wd_hbm, t_first, gates_in, pick,
    out_first, out_second, gates_out, grads_hbm, p_hbm,
    land_s, land_y, land_z, land_d, land_dz, land_xb, land_zb, gates_land, early_x, early_y, grads,
    send_sem, recv_sem, load_sem,
):
    place = Place()
    loads = []

    def load(src, dst):
        copy = pltpu.make_async_copy(src, dst, load_sem.at[len(loads)])
        copy.start()
        loads.append(copy)
        return copy

    rows_out = (out_first, out_second)
    sends = Sends(send_sem, recv_sem, place)

    def yy(d):
        return lax.rem(place.y + (d % NY), NY) if d % NY else place.y

    def p_slice(m, e, d, z):
        at = pl.multiple_of((yy(d) * 2 + z) * W_COLS, W_COLS)
        return p_hbm.at[m, e, :, pl.ds(at, W_COLS)]

    trees = {}
    down_z = {}

    def open_partial(m, e):
        if (m, e) in Y_FIRST:
            i = Y_FIRST.index((m, e))
            tree = Tree(
                sends, place.col,
                lambda d, h: p_slice(m, e, d, h),
                lambda k, h: land_y.at[i, k, h],
                None, 64,
            )
            tree.open()
            trees[i] = tree
        else:
            i = Z_FIRST.index((m, e))
            for d in (2, 1, 3, 0):
                down_z[i, d] = sends.start(
                    p_slice(m, e, d, 1 - place.zh), lambda d=d: land_dz.at[i, d], place.col(0, 1)
                )

    shares = {}
    row_state = {}

    def first_phase(
        routed, dy, pre, hidden_t, wg, wu, wd, dhd, dg, du, dg_t, du_t, stage
    ):
        ld = [
            load(hidden_hbm, hidden_t), load(dy_hbm, dy), load(wd_hbm.at[0], wd),
            load(pre_hbm.at[0], pre), load(routed_hbm, routed),
            load(wg_hbm.at[0], wg), load(wu_hbm.at[0], wu),
        ]
        peers = [place.group(*r) for r in GROUP[1:]]
        enter(peers + [place.col(1), place.col(-1), place.col(0, 1)])
        for dz in (1, 0):
            tree = Tree(
                sends, place.group,
                lambda d, h, dz=dz: t_first.at[(d % NX) * 2 + dz, pl.ds(64 * h, 64)],
                lambda k, h, dz=dz: land_xb.at[0, dz, k, h],
                None, 32,
            )
            tree.open()
            row_state.setdefault(0, []).append(tree)
        x_loads = [
            load(t_first.at[6 + dz, pl.ds(0, 64)], early_x.at[dz, 0]) for dz in range(2)
        ] + [
            load(t_first.at[2 + dz, pl.ds(64, 64)], early_x.at[dz, 1]) for dz in range(2)
        ]

        def early_rows():
            for copy in x_loads:
                copy.wait()
            for tree, dz in zip(row_state[0], (1, 0)):
                tree.part = lambda d, h, dz=dz: early_x.at[dz, h]
                tree.out = lambda h, dz=dz: early_x.at[dz, h]
                tree.relay()

        def early_partial():
            y_loads = [
                load(p_slice(*Y_FIRST[0], -1, 0), early_y.at[0]),
                load(p_slice(*Y_FIRST[0], 1, 1), early_y.at[1]),
            ]
            for copy in y_loads:
                copy.wait()
            trees[0].part = lambda d, h: early_y.at[h]
            trees[0].out = lambda h: early_y.at[h]
            trees[0].relay()

        gate_sends = []
        for r in GROUP[1:]:
            to = slot_of(-r[0], r[1], r[2])
            gate_sends.append(
                sends.start(
                    gates_in.at[slot_of(*r)], lambda to=to: gates_land.at[to], place.group(*r)
                )
            )
        pending = []

        def flush():
            for copies, m, e in pending:
                for copy in copies:
                    copy.wait()
                open_partial(m, e)
            pending.clear()

        def partial(m, e, left, right):
            copies = []
            before = list(pending)
            for n in range(2):
                for entry in before:
                    entry[0][n].wait()

                @pl.loop(0, 2)
                def _(k):
                    at = pl.ds(pl.multiple_of(k * 512, 512), 512)
                    src = pl.ds(pl.multiple_of(n * 1024 + k * 512, 512), 512)
                    stage[n, :, at] = dot_nn(left[...], right[:, src]).astype(BF16)

                copies.append(
                    load(stage.at[n], p_hbm.at[m, e, :, pl.ds(n * 1024, 1024)])
                )
            for entry in before:
                open_partial(entry[1], entry[2])
                pending.remove(entry)
            pending.append((copies, m, e))

        ld[0].wait()
        ld[1].wait()
        partial(2, 0, hidden_t.at[0], dy.at[0])
        partial(2, 1, hidden_t.at[1], dy.at[1])
        for e in range(2):
            if e == 0:
                ld[2].wait()
                ld[3].wait()
                ld[4].wait()
                ld[5].wait()
                ld[6].wait()
            else:
                next_wd.wait()
                next_pre.wait()
            dhd[...] = dot_nt(dy[e], wd[...])
            flush()
            if e == 0:
                next_wd = load(wd_hbm.at[1], wd)

            @pl.loop(0, 16)
            def _(i):
                at = pl.ds(pl.multiple_of(i * 32, 32), 32)
                gate = pre[0, at]
                s = jax.nn.sigmoid(gate)
                back = dhd[at]
                dg[at] = (back * pre[1, at] * s * (1.0 + gate * (1.0 - s))).astype(BF16)
                du[at] = (back * gate * s).astype(BF16)

            if e == 0:
                next_pre = load(pre_hbm.at[1], pre)
            dg_t[...] = dg[...].T
            du_t[...] = du[...].T
            if e == 0:
                partial(0, e, dg_t, routed.at[e])
                partial(1, e, du_t, routed.at[e])
            else:
                for copy in next_w:
                    copy.wait()

            def back(n):
                at = pl.ds(pl.multiple_of(n * 512, 512), 512)
                total = dot_nn(dg[...], wg[:, at]) + dot_nn(du[...], wu[:, at])
                dy[e, :, at] = total.astype(BF16)

            pl.loop(0, 1)(back)
            flush()
            pl.loop(1, 4)(back)

            if e == 0:
                next_w = [load(wg_hbm.at[1], wg), load(wu_hbm.at[1], wu)]
                early_rows()

        def back_rows(j):
            at = pl.ds(pl.multiple_of(j * 32, 32), 32)
            rows = jnp.concatenate([dy[0, at], dy[1, at]], axis=0)
            return dot_tn(pick[j], rows)

        @pl.loop(0, 4)
        def _(i):
            at = pl.ds(pl.multiple_of(i * 128, 128), 128)
            wg[at] = back_rows(i * 2 + 1).astype(BF16)
            wu[at] = back_rows(i * 2 + 9).astype(BF16)

        for i in range(8):
            shares[i] = sends.start(
                (wg, wu)[i // 4].at[pl.ds((i % 4) * 128, 128)], lambda i=i: land_s.at[i],
                place.group(0, 0, 1),
            )
        partial(0, 1, dg_t, routed.at[1])
        partial(1, 1, du_t, routed.at[1])
        flush()
        early_partial()
        for i in range(8):
            shares[i].wait_recv()

        @pl.loop(0, 8)
        def _(i):
            land_s[i] = (back_rows(i * 2) + land_s[i].astype(F32)).astype(BF16)

        for dz in (1, 0):

            def part(d, h, dz=dz):
                return land_s.at[(d % NX) * 2 + dz, pl.ds(64 * h, 64)]

            tree = Tree(
                sends, place.group, part,
                lambda k, h, dz=dz: land_xb.at[1, dz, k, h],
                lambda h, part=part: part((-1, 1)[h], h),
                32,
            )
            tree.open()
            row_state.setdefault(1, []).append(tree)
        for i in range(8):
            shares[i].wait_send()
        for copy in gate_sends:
            copy.wait_recv()
        total = gates_in[0]
        for i in range(1, 16):
            total = total + gates_land[i]
        gates_out[...] = total

    def second_phase(own_p, out_z, t_down, out_d, own_x, v_rows):
        x_own = [load(t_first.at[dz], own_x.at[dz]) for dz in range(2)]
        own_loads = {}
        for i, (m, e) in enumerate(Y_FIRST):
            own_loads[i] = [
                load(p_slice(m, e, -1, 0), own_p.at[i, 0]),
                load(p_slice(m, e, 1, 1), own_p.at[i, 1]),
                load(p_slice(m, e, 0, 0), own_p.at[i, 2]),
                load(p_slice(m, e, 0, 1), own_p.at[i, 3]),
            ]
        down_loads = {}
        for i, (m, e) in enumerate(Z_FIRST):
            down_loads[i] = [load(p_slice(m, e, d, place.zh), t_down.at[i, d]) for d in range(NY)]

        def rows_mid():
            for tree in row_state[1]:
                tree.relay()

        def rows_end(r):
            if r == 0:
                for copy in x_own:
                    copy.wait()
                for tree, dz in zip(row_state[0], (1, 0)):
                    tree.part = lambda d, h, dz=dz: own_x.at[dz, pl.ds(64 * h, 64)]
            for h in range(2):
                add_into(v_rows.at[r, 1, pl.ds(64 * h, 64)], row_state[r][0].close(h), 32)
            copy = sends.start(v_rows.at[r, 1], lambda: land_zb.at[r], place.group(0, 1, 0))
            for h in range(2):
                add_into(v_rows.at[r, 0, pl.ds(64 * h, 64)], row_state[r][1].close(h), 32)
            return copy

        def rows_last(r, copy):
            copy.wait_recv()
            add_into(rows_out[r], [v_rows.at[r, 0], land_zb.at[r]], 32)

        def down_mid(i):
            for copy in down_loads[i]:
                copy.wait()
            for d in (2, 1, 3, 0):
                down_z[i, d].wait_recv()
                add_into(t_down.at[i, d], [t_down.at[i, d], land_dz.at[i, d]], 64)
            half = H_ROWS // 2
            tree = Tree(
                sends, place.col,
                lambda d, h: t_down.at[i, d % NY, pl.ds(half * h, half)],
                lambda k, h: land_d.at[i, k, pl.ds(half * h, half)],
                lambda h: out_d.at[i, pl.ds(half * h, half)],
                32,
            )
            tree.open()
            return tree

        def down_end(i, tree):
            m, e = Z_FIRST[i]
            half = H_ROWS // 2
            for h in range(2):
                add_into(grads.at[m, e, pl.ds(half * h, half)], tree.close(h), 32)
            finals.append(load(grads.at[m, e], grads_hbm.at[m, e]))

        def y_relay(i):
            for copy in own_loads[i]:
                copy.wait()
            trees[i].part = lambda d, h: own_p.at[i, {-1: 0, 1: 1, 0: 2 + h}[d]]
            trees[i].out = lambda h: own_p.at[i, h]
            if i > 0:
                trees[i].relay()

        def y_end(i):
            m, e = Y_FIRST[i]
            for h in range(2):
                terms = trees[i].close(h)

                @pl.when(place.zh != h)
                def _():
                    add_into(out_z.at[i], terms, 64)

                @pl.when(place.zh == h)
                def _():
                    add_into(grads.at[m, e], terms, 64)

            return sends.start(out_z.at[i], lambda: land_z.at[i], place.col(0, 1))

        def z_end(i, copy):
            m, e = Y_FIRST[i]
            copy.wait_recv()
            dst = grads.at[m, e]
            add_into(dst, [dst, land_z.at[i]], 64)
            finals.append(load(dst, grads_hbm.at[m, e]))

        y_relay(0)
        y_relay(1)
        d0 = down_mid(0)
        finals = []
        r0 = rows_end(0)
        z0 = y_end(0)
        rows_mid()
        z1 = y_end(1)
        y_relay(2)
        y_relay(3)
        d1 = down_mid(1)
        rows_last(0, r0)
        d0.relay()
        z_end(0, z0)
        z2 = y_end(2)
        r1 = rows_end(1)
        d1.relay()
        z_end(1, z1)
        z3 = y_end(3)
        down_end(0, d0)
        rows_last(1, r1)
        down_end(1, d1)
        z_end(2, z2)
        z_end(3, z3)
        for copy in finals:
            copy.wait()
        for copy in sends.made:
            if all(copy is not c for c in shares.values()):
                copy.wait_send()

    def buf(*shape):
        return pltpu.VMEM(shape, BF16)

    d = t_first.shape[-1]
    slab = (H_ROWS, W_COLS)
    pl.run_scoped(
        first_phase,
        buf(2, 512, d), buf(2, 512, d), pltpu.VMEM((2, 512, H_ROWS), F32), buf(2, H_ROWS, 512),
        buf(H_ROWS, d), buf(H_ROWS, d), buf(H_ROWS, d), pltpu.VMEM((512, H_ROWS), F32),
        buf(512, H_ROWS), buf(512, H_ROWS), buf(H_ROWS, 512), buf(H_ROWS, 512),
        buf(2, H_ROWS, 1024),
    )
    pl.run_scoped(
        second_phase,
        buf(4, 4, *slab), buf(4, *slab), buf(2, 4, *slab), buf(2, *slab),
        buf(2, 128, d), buf(2, 2, 128, d),
    )


def backward(*operands):
    d = operands[0].shape[-1]
    n = 192
    hbm = pl.BlockSpec(memory_space=pl.ANY)
    vmem = pl.BlockSpec(memory_space=pltpu.VMEM)
    slab = (H_ROWS, W_COLS)

    def buf(*shape):
        return pltpu.VMEM(shape, BF16)

    return pl.pallas_call(
        backward_kernel,
        out_shape=(
            jax.ShapeDtypeStruct((128, d), BF16),
            jax.ShapeDtypeStruct((128, d), BF16),
            jax.ShapeDtypeStruct((8, 128), F32),
            jax.ShapeDtypeStruct((3, 2) + slab, F32),
            jax.ShapeDtypeStruct((3, 2, H_ROWS, d), BF16),
        ),
        in_specs=[hbm] * 8 + [vmem] * 2,
        out_specs=(vmem,) * 3 + (hbm,) * 2,
        scratch_shapes=[
            buf(8, 128, d), buf(4, 3, 2, *slab), buf(4, *slab), buf(2, 3, *slab), buf(2, 4, *slab),
            buf(2, 2, 3, 2, 64, d), buf(2, 128, d),
            pltpu.VMEM((16, 8, 128), F32),
            buf(2, 2, 64, d), buf(2, *slab), pltpu.VMEM((3, 2) + slab, F32),
            pltpu.SemaphoreType.DMA((n,)),
            pltpu.SemaphoreType.DMA((n,)),
            pltpu.SemaphoreType.DMA((112,)),
        ],
        compiler_params=pltpu.CompilerParams(
            collective_id=1, has_side_effects=True, vmem_limit_bytes=63 * 2**20
        ),
    )(*operands)[:4]


def shards(tokens, cotangent, route_gates, expert_ids, slot_index, w_gate, w_up, w_down):
    wg, wu = w_gate.transpose(0, 2, 1), w_up.transpose(0, 2, 1)
    routed, grad_rows, pre, hidden_t, o_out, gates_in, pick = forward(
        tokens, cotangent, expert_ids.T, slot_index.T, route_gates.T, wg, wu, w_down
    )
    out, grad, gates, grads = backward(
        routed, grad_rows, pre, hidden_t, wg, wu, w_down, o_out, gates_in, pick
    )
    return (
        out,
        grad,
        gates[0:6].T,
        grads[0].transpose(0, 2, 1),
        grads[1].transpose(0, 2, 1),
        grads[2],
    )


def solution(mesh):
    row = P(("expert", "dp"), None)
    weight = P("expert", None, None)
    return jax.shard_map(
        shards,
        mesh=mesh,
        in_specs=(row, row, row, row, row, weight, weight, weight),
        out_specs=(row, row, row, P("expert", "dp", None), P("expert", "dp", None), P("expert", None, "dp")),
        check_vma=False,
    )
```
